32 devices in a mesh: ctx: 8 (over y, x, core), fsdp: 4 (over z).
Axes of the slice: x: 2, y: 2, z: 4, core: 2. Of those that a mesh axis runs over, the one named last changes fastest.
Arguments:
- tokens: bfloat16 [4, 2048, 1600], P('fsdp', 'ctx'), may hold values from -6 to 6
- cotangent: bfloat16 [4, 2048, 1600], P('fsdp', 'ctx'), may hold values from -6 to 6
- unit_order: int32 [4, 16], P('fsdp'), may hold values from 0 to 15, as said below
- block_seq: int32 [4, 8], P('fsdp'), may hold values from 0 to 1, as said below
- meta_tokens: bfloat16 [128, 1600], P('fsdp', 'ctx'), may hold values from -6 to 6
- input_gain: bfloat16 [1600], P('ctx'), may hold values from 0.5 to 1.5
- query_key_value_weight: bfloat16 [1600, 2240], P('fsdp', 'ctx'), may hold values from -0.15625 to 0.15625
- w_xz: bfloat16 [1600, 6400], P('fsdp', 'ctx'), may hold values from -0.15625 to 0.15625
- conv_kernel: bfloat16 [4, 3200], P('fsdp', 'ctx'), may hold values from -3 to 3
- state_proj: bfloat16 [132, 3200], P('fsdp', 'ctx'), may hold values from -0.109375 to 0.109375
- step_proj: bfloat16 [100, 3200], P('fsdp', 'ctx'), may hold values from -0.625 to 0.625
- step_bias: bfloat16 [3200], P('ctx'), may hold values from -9 to -2.5
- decay_log: bfloat16 [16, 3200], P('fsdp', 'ctx'), may hold values from -2 to 2
- skip_gain: bfloat16 [3200], P('ctx'), may hold values from 0.5 to 1.5
- attn_gain: bfloat16 [1600], P('ctx'), may hold values from 0.5 to 1.5
- ssm_gain: bfloat16 [3200], P('ctx'), may hold values from 0.5 to 1.5
- out_proj: bfloat16 [4800, 1600], P('fsdp', 'ctx'), may hold values from -0.1875 to 0.1875
- ffn_gain: bfloat16 [1600], P('ctx'), may hold values from 0.5 to 1.5
- w_gate: bfloat16 [1600, 5504], P('fsdp', 'ctx'), may hold values from -0.15625 to 0.15625
- w_up: bfloat16 [1600, 5504], P('fsdp', 'ctx'), may hold values from -0.15625 to 0.15625
- w_down: bfloat16 [5504, 1600], P('fsdp', 'ctx'), may hold values from -0.15625 to 0.15625
Outputs:
- layer_out: bfloat16 [4, 2048, 1600], P('fsdp', 'ctx')
- tokens_grad: bfloat16 [4, 2048, 1600], P('fsdp', 'ctx')
- meta_grad: float32 [128, 1600], P('fsdp', 'ctx')
- input_gain_grad: float32 [1600], P('ctx')
- qkv_grad: float32 [1600, 2240], P('fsdp', 'ctx')
- xz_grad: float32 [1600, 6400], P('fsdp', 'ctx')
- conv_grad: float32 [4, 3200], P('fsdp', 'ctx')
- state_proj_grad: float32 [132, 3200], P('fsdp', 'ctx')
- step_proj_grad: float32 [100, 3200], P('fsdp', 'ctx')
- step_bias_grad: float32 [3200], P('ctx')
- decay_log_grad: float32 [16, 3200], P('fsdp', 'ctx')
- skip_gain_grad: float32 [3200], P('ctx')
- attn_gain_grad: float32 [1600], P('ctx')
- ssm_gain_grad: float32 [3200], P('ctx')
- out_proj_grad: float32 [4800, 1600], P('fsdp', 'ctx')
- ffn_gain_grad: float32 [1600], P('ctx')
- gate_grad: float32 [1600, 5504], P('fsdp', 'ctx')
- up_grad: float32 [1600, 5504], P('fsdp', 'ctx')
- down_grad: float32 [5504, 1600], P('fsdp', 'ctx')
The draws below stay inside these ranges and needn't reach their ends.
Inputs may be any that keep to these rules, and one draw needn't show every extreme that they name: `unit_order`: each row is a permutation of 0 to 15; slots 2c and 2c + 1 hold units u and 15 - u for some u. `block_seq`: each row is 0 on its first blocks and 1 on the rest; each value covers 2 or more blocks.
All inputs are finite; a program needn't handle non-finite values.
Results may differ from the reference program's by a relative error of at most 0.02.
Values may be sent and summed in bfloat16 or wider, within the bound.
No kernel may reach another device: no remote copies, remote signals or barrier semaphores. Data moves between devices by JAX's collectives and lax.ppermute only.
A program may use at most 576 MiB of HBM per device.

```python
import jax
import jax.numpy as jnp
from jax import lax

MODEL_DIM = 1600
QUERY_HEADS = 25
KEY_VALUE_HEADS = 5
HEAD_SIZE = 64
INNER = 3200
STATE = 16
CONV = 4
DT_RANK = 100
FF = 5504
META = 128
BLOCK_ROWS = 256
GROUPS = 4
UNITS_G = 16
BLOCKS_G = 8
GT = 2048


def draw_unit_order(key, part):
    group_keys = jax.random.split(key, GROUPS)

    def per_group(group_key):
        pair_key, flip_key = jax.random.split(group_key)
        pair_ids = jax.random.permutation(pair_key, UNITS_G // 2).astype(jnp.int32)
        flip_bits = jax.random.randint(flip_key, (UNITS_G // 2,), 0, 2).astype(jnp.int32)
        first_unit = jnp.where(flip_bits == 1, UNITS_G - 1 - pair_ids, pair_ids)
        second = UNITS_G - 1 - first_unit
        return jnp.stack([first_unit, second], axis=1).reshape(UNITS_G)
    return jax.vmap(per_group)(group_keys)


def draw_block_seq(key, part):
    boundary = jax.random.randint(key, (GROUPS, 1), 2, BLOCKS_G - 1).astype(jnp.int32)
    return (jnp.arange(BLOCKS_G, dtype=jnp.int32)[None, :] >= boundary).astype(jnp.int32)


def level_of(key, extent, cuts, least, high):
    factor_of = 1.0
    for position, blocks in cuts:
        draws = jax.random.uniform(jax.random.fold_in(jax.random.fold_in(key, 6), position), (blocks,), jnp.float32, least / len(cuts), high / len(cuts))
        factor_of = factor_of * jnp.repeat(jnp.exp(draws), extent[position] // blocks).reshape((-1,) + (1,) * (len(extent) - 1 - position))
    return factor_of


def noise(own_key, dims, spread, most, pieces=(), kind=jnp.bfloat16):
    drawn = jax.random.normal(own_key, dims, jnp.float32) * spread
    if len(pieces) > 0:
        drawn = level_of(own_key, dims, pieces, -0.22, 0.18) * drawn
    return jnp.clip(drawn, min=-most, max=most).astype(kind)


def setup_inputs(seed: int = 0) -> dict:
    key_list = jax.random.split(jax.random.key(seed), 22)
    return {
        "tokens": noise(key_list[0], (GROUPS, GT, MODEL_DIM), 1.0, 6.0, ((0, 4), (1, 8))),
        "cotangent": noise(key_list[1], (GROUPS, GT, MODEL_DIM), 1.0, 6.0, ((0, 4), (1, 8))),
        "unit_order": draw_unit_order(jax.random.fold_in(key_list[21], 71), 0),
        "block_seq": draw_block_seq(jax.random.fold_in(key_list[21], 71), 0),
        "meta_tokens": noise(key_list[4], (META, MODEL_DIM), 1.0, 6.0, ((0, 4), (1, 8))),
        "input_gain": jnp.clip(1.0 + 0.1 * jax.random.normal(key_list[5], (MODEL_DIM,), jnp.float32), 0.5, 1.5).astype(jnp.bfloat16),
        "query_key_value_weight": noise(key_list[6], (MODEL_DIM, (QUERY_HEADS + 2 * KEY_VALUE_HEADS) * HEAD_SIZE), MODEL_DIM ** -0.5, 0.15625, ((0, 4), (1, 8))),
        "w_xz": noise(key_list[7], (MODEL_DIM, 2 * INNER), MODEL_DIM ** -0.5, 0.15625, ((0, 4), (1, 8))),
        "conv_kernel": noise(key_list[8], (CONV, INNER), 0.5, 3.0, ((0, 4), (1, 8))),
        "state_proj": noise(key_list[9], (DT_RANK + 2 * STATE, INNER), INNER ** -0.5, 0.109375, ((0, 4), (1, 8))),
        "step_proj": noise(key_list[10], (DT_RANK, INNER), DT_RANK ** -0.5, 0.625, ((0, 4), (1, 8))),
        "step_bias": jnp.clip(-9.0 + 6.5 * jax.random.uniform(key_list[11], (INNER,), jnp.float32) ** level_of(key_list[11], (INNER,), ((0, 8),), -0.2, 0.2), -9.0, -2.5).astype(jnp.bfloat16),
        "decay_log": jnp.clip(jax.random.uniform(key_list[12], (STATE, INNER), jnp.float32, -2.0, 2.0) * level_of(key_list[12], (STATE, INNER), ((0, 4), (1, 8)), -0.4, 0.0), -2.0, 2.0).astype(jnp.bfloat16),
        "skip_gain": jnp.clip(0.5 + 1.0 * jax.random.uniform(key_list[13], (INNER,), jnp.float32) ** level_of(key_list[13], (INNER,), ((0, 8),), -0.2, 0.2), 0.5, 1.5).astype(jnp.bfloat16),
        "attn_gain": jnp.clip(1.0 + 0.1 * jax.random.normal(key_list[14], (QUERY_HEADS * HEAD_SIZE,), jnp.float32), 0.5, 1.5).astype(jnp.bfloat16),
        "ssm_gain": jnp.clip(1.0 + 0.1 * jax.random.normal(key_list[15], (INNER,), jnp.float32), 0.5, 1.5).astype(jnp.bfloat16),
        "out_proj": noise(key_list[16], (QUERY_HEADS * HEAD_SIZE + INNER, MODEL_DIM), ((QUERY_HEADS * HEAD_SIZE + INNER) // 4) ** -0.5, 0.1875, ((0, 4), (1, 8))),
        "ffn_gain": jnp.clip(1.0 + 0.1 * jax.random.normal(key_list[17], (MODEL_DIM,), jnp.float32), 0.5, 1.5).astype(jnp.bfloat16),
        "w_gate": noise(key_list[18], (MODEL_DIM, FF), MODEL_DIM ** -0.5, 0.15625, ((0, 4), (1, 8))),
        "w_up": noise(key_list[19], (MODEL_DIM, FF), MODEL_DIM ** -0.5, 0.15625, ((0, 4), (1, 8))),
        "w_down": noise(key_list[20], (FF, MODEL_DIM), (FF // 4) ** -0.5, 0.15625, ((0, 4), (1, 8))),
    }


EPS = 1e-06
HIGH = lax.Precision.HIGHEST
NEGATIVE_FILL = -1e+30

@jax.custom_vjp
def low(v):
    return lax.optimization_barrier(v.astype(jnp.bfloat16)).astype(jnp.float32)

@jax.custom_vjp
def low_back(v):
    return v

def low_keep(v):
    return (low(v), None)

def low_pass(kept, grad):
    return (grad,)

def back_keep(v):
    return (v, None)

def back_low(kept, grad):
    return (low(grad),)
low.defvjp(low_keep, low_pass)
low_back.defvjp(back_keep, back_low)

def matmul(left, right):
    return jnp.dot(left, right, precision=HIGH, preferred_element_type=jnp.float32)

def rms_norm(value, gain):
    return value * lax.rsqrt(lax.optimization_barrier(jnp.mean(value * value, axis=-1, keepdims=True)) + EPS) * gain

def silu(value):
    return value * jax.nn.sigmoid(value)

def group_forward(tok_rows, slot_unit, seq_of_block, params):
    meta_tokens, input_gain, query_key_value_weight, w_xz, conv_kernel, state_proj, step_proj, step_bias, decay_log, skip_gain, attn_gain, ssm_gain, out_proj, ffn_gain, w_gate, w_up, w_down = params
    units_all = slot_unit.shape[0]
    unit_rows = tok_rows.shape[0] // units_all
    model_width = tok_rows.shape[1]
    grouped_rows = units_all * unit_rows
    slot_ids = jnp.arange(units_all, dtype=jnp.int32)
    inverse = jnp.zeros((units_all,), jnp.int32).at[slot_unit].set(slot_ids)
    unit_seq = jnp.repeat(seq_of_block, 2)
    starts = jnp.concatenate([jnp.ones((1,), jnp.bool_), unit_seq[1:] != unit_seq[:-1]])
    x_units = tok_rows.reshape(units_all, unit_rows, model_width)[inverse]
    x_units = jnp.where(starts[:, None, None], meta_tokens[None], x_units)
    resid_in = x_units.reshape(grouped_rows, model_width)
    sequence_of_row = jnp.repeat(unit_seq, unit_rows)
    block_of_row = jnp.arange(grouped_rows, dtype=jnp.int32) // BLOCK_ROWS
    normed = low(rms_norm(resid_in, input_gain))
    query_key_value_rows = low(low_back(matmul(normed, query_key_value_weight)))
    query_width = QUERY_HEADS * HEAD_SIZE
    key_value_width = KEY_VALUE_HEADS * HEAD_SIZE
    queries_per_key_head = QUERY_HEADS // KEY_VALUE_HEADS
    query_rows = query_key_value_rows[:, :query_width].reshape(grouped_rows, KEY_VALUE_HEADS, queries_per_key_head, HEAD_SIZE)
    every_key = query_key_value_rows[:, query_width:query_width + key_value_width].reshape(grouped_rows, KEY_VALUE_HEADS, HEAD_SIZE)
    every_value = query_key_value_rows[:, query_width + key_value_width:].reshape(grouped_rows, KEY_VALUE_HEADS, HEAD_SIZE)
    score_scale = HEAD_SIZE ** (-0.5)

    @jax.checkpoint
    def attend_blocks(block_args):
        query_part, query_seq, query_block = block_args
        scores = jnp.einsum('qhgd,khd->hgqk', query_part, every_key, precision=HIGH) * score_scale
        scores = low_back(scores)
        allowed = (sequence_of_row[None, :] == query_seq[:, None]) & (block_of_row[None, :] <= query_block[:, None])
        scores = jnp.where(allowed[None, None], scores, NEGATIVE_FILL)
        top_score = lax.optimization_barrier(jnp.max(scores, axis=-1, keepdims=True))
        weights = jnp.exp(scores - top_score)
        probs = low(weights / lax.optimization_barrier(jnp.sum(weights, axis=-1, keepdims=True)))
        return jnp.einsum('hgqk,khd->qhgd', probs, every_value, precision=HIGH)
    count_of_blocks = grouped_rows // BLOCK_ROWS
    attention_output = lax.map(attend_blocks, (query_rows.reshape(count_of_blocks, BLOCK_ROWS, KEY_VALUE_HEADS, queries_per_key_head, HEAD_SIZE), sequence_of_row.reshape(count_of_blocks, BLOCK_ROWS), block_of_row.reshape(count_of_blocks, BLOCK_ROWS)))
    attention_output = attention_output.reshape(grouped_rows, query_width)
    xz_rows = low(low_back(matmul(normed, w_xz)))
    conv_in = xz_rows[:, :INNER]
    z_gate = xz_rows[:, INNER:]
    conv_out = conv_kernel[CONV - 1] * conv_in
    for shift in range(1, CONV):
        moved = jnp.concatenate([jnp.zeros((shift, INNER), jnp.float32), conv_in[:-shift]], axis=0)
        same = jnp.concatenate([jnp.zeros((shift,), jnp.bool_), sequence_of_row[shift:] == sequence_of_row[:-shift]])
        conv_out = conv_out + conv_kernel[CONV - 1 - shift] * jnp.where(same[:, None], moved, 0.0)
    ssm_in = low(silu(conv_out))
    select = low_back(matmul(ssm_in, state_proj.T))
    step_low = low(select[:, :DT_RANK])
    b_in = select[:, DT_RANK:DT_RANK + STATE]
    c_out = select[:, DT_RANK + STATE:]
    steps = jax.nn.softplus(low_back(matmul(step_low, step_proj) + step_bias))
    decay = -jnp.exp(decay_log)

    @jax.checkpoint
    def unit_scan(state, unit_args):
        x_unit, step_unit, b_unit, c_unit, first_unit = unit_args
        state = jnp.where(first_unit, 0.0, state)

        def advance(inner_state, row):
            x_row, step_row, b_row, c_row = row
            inner_state = jnp.exp(step_row[None, :] * decay) * inner_state + (step_row * x_row)[None, :] * b_row[:, None]
            return (inner_state, lax.optimization_barrier(jnp.sum(c_row[:, None] * inner_state, axis=0)))
        state, y_unit = lax.scan(advance, state, (x_unit, step_unit, b_unit, c_unit))
        return (state, y_unit)
    _, y_scan = lax.scan(unit_scan, jnp.zeros((STATE, INNER), jnp.float32), (ssm_in.reshape(units_all, unit_rows, INNER), steps.reshape(units_all, unit_rows, INNER), b_in.reshape(units_all, unit_rows, STATE), c_out.reshape(units_all, unit_rows, STATE), starts))
    y_total = y_scan.reshape(grouped_rows, INNER) + skip_gain * ssm_in
    ssm_out = y_total * silu(z_gate)
    mixed = low(jnp.concatenate([0.5 * rms_norm(attention_output, attn_gain), 0.5 * rms_norm(ssm_out, ssm_gain)], axis=1))
    mid_rows = resid_in + low_back(matmul(mixed, out_proj))
    ffn_in = low(rms_norm(mid_rows, ffn_gain))
    gate_rows = low_back(matmul(ffn_in, w_gate))
    up_rows = low_back(matmul(ffn_in, w_up))
    hidden = low(silu(gate_rows) * up_rows)
    out_rows = mid_rows + matmul(hidden, w_down)
    return out_rows.reshape(units_all, unit_rows, model_width)[slot_unit].reshape(grouped_rows, model_width)

def reference(tokens, cotangent, unit_order, block_seq, meta_tokens, input_gain, query_key_value_weight, w_xz, conv_kernel, state_proj, step_proj, step_bias, decay_log, skip_gain, attn_gain, ssm_gain, out_proj, ffn_gain, w_gate, w_up, w_down):
    params = tuple((item.astype(jnp.float32) for item in (meta_tokens, input_gain, query_key_value_weight, w_xz, conv_kernel, state_proj, step_proj, step_bias, decay_log, skip_gain, attn_gain, ssm_gain, out_proj, ffn_gain, w_gate, w_up, w_down)))
    tok_all = tokens.astype(jnp.float32)

    def forward(tok_values, param_values):

        def per_group(group_args):
            return group_forward(group_args[0], group_args[1], group_args[2], param_values)
        return lax.map(per_group, (tok_values, unit_order, block_seq))
    layer_out, pullback = jax.vjp(forward, tok_all, params)
    tokens_grad, grads = pullback(cotangent.astype(jnp.float32))
    return (layer_out.astype(jnp.bfloat16), tokens_grad.astype(jnp.bfloat16), grads[0], grads[1], grads[2], grads[3], grads[4], grads[5], grads[6], grads[7], grads[8], grads[9], grads[10], grads[11], grads[12], grads[13], grads[14], grads[15], grads[16])
```

```python
import functools
import jax
import jax.numpy as jnp
from jax import lax
from jax.experimental import pallas as pl
from jax.experimental.pallas import tpu as pltpu
from jax.sharding import PartitionSpec as P

QUERY_HEADS = 25
KEY_VALUE_HEADS = 5
HEAD_SIZE = 64
INNER = 3200
STATE = 16
CONV = 4
DT_RANK = 100
EPS = 1e-06
LOG2E = 1.4426950408889634
LN2 = 0.6931471805599453
VMEM_LIMIT = 56 * 1024 * 1024
STEP_GROUP = 8
F32 = jnp.float32
BF16 = jnp.bfloat16


def sigmoid(value):
    return 1.0 / (1.0 + jnp.exp(-value))


def dot_nn(left, right):
    return lax.dot_general(left, right, (((1,), (0,)), ((), ())), preferred_element_type=F32)


def dot_nt(left, right):
    return lax.dot_general(left, right, (((1,), (1,)), ((), ())), preferred_element_type=F32)


def dot_tn(left, right):
    return lax.dot_general(left, right, (((0,), (0,)), ((), ())), preferred_element_type=F32)


def unit_spec(rows, width, reverse_units=None):
    if reverse_units is None:
        return pl.BlockSpec((rows, width), lambda u, slot, *_: (slot[u], 0))
    last = reverse_units - 1
    return pl.BlockSpec((rows, width), lambda i, slot, *_: (slot[last - i], 0))


def whole_spec(shape):
    zeros = (0,) * len(shape)
    return pl.BlockSpec(shape, lambda *_: zeros)


def params():
    return pltpu.CompilerParams(
        dimension_semantics=("arbitrary",), vmem_limit_bytes=VMEM_LIMIT
    )


def conv_kernel_fwd(slot, start, xin_ref, w_ref, sel_ref, xc_ref, xs_ref, part_ref, ext):
    u = pl.program_id(0)
    rows = xin_ref.shape[0]
    keep = jnp.where(start[u] == 1, 0.0, 1.0)

    @pl.when(u == 0)
    def _():
        ext[...] = jnp.zeros_like(ext)

    ext[0:8, :] = ext[rows : rows + 8, :] * keep
    ext[8 : 8 + rows, :] = xin_ref[...].astype(F32)
    acc = w_ref[0:1, :] * ext[5 : 5 + rows, :]
    for k in range(1, CONV):
        acc = acc + w_ref[k : k + 1, :] * ext[5 + k : 5 + k + rows, :]
    xc_ref[...] = acc
    xs = (acc * sigmoid(acc)).astype(BF16)
    xs_ref[...] = xs
    part_ref[...] = dot_nt(xs, sel_ref[...]).astype(BF16)


def conv_forward(slot, start, xin, conv_w, sel_w, unit_rows):
    rows, width = xin.shape
    units = rows // unit_rows
    sel_rows = sel_w.shape[0]
    return pl.pallas_call(
        conv_kernel_fwd,
        out_shape=(
            jax.ShapeDtypeStruct((rows, width), F32),
            jax.ShapeDtypeStruct((rows, width), BF16),
            jax.ShapeDtypeStruct((rows, sel_rows), BF16),
        ),
        grid_spec=pltpu.PrefetchScalarGridSpec(
            num_scalar_prefetch=2,
            grid=(units,),
            in_specs=[
                unit_spec(unit_rows, width),
                whole_spec((CONV, width)),
                whole_spec((sel_rows, width)),
            ],
            out_specs=[
                unit_spec(unit_rows, width),
                unit_spec(unit_rows, width),
                unit_spec(unit_rows, sel_rows),
            ],
            scratch_shapes=[pltpu.VMEM((unit_rows + 8, width), F32)],
        ),
        compiler_params=params(),
        cost_estimate=pl.CostEstimate(
            flops=2 * rows * width * (sel_rows + 8), bytes_accessed=rows * width * 8, transcendentals=rows * width
        ),
    )(slot, start, xin, conv_w, sel_w)


def conv_kernel_bwd(
    slot, start, dsel_ref, part_ref, xc_ref, xin_ref, w_ref, sel_ref,
    dxin_ref, gw_ref, dext, ext,
):
    i = pl.program_id(0)
    units = pl.num_programs(0)
    u = units - 1 - i
    rows = xin_ref.shape[0]
    after = jnp.where(start[jnp.minimum(u + 1, units - 1)] == 1, 0.0, 1.0)

    @pl.when(i == 0)
    def _():
        dext[...] = jnp.zeros_like(dext)
        gw_ref[...] = jnp.zeros_like(gw_ref)

    dext[rows : rows + 8, :] = dext[0:8, :] * after
    xc = xc_ref[...]
    sig = sigmoid(xc)
    dxs = dot_nn(dsel_ref[...], sel_ref[...]) + part_ref[...]
    dxc = dxs * (sig * (1.0 + xc * (1.0 - sig)))
    dext[0:rows, :] = dxc
    acc = w_ref[CONV - 1 : CONV, :] * dxc
    for k in range(CONV - 1):
        off = CONV - 1 - k
        acc = acc + w_ref[k : k + 1, :] * dext[off : off + rows, :]
    dxin_ref[...] = acc.astype(BF16)
    xin = xin_ref[...].astype(F32)
    for k in range(CONV):
        off = CONV - 1 - k
        gw_ref[k : k + 1, :] += jnp.sum(dext[off : off + rows, :] * xin, axis=0, keepdims=True)


def conv_backward(slot, start, dsel, part, xc, xin, conv_w, sel_w, unit_rows):
    rows, width = xin.shape
    units = rows // unit_rows
    sel_rows = sel_w.shape[0]
    return pl.pallas_call(
        conv_kernel_bwd,
        out_shape=(
            jax.ShapeDtypeStruct((rows, width), BF16),
            jax.ShapeDtypeStruct((8, width), F32),
        ),
        grid_spec=pltpu.PrefetchScalarGridSpec(
            num_scalar_prefetch=2,
            grid=(units,),
            in_specs=[
                unit_spec(unit_rows, sel_rows, units),
                unit_spec(unit_rows, width, units),
                unit_spec(unit_rows, width, units),
                unit_spec(unit_rows, width, units),
                whole_spec((CONV, width)),
                whole_spec((sel_rows, width)),
            ],
            out_specs=[unit_spec(unit_rows, width, units), whole_spec((8, width))],
            scratch_shapes=[
                pltpu.VMEM((unit_rows + 8, width), F32),
                pltpu.VMEM((8, width), F32),
            ],
        ),
        compiler_params=params(),
        cost_estimate=pl.CostEstimate(
            flops=2 * rows * width * (sel_rows + 16), bytes_accessed=rows * width * 12, transcendentals=rows * width
        ),
    )(slot, start, dsel, part, xc, xin, conv_w, sel_w)


def step_sizes(low_ref, step_ref, bias_ref):
    pre = dot_nn(low_ref[...], step_ref[...]) + bias_ref[...]
    return jnp.maximum(pre, 0.0) + jnp.log(1.0 + jnp.exp(-jnp.abs(pre)))


def scan_kernel_fwd(
    slot, start, xs_ref, z_ref, low_ref, bc_ref, step_ref, bias_ref, rate_ref, skip_ref, gain_ref,
    y_ref, comb_ref, square_ref, begin_ref, dt_buf, dtx_buf, y_buf, state,
):
    u = pl.program_id(0)
    rows = xs_ref.shape[0]
    width = xs_ref.shape[1]
    keep = jnp.where(start[u] == 1, 0.0, 1.0)

    @pl.when(u == 0)
    def _():
        state[...] = jnp.zeros_like(state)

    xs = xs_ref[...].astype(F32)
    dt = step_sizes(low_ref, step_ref, bias_ref)
    dt_buf[...] = dt
    dtx_buf[...] = dt * xs
    first = state[...] * keep
    begin_ref[0] = first
    rate = rate_ref[...]
    bc = bc_ref[0]

    def group(g, h):
        base = pl.multiple_of(g * STEP_GROUP, STEP_GROUP)
        turned = pltpu.roll(bc, lax.rem(rows - base, rows), 1)
        for k in range(STEP_GROUP):
            dt_row = jnp.broadcast_to(dt_buf[pl.ds(base + k, 1), :], (STATE, width))
            dtx_row = jnp.broadcast_to(dtx_buf[pl.ds(base + k, 1), :], (STATE, width))
            b = jnp.broadcast_to(turned[0:STATE, k : k + 1], (STATE, width))
            c = jnp.broadcast_to(turned[STATE : 2 * STATE, k : k + 1], (STATE, width))
            h = jnp.exp2(dt_row * rate) * h + dtx_row * b
            y_buf[pl.ds(base + k, 1), :] = jnp.sum(c * h, axis=0, keepdims=True)
        return h

    state[...] = lax.fori_loop(0, rows // STEP_GROUP, group, first)
    y = y_buf[...] + skip_ref[...] * xs
    y_ref[...] = y
    z = z_ref[...].astype(F32)
    ys = y * (z * sigmoid(z))
    comb_ref[...] = (ys * gain_ref[...]).astype(BF16)
    square_ref[...] = jnp.broadcast_to(jnp.sum(ys * ys, axis=1, keepdims=True), square_ref.shape)


def scan_forward(slot, start, xs, z, low, bc, step_w, bias, rate2, skip, gain, unit_rows):
    rows, width = xs.shape
    units = rows // unit_rows
    rank = low.shape[1]
    return pl.pallas_call(
        scan_kernel_fwd,
        out_shape=(
            jax.ShapeDtypeStruct((rows, width), F32),
            jax.ShapeDtypeStruct((rows, width), BF16),
            jax.ShapeDtypeStruct((rows, 128), F32),
            jax.ShapeDtypeStruct((units, STATE, width), F32),
        ),
        grid_spec=pltpu.PrefetchScalarGridSpec(
            num_scalar_prefetch=2,
            grid=(units,),
            in_specs=[
                unit_spec(unit_rows, width),
                unit_spec(unit_rows, width),
                unit_spec(unit_rows, rank),
                pl.BlockSpec((1, 2 * STATE, unit_rows), lambda u, slot, *_: (slot[u], 0, 0)),
                whole_spec((rank, width)),
                whole_spec((1, width)),
                whole_spec((STATE, width)),
                whole_spec((1, width)),
                whole_spec((1, width)),
            ],
            out_specs=[
                unit_spec(unit_rows, width),
                unit_spec(unit_rows, width),
                unit_spec(unit_rows, 128),
                pl.BlockSpec((1, STATE, width), lambda u, *_: (u, 0, 0)),
            ],
            scratch_shapes=[
                pltpu.VMEM((unit_rows, width), F32),
                pltpu.VMEM((unit_rows, width), F32),
                pltpu.VMEM((unit_rows, width), F32),
                pltpu.VMEM((STATE, width), F32),
            ],
        ),
        compiler_params=params(),
        cost_estimate=pl.CostEstimate(
            flops=rows * width * STATE * 8, bytes_accessed=rows * width * 12,
            transcendentals=rows * width * STATE,
        ),
    )(slot, start, xs, z, low, bc, step_w, bias, rate2, skip, gain)


def scan_kernel_bwd(
    slot, start, dc_ref, stat_ref, y_ref, z_ref, xs_ref, low_ref, bc_ref, begin_ref,
    step_ref, bias_ref, rate_ref, skip_ref, gain_ref,
    dz_ref, part_ref, dlow_ref, dbc_ref, gstep_ref, gvec_ref, gdecay_ref,
    dt_buf, dtx_buf, dy_buf, gx_buf, ddt_buf, h_buf, da_buf, pb_buf, pc_buf, adj,
):
    i = pl.program_id(0)
    units = pl.num_programs(0)
    u = units - 1 - i
    rows = xs_ref.shape[0]
    width = xs_ref.shape[1]
    after = jnp.where(start[jnp.minimum(u + 1, units - 1)] == 1, 0.0, 1.0)

    @pl.when(i == 0)
    def _():
        adj[...] = jnp.zeros_like(adj)
        gstep_ref[...] = jnp.zeros_like(gstep_ref)
        gvec_ref[...] = jnp.zeros_like(gvec_ref)
        gdecay_ref[...] = jnp.zeros_like(gdecay_ref)

    xs = xs_ref[...].astype(F32)
    dt = step_sizes(low_ref, step_ref, bias_ref)
    dt_buf[...] = dt
    dtx_buf[...] = dt * xs
    rate = rate_ref[...]
    bc = bc_ref[0]
    h_buf[0] = begin_ref[0]

    def replay(g, h):
        base = pl.multiple_of(g * STEP_GROUP, STEP_GROUP)
        turned = pltpu.roll(bc, lax.rem(rows - base, rows), 1)
        for k in range(STEP_GROUP):
            dt_row = jnp.broadcast_to(dt_buf[pl.ds(base + k, 1), :], (STATE, width))
            dtx_row = jnp.broadcast_to(dtx_buf[pl.ds(base + k, 1), :], (STATE, width))
            b = jnp.broadcast_to(turned[0:STATE, k : k + 1], (STATE, width))
            da = jnp.exp2(dt_row * rate)
            da_buf[base + k] = da
            h = da * h + dtx_row * b
            h_buf[base + k + 1] = h
        return h

    lax.fori_loop(0, rows // STEP_GROUP, replay, begin_ref[0])

    factor = stat_ref[:, 0:1]
    shift = stat_ref[:, 1:2]
    z = z_ref[...].astype(F32)
    sig = sigmoid(z)
    gate = z * sig
    y = y_ref[...]
    ys = y * gate
    half = 0.5 * dc_ref[...]
    dys = factor * (half * gain_ref[...]) - ys * shift
    dy = dys * gate
    dz_ref[...] = (dys * y * (sig * (1.0 + z * (1.0 - sig)))).astype(BF16)
    dy_buf[...] = dy
    gvec_ref[0:1, :] += jnp.sum(half * ys * factor, axis=0, keepdims=True)
    gvec_ref[1:2, :] += jnp.sum(dy * xs, axis=0, keepdims=True)

    pairs = -(-width // 128)

    def fold(value):
        total = None
        for p in range(pairs):
            lo, hi = p * 128, min(width, p * 128 + 128)
            piece = value[:, lo:hi]
            if hi - lo < 128:
                piece = jnp.concatenate([piece, jnp.zeros((STATE, 128 - (hi - lo)), F32)], axis=1)
            total = piece if total is None else total + piece
        return total

    def group(index, carry):
        lam, acc = carry
        g = rows // STEP_GROUP - 1 - index
        base = pl.multiple_of(g * STEP_GROUP, STEP_GROUP)
        turned = pltpu.roll(bc, lax.rem(rows - base, rows), 1)
        for k in range(STEP_GROUP - 1, -1, -1):
            t = base + k
            dt_row = jnp.broadcast_to(dt_buf[pl.ds(t, 1), :], (STATE, width))
            dtx_row = jnp.broadcast_to(dtx_buf[pl.ds(t, 1), :], (STATE, width))
            dy_row = jnp.broadcast_to(dy_buf[pl.ds(t, 1), :], (STATE, width))
            b = jnp.broadcast_to(turned[0:STATE, k : k + 1], (STATE, width))
            c = jnp.broadcast_to(turned[STATE : 2 * STATE, k : k + 1], (STATE, width))
            lam = lam + c * dy_row
            pc_buf[t] = fold(dy_row * h_buf[t + 1])
            pb_buf[t] = fold(dtx_row * lam)
            gx_buf[pl.ds(t, 1), :] = jnp.sum(b * lam, axis=0, keepdims=True)
            lam = da_buf[t] * lam
            w = lam * h_buf[t]
            ddt_buf[pl.ds(t, 1), :] = jnp.sum(rate * w, axis=0, keepdims=True)
            acc = acc + dt_row * w
        return lam, acc

    lam, acc = lax.fori_loop(
        0, rows // STEP_GROUP, group, (adj[...] * after, jnp.zeros((STATE, width), F32))
    )
    adj[...] = lam
    gdecay_ref[...] += acc
    gx = gx_buf[...]
    part_ref[...] = gx * dt + skip_ref[...] * dy
    ddt = gx * xs + LN2 * ddt_buf[...]
    dpre = (ddt * (1.0 - jnp.exp(-dt))).astype(BF16)
    gstep_ref[...] += dot_tn(low_ref[...], dpre)
    gvec_ref[2:3, :] += jnp.sum(dpre.astype(F32), axis=0, keepdims=True)
    dlow_ref[...] = dot_nt(dpre, step_ref[...]).astype(BF16)
    ones = jnp.ones((8, 128), BF16)
    dbc_ref[0, 0] = dot_nt(ones, pb_buf[...].reshape(rows * STATE, 128).astype(BF16))
    dbc_ref[0, 1] = dot_nt(ones, pc_buf[...].reshape(rows * STATE, 128).astype(BF16))


def scan_backward(
    slot, start, dc, stat, y, z, xs, low, bc, begin, step_w, bias, rate2, skip, gain, unit_rows
):
    rows, width = xs.shape
    units = rows // unit_rows
    rank = low.shape[1]
    last = units - 1
    return pl.pallas_call(
        scan_kernel_bwd,
        out_shape=(
            jax.ShapeDtypeStruct((rows, width), BF16),
            jax.ShapeDtypeStruct((rows, width), F32),
            jax.ShapeDtypeStruct((rows, rank), BF16),
            jax.ShapeDtypeStruct((units, 2, 8, unit_rows * STATE), F32),
            jax.ShapeDtypeStruct((rank, width), F32),
            jax.ShapeDtypeStruct((8, width), F32),
            jax.ShapeDtypeStruct((STATE, width), F32),
        ),
        grid_spec=pltpu.PrefetchScalarGridSpec(
            num_scalar_prefetch=2,
            grid=(units,),
            in_specs=[
                unit_spec(unit_rows, width, units),
                unit_spec(unit_rows, 128, units),
                unit_spec(unit_rows, width, units),
                unit_spec(unit_rows, width, units),
                unit_spec(unit_rows, width, units),
                unit_spec(unit_rows, rank, units),
                pl.BlockSpec(
                    (1, 2 * STATE, unit_rows), lambda i, slot, *_: (slot[last - i], 0, 0)
                ),
                pl.BlockSpec((1, STATE, width), lambda i, *_: (last - i, 0, 0)),
                whole_spec((rank, width)),
                whole_spec((1, width)),
                whole_spec((STATE, width)),
                whole_spec((1, width)),
                whole_spec((1, width)),
            ],
            out_specs=[
                unit_spec(unit_rows, width, units),
                unit_spec(unit_rows, width, units),
                unit_spec(unit_rows, rank, units),
                pl.BlockSpec(
                    (1, 2, 8, unit_rows * STATE), lambda i, slot, *_: (slot[last - i], 0, 0, 0)
                ),
                whole_spec((rank, width)),
                whole_spec((8, width)),
                whole_spec((STATE, width)),
            ],
            scratch_shapes=[
                pltpu.VMEM((unit_rows, width), F32),
                pltpu.VMEM((unit_rows, width), F32),
                pltpu.VMEM((unit_rows, width), F32),
                pltpu.VMEM((unit_rows, width), F32),
                pltpu.VMEM((unit_rows, width), F32),
                pltpu.VMEM((unit_rows + 1, STATE, width), F32),
                pltpu.VMEM((unit_rows, STATE, width), F32),
                pltpu.VMEM((unit_rows, STATE, 128), F32),
                pltpu.VMEM((unit_rows, STATE, 128), F32),
                pltpu.VMEM((STATE, width), F32),
            ],
        ),
        compiler_params=params(),
        cost_estimate=pl.CostEstimate(
            flops=rows * width * STATE * 24, bytes_accessed=rows * width * 24,
            transcendentals=rows * width * STATE,
        ),
    )(slot, start, dc, stat, y, z, xs, low, bc, begin, step_w, bias, rate2, skip, gain)


def attn_kernel_fwd(slot, low_block, pair, q_ref, k_ref, v_ref, gain_ref, o_ref, comb_ref, stat_ref):
    u = pl.program_id(0)
    rows = q_ref.shape[0]
    heads = q_ref.shape[1] // HEAD_SIZE
    q = q_ref[...] * BF16(HEAD_SIZE**-0.5)
    queries = [q[:, h * HEAD_SIZE : (h + 1) * HEAD_SIZE] for h in range(heads)]

    def block(ref, which, j):
        first = pl.multiple_of(slot[2 * j] * rows, rows)
        second = pl.multiple_of(slot[2 * j + 1] * rows, rows)
        return jnp.concatenate([ref[which, pl.ds(first, rows), :], ref[which, pl.ds(second, rows), :]], axis=0)

    def body(j, carry):
        out = []
        for h in range(heads):
            top, total, acc = carry[h]
            s = dot_nt(queries[h], block(k_ref, pair[h], j))
            new_top = jnp.maximum(top, jnp.max(s, axis=1, keepdims=True))
            p = jnp.exp(s - new_top)
            fade = jnp.exp(top - new_top)
            total = total * fade + jnp.sum(p, axis=1, keepdims=True)
            acc = acc * fade + dot_nn(p.astype(BF16), block(v_ref, pair[h], j))
            out.append((new_top, total, acc))
        return tuple(out)

    start = tuple(
        (jnp.full((rows, 1), -1e30, F32), jnp.zeros((rows, 1), F32), jnp.zeros((rows, HEAD_SIZE), F32))
        for _ in range(heads)
    )
    result = lax.fori_loop(low_block[u], u // 2 + 1, body, start)
    lane = lax.broadcasted_iota(jnp.int32, (rows, 128), 1)
    stat = jnp.zeros((rows, 128), F32)
    outs = []
    for h in range(heads):
        top, total, acc = result[h]
        outs.append(acc / total)
        stat = jnp.where(lane == h, top + jnp.log(total), stat)
    o = outs[0] if heads == 1 else jnp.concatenate(outs, axis=1)
    o_ref[...] = o
    comb_ref[...] = (o * gain_ref[...]).astype(BF16)
    stat_ref[...] = jnp.where(lane == 127, jnp.sum(o * o, axis=1, keepdims=True), stat)


def attn_forward(slot, low_block, pair, q, k, v, gain, unit_rows):
    rows, width = q.shape
    units = rows // unit_rows
    return pl.pallas_call(
        attn_kernel_fwd,
        out_shape=(
            jax.ShapeDtypeStruct((rows, width), F32),
            jax.ShapeDtypeStruct((rows, width), BF16),
            jax.ShapeDtypeStruct((rows, 128), F32),
        ),
        grid_spec=pltpu.PrefetchScalarGridSpec(
            num_scalar_prefetch=3,
            grid=(units,),
            in_specs=[
                unit_spec(unit_rows, width),
                whole_spec(k.shape),
                whole_spec(v.shape),
                whole_spec((1, width)),
            ],
            out_specs=[
                unit_spec(unit_rows, width),
                unit_spec(unit_rows, width),
                unit_spec(unit_rows, 128),
            ],
        ),
        compiler_params=params(),
        cost_estimate=pl.CostEstimate(
            flops=2 * rows * rows * width, bytes_accessed=rows * width * 8,
            transcendentals=rows * rows * (width // HEAD_SIZE) // 2,
        ),
    )(slot, low_block, pair, q, k, v, gain)


def attn_kernel_bwd(
    slot, low_block, pair, q_ref, o_ref, do_ref, stat_ref, k_ref, v_ref, dq_ref, dk_ref, dv_ref
):
    u = pl.program_id(0)
    rows = q_ref.shape[0]
    heads = q_ref.shape[1] // HEAD_SIZE

    @pl.when(u == 0)
    def _():
        dk_ref[...] = jnp.zeros_like(dk_ref)
        dv_ref[...] = jnp.zeros_like(dv_ref)

    q = q_ref[...] * BF16(HEAD_SIZE**-0.5)
    do = do_ref[...]
    prod = do.astype(F32) * o_ref[...]
    stat = stat_ref[...]
    cut = lambda a, h: a[:, h * HEAD_SIZE : (h + 1) * HEAD_SIZE]
    queries = [cut(q, h) for h in range(heads)]
    grads = [cut(do, h) for h in range(heads)]
    deltas = [jnp.sum(cut(prod, h), axis=1, keepdims=True) for h in range(heads)]

    def body(j, carry):
        first = pl.multiple_of(slot[2 * j] * rows, rows)
        second = pl.multiple_of(slot[2 * j + 1] * rows, rows)
        out = []
        for h in range(heads):
            which = pair[h]
            kb = jnp.concatenate([k_ref[which, pl.ds(first, rows), :], k_ref[which, pl.ds(second, rows), :]], axis=0)
            vb = jnp.concatenate([v_ref[which, pl.ds(first, rows), :], v_ref[which, pl.ds(second, rows), :]], axis=0)
            p = jnp.exp(dot_nt(queries[h], kb) - stat[:, h : h + 1])
            ds = (p * (dot_nt(grads[h], vb) - deltas[h])).astype(BF16)
            dv = dot_tn(p.astype(BF16), grads[h])
            dk = dot_tn(ds, queries[h])
            dv_ref[which, pl.ds(first, rows), :] += dv[0:rows]
            dv_ref[which, pl.ds(second, rows), :] += dv[rows : 2 * rows]
            dk_ref[which, pl.ds(first, rows), :] += dk[0:rows]
            dk_ref[which, pl.ds(second, rows), :] += dk[rows : 2 * rows]
            out.append(carry[h] + dot_nn(ds, kb))
        return tuple(out)

    start = tuple(jnp.zeros((rows, HEAD_SIZE), F32) for _ in range(heads))
    result = lax.fori_loop(low_block[u], u // 2 + 1, body, start)
    dq = result[0] if heads == 1 else jnp.concatenate(result, axis=1)
    dq_ref[...] = (dq * HEAD_SIZE**-0.5).astype(BF16)


def attn_backward(slot, low_block, pair, q, o, do, stat, k, v, unit_rows):
    rows, width = q.shape
    units = rows // unit_rows
    return pl.pallas_call(
        attn_kernel_bwd,
        out_shape=(
            jax.ShapeDtypeStruct((rows, width), BF16),
            jax.ShapeDtypeStruct(k.shape, F32),
            jax.ShapeDtypeStruct(v.shape, F32),
        ),
        grid_spec=pltpu.PrefetchScalarGridSpec(
            num_scalar_prefetch=3,
            grid=(units,),
            in_specs=[
                unit_spec(unit_rows, width),
                unit_spec(unit_rows, width),
                unit_spec(unit_rows, width),
                unit_spec(unit_rows, 128),
                whole_spec(k.shape),
                whole_spec(v.shape),
            ],
            out_specs=[unit_spec(unit_rows, width), whole_spec(k.shape), whole_spec(v.shape)],
        ),
        compiler_params=params(),
        cost_estimate=pl.CostEstimate(
            flops=5 * rows * rows * width, bytes_accessed=rows * width * 12,
            transcendentals=rows * rows * (width // HEAD_SIZE) // 2,
        ),
    )(slot, low_block, pair, q, o, do, stat, k, v)


def rows_gather(value):
    return lax.all_gather(value, "ctx", axis=0, tiled=True)


def rows_scatter(value):
    return lax.psum_scatter(value, "ctx", scatter_dimension=0, tiled=True)


def lane_gather(value):
    return lax.all_gather(value, "fsdp", axis=0, tiled=True)


def lane_scatter(value):
    return lax.psum_scatter(value, "fsdp", scatter_dimension=0, tiled=True)


def columns_to_rows(value, devices):
    width = value.shape[1]
    blocks = value.reshape(devices, -1, width)
    got = lax.all_to_all(blocks, "ctx", split_axis=0, concat_axis=0, tiled=True)
    return jnp.transpose(got, (1, 0, 2)).reshape(-1, devices * width)


def rows_to_columns(value, devices):
    rows = value.shape[0]
    blocks = jnp.transpose(value.reshape(rows, devices, -1), (1, 0, 2))
    got = lax.all_to_all(blocks, "ctx", split_axis=0, concat_axis=0, tiled=True)
    return got.reshape(devices * rows, -1)


def pair_routes(devices):
    half = devices // 2
    first = [(d, 2 * d) for d in range(half)] + [(d, 2 * (d - half) + 1) for d in range(half, devices)]
    second = [(d, 2 * d + 1) for d in range(half)] + [(d, 2 * (d - half)) for d in range(half, devices)]
    return first, second


def split_pairs(value, place, devices):
    width = value.shape[1] // 2
    first, second = pair_routes(devices)
    low, high = value[:, :width], value[:, width:]
    early = place < devices // 2
    got_a = lax.ppermute(jnp.where(early, low, high), "ctx", first)
    got_b = lax.ppermute(jnp.where(early, high, low), "ctx", second)
    even = place % 2 == 0
    return jnp.where(even, got_a, got_b), jnp.where(even, got_b, got_a)


def join_pairs(left, right, place, devices):
    first, second = pair_routes(devices)
    even = place % 2 == 0
    got_a = lax.ppermute(jnp.where(even, left, right), "ctx", [(b, a) for a, b in first])
    got_b = lax.ppermute(jnp.where(even, right, left), "ctx", [(b, a) for a, b in second])
    early = place < devices // 2
    return jnp.concatenate([jnp.where(early, got_a, got_b), jnp.where(early, got_b, got_a)], axis=1)


def pad_to(value, size, axis):
    widths = [(0, 0)] * value.ndim
    widths[axis] = (0, size - value.shape[axis])
    return jnp.pad(value, widths)


def rms_factor(value):
    return lax.rsqrt(jnp.mean(value * value, axis=-1, keepdims=True) + EPS)


def norm_back(value, factor, gain, grad):
    weighted = grad * gain
    d_value = factor * weighted - value * factor * factor * factor * jnp.mean(
        value * weighted, axis=-1, keepdims=True
    )
    return d_value, jnp.sum(grad * value * factor, axis=0)


def shards(
    tokens, cotangent, unit_order, block_seq, meta_tokens, input_gain, query_key_value_weight, w_xz,
    conv_kernel, state_proj, step_proj, step_bias, decay_log, skip_gain, attn_gain, ssm_gain,
    out_proj, ffn_gain, w_gate, w_up, w_down,
):
    devices = lax.axis_size("ctx")
    lanes = lax.axis_size("fsdp")
    place = lax.axis_index("ctx")
    own_rows = tokens.shape[1]
    model = tokens.shape[2]
    unit_rows = own_rows // 2
    slot_unit = unit_order[0]
    units = slot_unit.shape[0]
    rows = units * unit_rows
    width = conv_kernel.shape[1]
    hidden_width = w_gate.shape[1]
    heads = -(-QUERY_HEADS // devices)
    head_width = heads * HEAD_SIZE
    group = QUERY_HEADS // KEY_VALUE_HEADS
    query_width = QUERY_HEADS * HEAD_SIZE
    kv_width = KEY_VALUE_HEADS * HEAD_SIZE
    model_part = input_gain.shape[0]

    slot_ids = jnp.arange(units, dtype=jnp.int32)
    place_of = jnp.sum(
        jnp.where(slot_unit[None, :] == slot_ids[:, None], slot_ids[None, :], 0), axis=1
    ).astype(jnp.int32)
    unit_seq = jnp.repeat(block_seq[0], 2)
    starts = jnp.concatenate([jnp.ones((1,), jnp.bool_), unit_seq[1:] != unit_seq[:-1]])
    starts_int = starts.astype(jnp.int32)
    low_block = (jnp.sum(unit_seq[None, :] < unit_seq[:, None], axis=1) // 2).astype(jnp.int32)
    my_units = lax.dynamic_slice_in_dim(slot_unit, 2 * place, 2)
    my_start = jnp.any((my_units[:, None] == slot_ids[None, :]) & starts[None, :], axis=1)

    small = jnp.concatenate([conv_kernel, state_proj, step_proj, decay_log], axis=0)
    small_all = lax.all_gather(small, "fsdp", axis=0)
    marks = [conv_kernel.shape[0], state_proj.shape[0], step_proj.shape[0], decay_log.shape[0]]
    ends = [sum(marks[: i + 1]) for i in range(4)]
    conv_w = small_all[:, : ends[0]].reshape(-1, width).astype(F32)
    sel_w = small_all[:, ends[0] : ends[1]].reshape(-1, width)
    step_w = small_all[:, ends[1] : ends[2]].reshape(-1, width)
    decay = small_all[:, ends[2] :].reshape(-1, width).astype(F32)
    rate = -jnp.exp(decay)
    rate2 = rate * LOG2E
    meta_part = lax.all_gather(meta_tokens, "fsdp", axis=0, tiled=True)
    meta_rows = meta_part.shape[0]
    wide = jnp.concatenate(
        [meta_part, input_gain[None], ffn_gain[None], attn_gain[None]], axis=0
    )
    wide = lax.all_gather(wide, "ctx", axis=1, tiled=True).astype(F32)
    meta = wide[:meta_rows]
    gain_in = wide[meta_rows]
    gain_ffn = wide[meta_rows + 1]
    gain_attn = lax.dynamic_slice_in_dim(
        pad_to(wide[meta_rows + 2], devices * head_width, 0), place * head_width, head_width
    )[None]
    bias = step_bias.astype(F32)[None]
    skip = skip_gain.astype(F32)[None]
    gain_ssm = ssm_gain.astype(F32)[None]

    first_kv = (place * heads) // group
    qkv_row = lax.all_gather(query_key_value_weight, "ctx", axis=1, tiled=True)
    q_part = lax.dynamic_slice_in_dim(
        pad_to(qkv_row[:, :query_width], devices * head_width, 1), place * head_width, head_width, 1
    )
    kv_room = (devices * heads // group + 3) * HEAD_SIZE
    k_part = lax.dynamic_slice_in_dim(
        pad_to(qkv_row[:, query_width : query_width + kv_width], kv_room, 1),
        first_kv * HEAD_SIZE, 2 * HEAD_SIZE, 1,
    )
    v_part = lax.dynamic_slice_in_dim(
        pad_to(qkv_row[:, query_width + kv_width :], kv_room, 1),
        first_kv * HEAD_SIZE, 2 * HEAD_SIZE, 1,
    )
    pair = jnp.clip(
        (place * heads + jnp.arange(heads, dtype=jnp.int32)) // group - first_kv, 0, 1
    ).astype(jnp.int32)
    x_part, z_part = split_pairs(w_xz, place, devices)
    in_w = lane_gather(jnp.concatenate([q_part, k_part, v_part, x_part, z_part], axis=1))
    qkv_width = head_width + 4 * HEAD_SIZE
    qkv_w = in_w[:, :qkv_width]
    x_w = in_w[:, qkv_width : qkv_width + width]
    z_w = in_w[:, qkv_width + width :]

    out_cols = lane_gather(out_proj)
    blocks = jnp.concatenate(
        [
            pad_to(out_cols[:query_width], devices * head_width, 0).reshape(
                devices, head_width, model_part
            ),
            out_cols[query_width:].reshape(devices, width, model_part),
        ],
        axis=1,
    )
    out_w = columns_to_rows(blocks.reshape(-1, model_part), devices)
    gate_w = lane_gather(w_gate)
    up_w = lane_gather(w_up)
    down_w = columns_to_rows(lane_gather(w_down), devices)

    own_tok = tokens[0]
    resid = jnp.where(
        my_start[:, None, None], meta[None], own_tok.reshape(2, unit_rows, model).astype(F32)
    ).reshape(own_rows, model)
    in_factor = rms_factor(resid)
    normed = rows_gather((resid * in_factor * gain_in).astype(BF16))
    cot = rows_gather(cotangent[0])

    qkv = dot_nn(normed, qkv_w).astype(BF16)
    queries = qkv[:, :head_width]
    keys = jnp.transpose(
        qkv[:, head_width : head_width + 2 * HEAD_SIZE].reshape(rows, 2, HEAD_SIZE), (1, 0, 2)
    )
    values = jnp.transpose(
        qkv[:, head_width + 2 * HEAD_SIZE :].reshape(rows, 2, HEAD_SIZE), (1, 0, 2)
    )
    x_in = dot_nn(normed, x_w).astype(BF16)
    z_gate = dot_nn(normed, z_w).astype(BF16)
    conv_out, ssm_in, select = conv_forward(place_of, starts_int, x_in, conv_w, sel_w, unit_rows)
    select = lax.psum(select, "ctx").astype(F32)
    attn, attn_comb, attn_stat = attn_forward(
        place_of, low_block, pair, queries, keys, values, gain_attn, unit_rows
    )
    attn_out = rows_scatter(dot_nn(attn_comb, out_w[:head_width]).astype(BF16)).astype(F32)
    step_low = select[:, :DT_RANK].astype(BF16)
    bc = jnp.transpose(select[:, DT_RANK:].reshape(units, unit_rows, 2 * STATE), (0, 2, 1))
    y_total, ssm_comb, ssm_square, begins = scan_forward(
        place_of, starts_int, ssm_in, z_gate, step_low, bc, step_w, bias, rate2, skip, gain_ssm,
        unit_rows,
    )
    ssm_out = rows_scatter(dot_nn(ssm_comb, out_w[head_width:]).astype(BF16)).astype(F32)
    squares = jnp.stack([attn_stat[:, 127], ssm_square[:, 0]])
    squares = jnp.sum(lax.all_gather(squares, "ctx", axis=0), axis=0)
    factors = lax.rsqrt(
        squares / jnp.array([[query_width], [devices * width]], F32) + EPS
    )
    own_factors = lax.dynamic_slice_in_dim(factors, place * own_rows, own_rows, 1)
    mid = (
        resid
        + 0.5 * own_factors[0][:, None] * attn_out
        + 0.5 * own_factors[1][:, None] * ssm_out
    )
    mid_factor = rms_factor(mid)
    ffn_in = rows_gather((mid * mid_factor * gain_ffn).astype(BF16))

    gate = dot_nn(ffn_in, gate_w)
    up = dot_nn(ffn_in, up_w)
    sig = sigmoid(gate)
    act = gate * sig
    hidden = (act * up).astype(BF16)
    d_hidden = dot_nt(cot, down_w)
    d_gate = (d_hidden * up * (sig * (1.0 + gate * (1.0 - sig)))).astype(BF16)
    d_up = (d_hidden * act).astype(BF16)
    d_ffn = rows_scatter((dot_nt(d_gate, gate_w) + dot_nt(d_up, up_w)).astype(BF16)).astype(F32)
    ffn_out = rows_scatter(dot_nn(hidden, down_w).astype(BF16)).astype(F32)
    layer_out = (mid + ffn_out).astype(BF16)[None]
    gate_grad = lane_scatter(dot_tn(ffn_in, d_gate).astype(BF16)).astype(F32)
    up_grad = lane_scatter(dot_tn(ffn_in, d_up).astype(BF16)).astype(F32)
    down_grad = lane_scatter(
        rows_to_columns(dot_tn(hidden, cot).astype(BF16), devices)
    ).astype(F32)

    d_mid_norm, ffn_gain_part = norm_back(mid, mid_factor, gain_ffn, d_ffn)
    d_mid = cotangent[0].astype(F32) + d_mid_norm
    d_branch_own = d_mid.astype(BF16)
    d_branch = rows_gather(d_branch_own)
    branch_f = d_branch_own.astype(F32)
    dots = jnp.stack(
        [
            jnp.sum(branch_f * attn_out, axis=1) * (0.5 / query_width),
            jnp.sum(branch_f * ssm_out, axis=1) * (0.5 / (devices * width)),
        ]
    )
    dots = lax.all_gather(dots, "ctx", axis=1, tiled=True)
    shifts = dots * factors * factors * factors

    d_comb_attn = dot_nt(d_branch, out_w[:head_width])
    d_comb_ssm = dot_nt(d_branch, out_w[head_width:])
    attn_mixed = (attn * (0.5 * factors[0][:, None] * gain_attn)).astype(BF16)
    ssm_mixed = (ssm_comb.astype(F32) * (0.5 * factors[1][:, None])).astype(BF16)
    out_part = dot_tn(jnp.concatenate([attn_mixed, ssm_mixed], axis=1), d_branch).astype(BF16)
    out_back = rows_to_columns(out_part, devices).reshape(devices, -1, model_part)
    out_grad = lane_scatter(
        jnp.concatenate(
            [
                out_back[:, :head_width].reshape(-1, model_part)[:query_width],
                out_back[:, head_width:].reshape(-1, model_part),
            ],
            axis=0,
        )
    ).astype(F32)
    half = 0.5 * d_comb_attn
    d_attn = factors[0][:, None] * (half * gain_attn) - attn * shifts[0][:, None]
    attn_gain_part = jnp.sum(half * attn * factors[0][:, None], axis=0)
    stat = jnp.transpose(pad_to(jnp.stack([factors[1], shifts[1]]), 128, 0))
    d_z, x_part_grad, d_low, d_bc, step_grad, vec_grads, decay_sum = scan_backward(
        place_of, starts_int, d_comb_ssm, stat, y_total, z_gate, ssm_in, step_low, bc, begins,
        step_w, bias, rate2, skip, gain_ssm, unit_rows,
    )
    d_bc = jnp.transpose(
        d_bc[:, :, 0].reshape(units, 2, unit_rows, STATE), (0, 2, 1, 3)
    ).reshape(rows, 2 * STATE)
    d_select = lax.psum(jnp.concatenate([d_low, d_bc.astype(BF16)], axis=1), "ctx")
    d_query, d_keys, d_values = attn_backward(
        place_of, low_block, pair, queries, attn, d_attn.astype(BF16), attn_stat, keys, values,
        unit_rows,
    )
    d_x, conv_grads = conv_backward(
        place_of, starts_int, d_select, x_part_grad, conv_out, x_in, conv_w, sel_w, unit_rows
    )
    select_grad = dot_tn(d_select, ssm_in)
    d_in = jnp.concatenate(
        [
            d_query,
            jnp.transpose(d_keys, (1, 0, 2)).reshape(rows, 2 * HEAD_SIZE).astype(BF16),
            jnp.transpose(d_values, (1, 0, 2)).reshape(rows, 2 * HEAD_SIZE).astype(BF16),
            d_x,
            d_z,
        ],
        axis=1,
    )
    d_normed = rows_scatter(dot_nt(d_in, in_w).astype(BF16)).astype(F32)
    in_grad = lane_scatter(dot_tn(normed, d_in).astype(BF16))
    xz_grad = join_pairs(
        in_grad[:, qkv_width : qkv_width + width], in_grad[:, qkv_width + width :], place, devices
    ).astype(F32)
    spread = jnp.zeros((in_grad.shape[0], devices * head_width), BF16)
    spread = lax.dynamic_update_slice_in_dim(spread, in_grad[:, :head_width], place * head_width, 1)
    kv_zero = jnp.zeros((in_grad.shape[0], kv_room), BF16)
    qkv_full = jnp.concatenate(
        [
            spread[:, :query_width],
            lax.dynamic_update_slice_in_dim(
                kv_zero, in_grad[:, head_width : head_width + 2 * HEAD_SIZE],
                first_kv * HEAD_SIZE, 1,
            )[:, :kv_width],
            lax.dynamic_update_slice_in_dim(
                kv_zero, in_grad[:, head_width + 2 * HEAD_SIZE : qkv_width],
                first_kv * HEAD_SIZE, 1,
            )[:, :kv_width],
        ],
        axis=1,
    )
    part = query_key_value_weight.shape[1]
    qkv_blocks = jnp.transpose(qkv_full.reshape(-1, devices, part), (1, 0, 2))
    qkv_grad = jnp.sum(
        lax.all_to_all(qkv_blocks, "ctx", split_axis=0, concat_axis=0, tiled=True).astype(F32), axis=0
    )

    d_norm_in, in_gain_part = norm_back(resid, in_factor, gain_in, d_normed)
    d_resid = (d_mid + d_norm_in).reshape(2, unit_rows, model)
    flag = my_start[:, None, None]
    tokens_grad = jnp.where(flag, 0.0, d_resid).reshape(1, own_rows, model).astype(BF16)
    meta_sum = jnp.sum(jnp.where(flag, d_resid, 0.0), axis=0)

    gain_rows = jnp.stack(
        [
            in_gain_part,
            ffn_gain_part,
            lax.dynamic_update_slice_in_dim(
                jnp.zeros((devices * head_width,), F32), attn_gain_part, place * head_width, 0
            )[:query_width],
        ]
    )
    by_lane = jnp.concatenate(
        [
            meta_sum.reshape(lanes, -1, model),
            jnp.broadcast_to(gain_rows[None], (lanes, 3, model)),
        ],
        axis=1,
    )
    count = by_lane.shape[1]
    packed = jnp.transpose(
        by_lane.reshape(lanes, count, devices, model_part), (0, 2, 1, 3)
    ).reshape(lanes * devices, count, model_part)
    totals = jnp.sum(
        lax.all_to_all(
            packed.astype(BF16), ("fsdp", "ctx"), split_axis=0, concat_axis=0, tiled=True
        ).astype(F32),
        axis=0,
    )
    local = jnp.concatenate(
        [conv_grads[:CONV], select_grad, step_grad, rate * decay_sum, vec_grads[:3]], axis=0
    )
    local = jnp.sum(lax.all_gather(local, "fsdp", axis=0), axis=0)
    lane_place = lax.axis_index("fsdp")

    def lane_part(begin, count):
        each = count // lanes
        return lax.dynamic_slice_in_dim(local, begin + lane_place * each, each, 0)

    sel_count = select_grad.shape[0]
    at = [CONV, CONV + sel_count, CONV + sel_count + DT_RANK, CONV + sel_count + DT_RANK + STATE]
    return (
        layer_out,
        tokens_grad,
        totals[: count - 3],
        totals[count - 3],
        qkv_grad,
        xz_grad,
        lane_part(0, CONV),
        lane_part(at[0], sel_count),
        lane_part(at[1], DT_RANK),
        local[at[3] + 2],
        lane_part(at[2], STATE),
        local[at[3] + 1],
        totals[count - 1],
        local[at[3]],
        out_grad,
        totals[count - 2],
        gate_grad,
        up_grad,
        down_grad,
    )


def solution(mesh):
    rows = P("fsdp", "ctx", None)
    index = P("fsdp", None)
    mat = P("fsdp", "ctx")
    vec = P("ctx")
    return jax.shard_map(
        shards,
        mesh=mesh,
        in_specs=(
            rows, rows, index, index, mat, vec, mat, mat, mat, mat, mat, vec, mat, vec, vec, vec,
            mat, vec, mat, mat, mat,
        ),
        out_specs=(
            rows, rows, mat, vec, mat, mat, mat, mat, mat, vec, mat, vec, vec, vec, mat, vec, mat,
            mat, mat,
        ),
        check_vma=False,
    )
```

```python
import functools
import jax
import jax.numpy as jnp
from jax import lax
from jax.experimental import pallas as pl
from jax.experimental.pallas import tpu as pltpu
from jax.sharding import PartitionSpec as P

QUERY_HEADS = 25
KEY_VALUE_HEADS = 5
HEAD_SIZE = 64
INNER = 3200
STATE = 16
CONV = 4
DT_RANK = 100
EPS = 1e-06
LOG2E = 1.4426950408889634
LN2 = 0.6931471805599453
VMEM_LIMIT = 56 * 1024 * 1024
STEP_GROUP = 8
F32 = jnp.float32
BF16 = jnp.bfloat16


def sigmoid(value):
    return 0.5 * jnp.tanh(0.5 * value) + 0.5


def dot_nn(left, right):
    return lax.dot_general(left, right, (((1,), (0,)), ((), ())), preferred_element_type=F32)


def dot_nt(left, right):
    return lax.dot_general(left, right, (((1,), (1,)), ((), ())), preferred_element_type=F32)


def dot_tn(left, right):
    return lax.dot_general(left, right, (((0,), (0,)), ((), ())), preferred_element_type=F32)


def unit_spec(rows, width, reverse_units=None, which=0):
    if reverse_units is None:
        return pl.BlockSpec((rows, width), lambda u, *maps: (maps[which][u], 0))
    last = reverse_units - 1
    return pl.BlockSpec((rows, width), lambda i, *maps: (maps[which][last - i], 0))


def whole_spec(shape):
    zeros = (0,) * len(shape)
    return pl.BlockSpec(shape, lambda *_: zeros)


def params():
    return pltpu.CompilerParams(
        dimension_semantics=("arbitrary",), vmem_limit_bytes=VMEM_LIMIT
    )


def norm_unit(value, meta, gain, begins):
    value = jnp.where(begins == 1, meta, value.astype(F32))
    factor = lax.rsqrt(jnp.mean(value * value, axis=-1, keepdims=True) + EPS)
    return (value * factor * gain).astype(BF16)


def norm_pieces_kernel(begins, meta_ref, gain_ref, *refs):
    pieces, out_ref = refs[:-1], refs[-1]
    unit_rows = meta_ref.shape[0]
    unit = 0
    for piece in pieces:
        for i in range(piece.shape[0] // unit_rows):
            out_ref[unit * unit_rows : (unit + 1) * unit_rows, :] = norm_unit(
                piece[i * unit_rows : (i + 1) * unit_rows, :], meta_ref[...], gain_ref[...],
                begins[unit],
            )
            unit += 1


def norm_rows_kernel(begins, meta_ref, gain_ref, in_ref, out_ref):
    out_ref[...] = norm_unit(
        in_ref[...], meta_ref[...], gain_ref[...], begins[pl.program_id(0)]
    )


def norm_all(begins, meta, gain, pieces):
    unit_rows, width = meta.shape
    rows = sum(piece.shape[0] for piece in pieces)
    shape = jax.ShapeDtypeStruct((rows, width), BF16)
    if len(pieces) > 1:
        return pl.pallas_call(
            norm_pieces_kernel,
            out_shape=shape,
            in_specs=[pl.BlockSpec(memory_space=pltpu.SMEM)]
            + [pl.BlockSpec(memory_space=pltpu.VMEM)] * (2 + len(pieces)),
            out_specs=pl.BlockSpec(memory_space=pltpu.VMEM),
            compiler_params=pltpu.CompilerParams(vmem_limit_bytes=VMEM_LIMIT),
        )(begins, meta, gain, *pieces)
    by_unit = pl.BlockSpec((unit_rows, width), lambda u, *_: (u, 0))
    return pl.pallas_call(
        norm_rows_kernel,
        out_shape=shape,
        grid_spec=pltpu.PrefetchScalarGridSpec(
            num_scalar_prefetch=1,
            grid=(rows // unit_rows,),
            in_specs=[whole_spec((unit_rows, width)), whole_spec((1, width)), by_unit],
            out_specs=by_unit,
        ),
        compiler_params=params(),
    )(begins, meta, gain, pieces[0])


def conv_kernel_fwd(slot, fixed, start, xin_ref, w_ref, sel_ref, xc_ref, xs_ref, part_ref, ext):
    u = pl.program_id(0)
    rows = xin_ref.shape[0]
    keep = jnp.where(start[u] == 1, 0.0, 1.0)

    @pl.when(u == 0)
    def _():
        ext[...] = jnp.zeros_like(ext)

    ext[0:8, :] = ext[rows : rows + 8, :] * keep
    ext[8 : 8 + rows, :] = xin_ref[...].astype(F32)
    acc = w_ref[0:1, :] * ext[5 : 5 + rows, :]
    for k in range(1, CONV):
        acc = acc + w_ref[k : k + 1, :] * ext[5 + k : 5 + k + rows, :]
    xc_ref[...] = acc
    xs = (acc * sigmoid(acc)).astype(BF16)
    xs_ref[...] = xs
    part_ref[...] = dot_nt(xs, sel_ref[...]).astype(BF16)


def conv_forward(slot, fixed, start, xin, conv_w, sel_w, unit_rows):
    rows, width = xin.shape
    units = rows // unit_rows
    sel_rows = sel_w.shape[0]
    return pl.pallas_call(
        conv_kernel_fwd,
        out_shape=(
            jax.ShapeDtypeStruct((rows, width), F32),
            jax.ShapeDtypeStruct((rows, width), BF16),
            jax.ShapeDtypeStruct((rows, sel_rows), BF16),
        ),
        grid_spec=pltpu.PrefetchScalarGridSpec(
            num_scalar_prefetch=3,
            grid=(units,),
            in_specs=[
                unit_spec(unit_rows, width),
                whole_spec((CONV, width)),
                whole_spec((sel_rows, width)),
            ],
            out_specs=[
                unit_spec(unit_rows, width),
                unit_spec(unit_rows, width),
                unit_spec(unit_rows, sel_rows, None, 1),
            ],
            scratch_shapes=[pltpu.VMEM((unit_rows + 8, width), F32)],
        ),
        compiler_params=params(),
        cost_estimate=pl.CostEstimate(
            flops=2 * rows * width * (sel_rows + 8), bytes_accessed=rows * width * 8, transcendentals=rows * width
        ),
    )(slot, fixed, start, xin, conv_w, sel_w)


def conv_kernel_bwd(
    slot, fixed, start, dsel_ref, part_ref, xc_ref, xin_ref, xs_ref, w_ref, sel_ref,
    dxin_ref, gw_ref, gsel_ref, dext,
):
    i = pl.program_id(0)
    units = pl.num_programs(0)
    u = units - 1 - i
    rows = xin_ref.shape[0]
    after = jnp.where(start[jnp.minimum(u + 1, units - 1)] == 1, 0.0, 1.0)

    @pl.when(i == 0)
    def _():
        dext[...] = jnp.zeros_like(dext)
        gw_ref[...] = jnp.zeros_like(gw_ref)
        gsel_ref[...] = jnp.zeros_like(gsel_ref)

    gsel_ref[...] += dot_tn(dsel_ref[...], xs_ref[...])
    dext[rows : rows + 8, :] = dext[0:8, :] * after
    xc = xc_ref[...]
    sig = sigmoid(xc)
    dxs = dot_nn(dsel_ref[...], sel_ref[...]) + part_ref[...]
    dxc = dxs * (sig * (1.0 + xc * (1.0 - sig)))
    dext[0:rows, :] = dxc
    acc = w_ref[CONV - 1 : CONV, :] * dxc
    for k in range(CONV - 1):
        off = CONV - 1 - k
        acc = acc + w_ref[k : k + 1, :] * dext[off : off + rows, :]
    dxin_ref[...] = acc.astype(BF16)
    xin = xin_ref[...].astype(F32)
    for k in range(CONV):
        off = CONV - 1 - k
        gw_ref[k : k + 1, :] += jnp.sum(dext[off : off + rows, :] * xin, axis=0, keepdims=True)


def conv_backward(slot, fixed, start, dsel, part, xc, xin, xs, conv_w, sel_w, unit_rows):
    rows, width = xin.shape
    units = rows // unit_rows
    sel_rows = sel_w.shape[0]
    return pl.pallas_call(
        conv_kernel_bwd,
        out_shape=(
            jax.ShapeDtypeStruct((rows, width), BF16),
            jax.ShapeDtypeStruct((8, width), F32),
            jax.ShapeDtypeStruct((sel_rows, width), F32),
        ),
        grid_spec=pltpu.PrefetchScalarGridSpec(
            num_scalar_prefetch=3,
            grid=(units,),
            in_specs=[
                unit_spec(unit_rows, sel_rows, units, 1),
                unit_spec(unit_rows, width, units),
                unit_spec(unit_rows, width, units),
                unit_spec(unit_rows, width, units),
                unit_spec(unit_rows, width, units),
                whole_spec((CONV, width)),
                whole_spec((sel_rows, width)),
            ],
            out_specs=[
                unit_spec(unit_rows, width, units),
                whole_spec((8, width)),
                whole_spec((sel_rows, width)),
            ],
            scratch_shapes=[pltpu.VMEM((unit_rows + 8, width), F32)],
        ),
        compiler_params=params(),
        cost_estimate=pl.CostEstimate(
            flops=2 * rows * width * (sel_rows + 16), bytes_accessed=rows * width * 12, transcendentals=rows * width
        ),
    )(slot, fixed, start, dsel, part, xc, xin, xs, conv_w, sel_w)


def step_sizes(low_ref, step_ref, bias_ref):
    pre = dot_nn(low_ref[...], step_ref[...]) + bias_ref[...]
    return jnp.maximum(pre, 0.0) + jnp.log(1.0 + jnp.exp(-jnp.abs(pre)))


def lane_tiles(width):
    return [(lo, min(width, lo + 128)) for lo in range(0, width, 128)]


def fold_into(total, value, k):
    line = lax.broadcasted_iota(jnp.int32, (STEP_GROUP, 128), 0)
    return jnp.where(
        line == k, jnp.sum(value[0:8] + value[8:STATE], axis=0, keepdims=True), total
    )


def store_tiles(ref, value):
    for i, (lo, hi) in enumerate(lane_tiles(value.shape[1])):
        ref[i] = widen(value[:, lo:hi])


def load_tiles(ref, width):
    tiles = lane_tiles(width)
    return jnp.concatenate([ref[i, :, : hi - lo] for i, (lo, hi) in enumerate(tiles)], axis=1)


def widen(value):
    size = value.shape[1]
    if size == 128:
        return value
    return jnp.concatenate([value, jnp.zeros((value.shape[0], 128 - size), value.dtype)], axis=1)


def row_over_states(ref, i, t):
    return jnp.broadcast_to(ref[i, pl.ds(t, 1), :], (STATE, 128))


def scan_kernel_fwd(
    slot, fixed, start, xs_ref, z_ref, low_ref, bc_ref, step_ref, bias_ref, rate_ref, skip_ref,
    gain_ref, y_ref, comb_ref, square_ref, wide_ref, before_ref, last_ref, dt_buf, dtx_buf, y_buf,
    state,
):
    u = pl.program_id(0)
    rows = xs_ref.shape[0]
    width = xs_ref.shape[1]
    tiles = lane_tiles(width)
    count = len(tiles)
    keep = jnp.where(start[u] == 1, 0.0, 1.0)

    @pl.when(u == 0)
    def _():
        state[...] = jnp.zeros_like(state)

    xs = xs_ref[...].astype(F32)
    dt = step_sizes(low_ref, step_ref, bias_ref)
    store_tiles(dt_buf, dt)
    store_tiles(dtx_buf, dt * xs)
    rates = [widen(rate_ref[:, lo:hi]) for lo, hi in tiles]
    bc = bc_ref[0]
    for t in range(rows):
        wide_ref[0, t] = jnp.broadcast_to(bc[:, t : t + 1], (2 * STATE, 128))

    def group(g, carry):
        base = pl.multiple_of(g * STEP_GROUP, STEP_GROUP)
        h = list(carry)
        y = [jnp.zeros((STEP_GROUP, 128), F32) for _ in tiles]
        for k in range(STEP_GROUP):
            b = wide_ref[0, base + k, 0:STATE]
            c = wide_ref[0, base + k, STATE : 2 * STATE]
            for i in range(count):
                before_ref[0, base + k, i] = h[i]
                decay = jnp.exp2(row_over_states(dt_buf, i, base + k) * rates[i])
                h[i] = decay * h[i] + row_over_states(dtx_buf, i, base + k) * b
                y[i] = fold_into(y[i], c * h[i], k)
        for i in range(count):
            y_buf[i, pl.ds(base, STEP_GROUP), :] = y[i]
        return tuple(h)

    last = lax.fori_loop(
        0, rows // STEP_GROUP, group, tuple(state[i] * keep for i in range(count)), unroll=2
    )
    for i in range(count):
        state[i] = last[i]
        last_ref[0, i] = last[i]
    y = load_tiles(y_buf, width) + skip_ref[...] * xs
    y_ref[...] = y
    z = z_ref[...].astype(F32)
    ys = y * (z * sigmoid(z))
    comb_ref[...] = (ys * gain_ref[...]).astype(BF16)
    square_ref[...] = jnp.broadcast_to(jnp.sum(ys * ys, axis=1, keepdims=True), square_ref.shape)


def scan_forward(slot, fixed, start, xs, z, low, bc, step_w, bias, rate2, skip, gain, unit_rows):
    rows, width = xs.shape
    units = rows // unit_rows
    rank = low.shape[1]
    count = -(-width // 128)
    return pl.pallas_call(
        scan_kernel_fwd,
        out_shape=(
            jax.ShapeDtypeStruct((rows, width), F32),
            jax.ShapeDtypeStruct((rows, width), BF16),
            jax.ShapeDtypeStruct((rows, 128), F32),
            jax.ShapeDtypeStruct((units, unit_rows, 2 * STATE, 128), F32),
            jax.ShapeDtypeStruct((units, unit_rows, count, STATE, 128), F32),
            jax.ShapeDtypeStruct((units, count, STATE, 128), F32),
        ),
        grid_spec=pltpu.PrefetchScalarGridSpec(
            num_scalar_prefetch=3,
            grid=(units,),
            in_specs=[
                unit_spec(unit_rows, width),
                unit_spec(unit_rows, width),
                unit_spec(unit_rows, rank, None, 1),
                pl.BlockSpec(
                    (1, 2 * STATE, unit_rows), lambda u, slot, fixed, *_: (fixed[u], 0, 0)
                ),
                whole_spec((rank, width)),
                whole_spec((1, width)),
                whole_spec((STATE, width)),
                whole_spec((1, width)),
                whole_spec((1, width)),
            ],
            out_specs=[
                unit_spec(unit_rows, width),
                unit_spec(unit_rows, width),
                unit_spec(unit_rows, 128),
                pl.BlockSpec((1, unit_rows, 2 * STATE, 128), lambda u, *_: (u, 0, 0, 0)),
                pl.BlockSpec((1, unit_rows, count, STATE, 128), lambda u, *_: (u, 0, 0, 0, 0)),
                pl.BlockSpec((1, count, STATE, 128), lambda u, *_: (u, 0, 0, 0)),
            ],
            scratch_shapes=[
                pltpu.VMEM((count, unit_rows, 128), F32),
                pltpu.VMEM((count, unit_rows, 128), F32),
                pltpu.VMEM((count, unit_rows, 128), F32),
                pltpu.VMEM((count, STATE, 128), F32),
            ],
        ),
        compiler_params=params(),
        cost_estimate=pl.CostEstimate(
            flops=rows * width * STATE * 8, bytes_accessed=rows * width * 12,
            transcendentals=rows * width * STATE,
        ),
    )(slot, fixed, start, xs, z, low, bc, step_w, bias, rate2, skip, gain)


def scan_kernel_bwd(
    slot, fixed, start, dc_ref, stat_ref, y_ref, z_ref, xs_ref, low_ref, wide_ref, before_ref,
    last_ref, step_ref, bias_ref, rate_ref, skip_ref, gain_ref,
    dz_ref, part_ref, dlow_ref, dbc_ref, gstep_ref, gvec_ref, gdecay_ref,
    dt_buf, dtx_buf, dy_buf, gx_buf, ddt_buf, pb_buf, pc_buf, adj,
):
    i = pl.program_id(0)
    units = pl.num_programs(0)
    u = units - 1 - i
    rows = xs_ref.shape[0]
    width = xs_ref.shape[1]
    after = jnp.where(start[jnp.minimum(u + 1, units - 1)] == 1, 0.0, 1.0)

    @pl.when(i == 0)
    def _():
        adj[...] = jnp.zeros_like(adj)
        gstep_ref[...] = jnp.zeros_like(gstep_ref)
        gvec_ref[...] = jnp.zeros_like(gvec_ref)
        gdecay_ref[...] = jnp.zeros_like(gdecay_ref)

    xs = xs_ref[...].astype(F32)
    dt = step_sizes(low_ref, step_ref, bias_ref)
    store_tiles(dt_buf, dt)
    store_tiles(dtx_buf, dt * xs)
    tiles = lane_tiles(width)
    count = len(tiles)
    rates = [widen(rate_ref[:, lo:hi]) for lo, hi in tiles]

    factor = stat_ref[:, 0:1]
    shift = stat_ref[:, 1:2]
    z = z_ref[...].astype(F32)
    sig = sigmoid(z)
    gate = z * sig
    y = y_ref[...]
    ys = y * gate
    half = 0.5 * dc_ref[...]
    dys = factor * (half * gain_ref[...]) - ys * shift
    dy = dys * gate
    dz_ref[...] = (dys * y * (sig * (1.0 + z * (1.0 - sig)))).astype(BF16)
    store_tiles(dy_buf, dy)
    gvec_ref[0:1, :] += jnp.sum(half * ys * factor, axis=0, keepdims=True)
    gvec_ref[1:2, :] += jnp.sum(dy * xs, axis=0, keepdims=True)

    def group(index, carry):
        lams, accs, states = list(carry[0]), list(carry[1]), list(carry[2])
        g = rows // STEP_GROUP - 1 - index
        base = pl.multiple_of(g * STEP_GROUP, STEP_GROUP)
        gx = [jnp.zeros((STEP_GROUP, 128), F32) for _ in tiles]
        ddt = [jnp.zeros((STEP_GROUP, 128), F32) for _ in tiles]
        for k in range(STEP_GROUP - 1, -1, -1):
            t = base + k
            b = wide_ref[0, t, 0:STATE]
            c = wide_ref[0, t, STATE : 2 * STATE]
            pb = pc = None
            for i in range(count):
                dt_row = row_over_states(dt_buf, i, t)
                dy_row = row_over_states(dy_buf, i, t)
                lam = lams[i] + c * dy_row
                more_c = dy_row * states[i]
                more_b = row_over_states(dtx_buf, i, t) * lam
                pc = more_c if pc is None else pc + more_c
                pb = more_b if pb is None else pb + more_b
                gx[i] = fold_into(gx[i], b * lam, k)
                lams[i] = jnp.exp2(dt_row * rates[i]) * lam
                states[i] = before_ref[0, t, i]
                w = lams[i] * states[i]
                ddt[i] = fold_into(ddt[i], rates[i] * w, k)
                accs[i] = accs[i] + dt_row * w
            pb_buf[t] = pb
            pc_buf[t] = pc
        for i in range(count):
            gx_buf[i, pl.ds(base, STEP_GROUP), :] = gx[i]
            ddt_buf[i, pl.ds(base, STEP_GROUP), :] = ddt[i]
        return tuple(lams), tuple(accs), tuple(states)

    lams, accs, _ = lax.fori_loop(
        0,
        rows // STEP_GROUP,
        group,
        (
            tuple(adj[i] * after for i in range(count)),
            tuple(jnp.zeros((STATE, 128), F32) for _ in tiles),
            tuple(last_ref[0, i] for i in range(count)),
        ),
    )
    for i, (lo, hi) in enumerate(tiles):
        adj[i] = lams[i]
        gdecay_ref[:, lo:hi] += accs[i][:, : hi - lo]
    gx = load_tiles(gx_buf, width)
    part_ref[...] = gx * dt + skip_ref[...] * dy
    ddt = gx * xs + LN2 * load_tiles(ddt_buf, width)
    dpre = (ddt * (1.0 - jnp.exp(-dt))).astype(BF16)
    gstep_ref[...] += dot_tn(low_ref[...], dpre)
    gvec_ref[2:3, :] += jnp.sum(dpre.astype(F32), axis=0, keepdims=True)
    dlow_ref[...] = dot_nt(dpre, step_ref[...]).astype(BF16)
    ones = jnp.ones((8, 128), BF16)
    dbc_ref[0, 0] = dot_nt(ones, pb_buf[...].reshape(rows * STATE, 128).astype(BF16))
    dbc_ref[0, 1] = dot_nt(ones, pc_buf[...].reshape(rows * STATE, 128).astype(BF16))


def scan_backward(
    slot, fixed, start, dc, stat, y, z, xs, low, wide, before, final, step_w, bias, rate2, skip, gain, unit_rows
):
    rows, width = xs.shape
    units = rows // unit_rows
    rank = low.shape[1]
    count = -(-width // 128)
    last = units - 1
    return pl.pallas_call(
        scan_kernel_bwd,
        out_shape=(
            jax.ShapeDtypeStruct((rows, width), BF16),
            jax.ShapeDtypeStruct((rows, width), F32),
            jax.ShapeDtypeStruct((rows, rank), BF16),
            jax.ShapeDtypeStruct((units, 2, 8, unit_rows * STATE), F32),
            jax.ShapeDtypeStruct((rank, width), F32),
            jax.ShapeDtypeStruct((8, width), F32),
            jax.ShapeDtypeStruct((STATE, width), F32),
        ),
        grid_spec=pltpu.PrefetchScalarGridSpec(
            num_scalar_prefetch=3,
            grid=(units,),
            in_specs=[
                unit_spec(unit_rows, width, units),
                unit_spec(unit_rows, 128, units),
                unit_spec(unit_rows, width, units),
                unit_spec(unit_rows, width, units),
                unit_spec(unit_rows, width, units),
                unit_spec(unit_rows, rank, units, 1),
                pl.BlockSpec((1, unit_rows, 2 * STATE, 128), lambda i, *_: (last - i, 0, 0, 0)),
                pl.BlockSpec(
                    (1, unit_rows, count, STATE, 128), lambda i, *_: (last - i, 0, 0, 0, 0)
                ),
                pl.BlockSpec((1, count, STATE, 128), lambda i, *_: (last - i, 0, 0, 0)),
                whole_spec((rank, width)),
                whole_spec((1, width)),
                whole_spec((STATE, width)),
                whole_spec((1, width)),
                whole_spec((1, width)),
            ],
            out_specs=[
                unit_spec(unit_rows, width, units),
                unit_spec(unit_rows, width, units),
                unit_spec(unit_rows, rank, units, 1),
                pl.BlockSpec(
                    (1, 2, 8, unit_rows * STATE),
                    lambda i, slot, fixed, *_: (fixed[last - i], 0, 0, 0),
                ),
                whole_spec((rank, width)),
                whole_spec((8, width)),
                whole_spec((STATE, width)),
            ],
            scratch_shapes=[
                pltpu.VMEM((count, unit_rows, 128), F32),
                pltpu.VMEM((count, unit_rows, 128), F32),
                pltpu.VMEM((count, unit_rows, 128), F32),
                pltpu.VMEM((count, unit_rows, 128), F32),
                pltpu.VMEM((count, unit_rows, 128), F32),
                pltpu.VMEM((unit_rows, STATE, 128), F32),
                pltpu.VMEM((unit_rows, STATE, 128), F32),
                pltpu.VMEM((count, STATE, 128), F32),
            ],
        ),
        compiler_params=params(),
        cost_estimate=pl.CostEstimate(
            flops=rows * width * STATE * 24, bytes_accessed=rows * width * 24,
            transcendentals=rows * width * STATE,
        ),
    )(slot, fixed, start, dc, stat, y, z, xs, low, wide, before, final, step_w, bias, rate2, skip, gain)


PAIR_WIDTH = 2 * HEAD_SIZE


def stack_heads(value, pair):
    parts = []
    for h in range(value.shape[1] // HEAD_SIZE):
        part = value[:, h * HEAD_SIZE : (h + 1) * HEAD_SIZE]
        none = jnp.zeros_like(part)
        left = jnp.where(pair[h] == 0, part, none)
        right = jnp.where(pair[h] == 0, none, part)
        parts.append(jnp.concatenate([left, right], axis=1))
    return parts[0] if len(parts) == 1 else jnp.concatenate(parts, axis=0)


def unstack_heads(value, pair, rows):
    parts = []
    for h in range(value.shape[1] // rows):
        part = value[:, h * rows : (h + 1) * rows]
        parts.append(jnp.where(pair[h] == 0, part[:HEAD_SIZE], part[HEAD_SIZE:]))
    return jnp.transpose(parts[0] if len(parts) == 1 else jnp.concatenate(parts, axis=0))


def attn_kernel_fwd(
    slot, low_block, pair, q_ref, k_ref, vt_ref, gain_ref, o_ref, comb_ref, stat_ref
):
    u = pl.program_id(0)
    rows = q_ref.shape[0]
    heads = q_ref.shape[1] // HEAD_SIZE
    stacked = stack_heads(q_ref[...] * BF16(HEAD_SIZE**-0.5), pair)
    ones = jnp.ones((16, 2 * rows), BF16)

    def body(j, carry):
        top, acc = carry
        first = pl.multiple_of(slot[2 * j] * rows, rows)
        second = pl.multiple_of(slot[2 * j + 1] * rows, rows)
        kb = jnp.concatenate([k_ref[pl.ds(first, rows), :], k_ref[pl.ds(second, rows), :]], axis=0)
        vt = jnp.concatenate(
            [vt_ref[:, pl.ds(first, rows)], vt_ref[:, pl.ds(second, rows)]], axis=1
        )
        s = dot_nt(kb, stacked)
        new_top = jnp.maximum(top, jnp.max(s, axis=0, keepdims=True))
        p = jnp.exp(s - new_top).astype(BF16)
        acc = acc * jnp.exp(top - new_top) + dot_nn(jnp.concatenate([vt, ones], axis=0), p)
        return new_top, acc

    start = (
        jnp.full((1, heads * rows), -1e30, F32),
        jnp.zeros((PAIR_WIDTH + 16, heads * rows), F32),
    )
    top, acc = lax.fori_loop(low_block[u], u // 2 + 1, body, start)
    total = acc[PAIR_WIDTH : PAIR_WIDTH + 1]
    o = unstack_heads(acc[:PAIR_WIDTH] / total, pair, rows)
    o_ref[...] = o
    comb_ref[...] = (o * gain_ref[...]).astype(BF16)
    stat_ref[0, 0:1, :] = top + jnp.log(total)
    ones_row = jnp.ones((8, heads * HEAD_SIZE), F32)
    stat_ref[0, 1:2, 0:rows] = lax.dot_general(
        ones_row, o * o, (((1,), (1,)), ((), ())), precision=lax.Precision.HIGHEST,
        preferred_element_type=F32,
    )[0:1]


def attn_forward(slot, low_block, pair, q, k, vt, gain, unit_rows):
    rows, width = q.shape
    units = rows // unit_rows
    lanes = width // HEAD_SIZE * unit_rows
    return pl.pallas_call(
        attn_kernel_fwd,
        out_shape=(
            jax.ShapeDtypeStruct((rows, width), F32),
            jax.ShapeDtypeStruct((rows, width), BF16),
            jax.ShapeDtypeStruct((units, 8, lanes), F32),
        ),
        grid_spec=pltpu.PrefetchScalarGridSpec(
            num_scalar_prefetch=3,
            grid=(units,),
            in_specs=[
                unit_spec(unit_rows, width),
                whole_spec(k.shape),
                whole_spec(vt.shape),
                whole_spec((1, width)),
            ],
            out_specs=[
                unit_spec(unit_rows, width),
                unit_spec(unit_rows, width),
                pl.BlockSpec((1, 8, lanes), lambda u, slot, *_: (slot[u], 0, 0)),
            ],
        ),
        compiler_params=params(),
        cost_estimate=pl.CostEstimate(
            flops=2 * rows * rows * width, bytes_accessed=rows * width * 8,
            transcendentals=rows * rows * (width // HEAD_SIZE) // 2,
        ),
    )(slot, low_block, pair, q, k, vt, gain)


def attn_kernel_bwd(
    slot, low_block, pair, q_ref, o_ref, do_ref, stat_ref, k_ref, kt_ref, v_ref,
    dq_ref, dk_ref, dv_ref,
):
    u = pl.program_id(0)
    rows = q_ref.shape[0]
    heads = q_ref.shape[1] // HEAD_SIZE

    @pl.when(u == 0)
    def _():
        dk_ref[...] = jnp.zeros_like(dk_ref)
        dv_ref[...] = jnp.zeros_like(dv_ref)

    queries = stack_heads(q_ref[...] * BF16(HEAD_SIZE**-0.5), pair)
    do = do_ref[...]
    grads = stack_heads(do, pair)
    prod = do.astype(F32) * o_ref[...]
    prod = [prod[:, h * HEAD_SIZE : (h + 1) * HEAD_SIZE] for h in range(heads)]
    prod = prod[0] if heads == 1 else jnp.concatenate(prod, axis=0)
    delta = lax.dot_general(
        jnp.ones((8, HEAD_SIZE), F32), prod, (((1,), (1,)), ((), ())),
        precision=lax.Precision.HIGHEST, preferred_element_type=F32,
    )[0:1]
    log_total = stat_ref[0, 0:1, :]

    def body(j, dq):
        first = pl.multiple_of(slot[2 * j] * rows, rows)
        second = pl.multiple_of(slot[2 * j + 1] * rows, rows)
        kb = jnp.concatenate([k_ref[pl.ds(first, rows), :], k_ref[pl.ds(second, rows), :]], axis=0)
        vb = jnp.concatenate([v_ref[pl.ds(first, rows), :], v_ref[pl.ds(second, rows), :]], axis=0)
        kt = jnp.concatenate(
            [kt_ref[:, pl.ds(first, rows)], kt_ref[:, pl.ds(second, rows)]], axis=1
        )
        p = jnp.exp(dot_nt(kb, queries) - log_total)
        ds = (p * (dot_nt(vb, grads) - delta)).astype(BF16)
        dv = dot_nn(p.astype(BF16), grads)
        dk = dot_nn(ds, queries)
        dv_ref[pl.ds(first, rows), :] += dv[0:rows]
        dv_ref[pl.ds(second, rows), :] += dv[rows : 2 * rows]
        dk_ref[pl.ds(first, rows), :] += dk[0:rows]
        dk_ref[pl.ds(second, rows), :] += dk[rows : 2 * rows]
        return dq + dot_nn(kt, ds)

    dq = lax.fori_loop(
        low_block[u], u // 2 + 1, body, jnp.zeros((PAIR_WIDTH, heads * rows), F32)
    )
    dq_ref[...] = (unstack_heads(dq, pair, rows) * HEAD_SIZE**-0.5).astype(BF16)


def attn_backward(slot, low_block, pair, q, o, do, stat, k, kt, v, unit_rows):
    rows, width = q.shape
    units = rows // unit_rows
    lanes = width // HEAD_SIZE * unit_rows
    return pl.pallas_call(
        attn_kernel_bwd,
        out_shape=(
            jax.ShapeDtypeStruct((rows, width), BF16),
            jax.ShapeDtypeStruct(k.shape, F32),
            jax.ShapeDtypeStruct(v.shape, F32),
        ),
        grid_spec=pltpu.PrefetchScalarGridSpec(
            num_scalar_prefetch=3,
            grid=(units,),
            in_specs=[
                unit_spec(unit_rows, width),
                unit_spec(unit_rows, width),
                unit_spec(unit_rows, width),
                pl.BlockSpec((1, 8, lanes), lambda u, slot, *_: (slot[u], 0, 0)),
                whole_spec(k.shape),
                whole_spec(kt.shape),
                whole_spec(v.shape),
            ],
            out_specs=[unit_spec(unit_rows, width), whole_spec(k.shape), whole_spec(v.shape)],
        ),
        compiler_params=params(),
        cost_estimate=pl.CostEstimate(
            flops=5 * rows * rows * width, bytes_accessed=rows * width * 12,
            transcendentals=rows * rows * (width // HEAD_SIZE) // 2,
        ),
    )(slot, low_block, pair, q, o, do, stat, k, kt, v)


ORDER = (0, 2, 4, 6, 1, 3, 5, 7)
CUBE = len(ORDER)


def swap(value, mask):
    return lax.ppermute(value, "ctx", [(d, d ^ mask) for d in range(CUBE)])


def block_order(place, devices):
    if devices == CUBE:
        return place ^ jnp.array(ORDER, jnp.int32)
    return jnp.arange(devices, dtype=jnp.int32)


def block_index(owner, place, devices):
    if devices == CUBE:
        k = owner ^ place
        return k // 2 + (k % 2) * (CUBE // 2)
    return owner


def rows_gather(own, devices):
    pieces = gather_pieces(own, devices)
    return pieces[0] if len(pieces) == 1 else jnp.concatenate(pieces, axis=0)


def gather_pieces(own, devices):
    if devices != CUBE:
        return [lax.all_gather(own, "ctx", axis=0, tiled=True)]
    half = own.shape[0] // 2
    by_x, by_y, mate = swap(own, 2), swap(own, 4), swap(own, 1)
    far = jnp.concatenate([swap(by_x[:half], 4), swap(by_y[half:], 2)], axis=0)
    mates = [mate, swap(by_x, 1), swap(by_y, 1), swap(far, 1)]
    return [own, by_x, by_y, far] + mates


def rows_scatter(make, rows, devices):
    if devices != CUBE:
        return lax.psum_scatter(make(0, rows), "ctx", scatter_dimension=0, tiled=True).astype(F32)
    size = rows // CUBE
    half = size // 2
    from_mate = swap(make(rows // 2, rows), 1)
    total = make(0, rows // 2).astype(F32) + from_mate.astype(F32)
    cut = lambda i, a, b: total[i * size + a : i * size + b]
    far_x = swap(cut(3, 0, half).astype(BF16), 2)
    far_y = swap(cut(3, half, size).astype(BF16), 4)
    x_top = swap(cut(1, 0, half).astype(BF16), 2)
    y_end = swap(cut(2, half, size).astype(BF16), 4)
    x_end = swap((cut(1, half, size) + far_y.astype(F32)).astype(BF16), 2)
    y_top = swap((cut(2, 0, half) + far_x.astype(F32)).astype(BF16), 4)
    top = cut(0, 0, half) + x_top.astype(F32) + y_top.astype(F32)
    end = cut(0, half, size) + x_end.astype(F32) + y_end.astype(F32)
    return jnp.concatenate([top, end], axis=0)


def offload_gather(own, place, devices):
    got = lax.all_gather(own, "ctx", axis=0)
    if devices == CUBE:
        got = got[block_order(place, devices)]
    return got.reshape(-1, own.shape[1])


def offload_scatter(value, place, devices):
    blocks = value.reshape(devices, -1, value.shape[1])
    if devices == CUBE:
        blocks = blocks[block_index(jnp.arange(CUBE, dtype=jnp.int32), place, devices)]
    return lax.psum_scatter(blocks, "ctx", scatter_dimension=0, tiled=False).astype(F32)


def exchange(blocks):
    return lax.all_to_all(blocks, "ctx", split_axis=0, concat_axis=0, tiled=True)


def small_scatter(value, place, devices):
    if devices != CUBE:
        return lax.psum_scatter(value, "ctx", scatter_dimension=0, tiled=False)
    return sum(swap(value[i], k) if k else value[i] for i, k in enumerate(ORDER))


def small_gather(value, place, devices):
    if devices != CUBE:
        return lax.all_gather(value, "ctx", axis=0)
    return jnp.stack([swap(value, k) if k else value for k in ORDER])


def place_gather(value, place, devices):
    got = small_gather(value, place, devices)
    if devices != CUBE:
        return got
    return got[block_index(jnp.arange(CUBE, dtype=jnp.int32), place, devices)]


def all_sum(value, devices):
    if devices != CUBE:
        return lax.psum(value, "ctx")
    add = lambda a, b: (a.astype(F32) + b.astype(F32)).astype(BF16)
    value = add(value, swap(value, 1))
    half = value.shape[0] // 2
    top, end = value[:half], value[half:]
    top, end = add(top, swap(top, 2)), add(end, swap(end, 4))
    top, end = add(top, swap(top, 4)), add(end, swap(end, 2))
    return jnp.concatenate([top, end], axis=0)


def lane_gather(value):
    return lax.all_gather(value, "fsdp", axis=0, tiled=True)


def lane_scatter(value):
    return lax.psum_scatter(value, "fsdp", scatter_dimension=0, tiled=True)


def lane_shift(value, lanes, step):
    return lax.ppermute(value, "fsdp", [(z, (z + step) % lanes) for z in range(lanes)])


def lane_small_gather(value, lanes):
    lane = lax.axis_index("fsdp")
    got = jnp.stack([value] + [lane_shift(value, lanes, k) for k in range(1, lanes)])
    return got[(lane - jnp.arange(lanes, dtype=jnp.int32)) % lanes]


def lane_small_scatter(blocks, lanes):
    lane = lax.axis_index("fsdp")
    pick = lambda k: lax.dynamic_index_in_dim(blocks, (lane + k) % lanes, 0, False)
    return pick(0) + sum(lane_shift(pick(k), lanes, k) for k in range(1, lanes))


def after(value, *earlier):
    return lax.optimization_barrier((value,) + earlier)[0]


def columns_to_rows(value, devices):
    width = value.shape[1]
    got = exchange(value.reshape(devices, -1, width))
    return jnp.transpose(got, (1, 0, 2)).reshape(-1, devices * width)


def rows_to_columns(value, devices):
    rows = value.shape[0]
    blocks = jnp.transpose(value.reshape(rows, devices, -1), (1, 0, 2))
    return exchange(blocks).reshape(devices * rows, -1)


def pair_routes(devices):
    half = devices // 2
    first = [(d, 2 * d) for d in range(half)] + [(d, 2 * (d - half) + 1) for d in range(half, devices)]
    second = [(d, 2 * d + 1) for d in range(half)] + [(d, 2 * (d - half)) for d in range(half, devices)]
    return first, second


def split_pairs(value, place, devices):
    width = value.shape[1] // 2
    first, second = pair_routes(devices)
    low, high = value[:, :width], value[:, width:]
    early = place < devices // 2
    got_a = lax.ppermute(jnp.where(early, low, high), "ctx", first)
    got_b = lax.ppermute(jnp.where(early, high, low), "ctx", second)
    even = place % 2 == 0
    return jnp.where(even, got_a, got_b), jnp.where(even, got_b, got_a)


def join_pairs(left, right, place, devices):
    first, second = pair_routes(devices)
    even = place % 2 == 0
    got_a = lax.ppermute(jnp.where(even, left, right), "ctx", [(b, a) for a, b in first])
    got_b = lax.ppermute(jnp.where(even, right, left), "ctx", [(b, a) for a, b in second])
    early = place < devices // 2
    return jnp.concatenate([jnp.where(early, got_a, got_b), jnp.where(early, got_b, got_a)], axis=1)


def pad_to(value, size, axis):
    widths = [(0, 0)] * value.ndim
    widths[axis] = (0, size - value.shape[axis])
    return jnp.pad(value, widths)


def rms_factor(value):
    return lax.rsqrt(jnp.mean(value * value, axis=-1, keepdims=True) + EPS)


def norm_back(value, factor, gain, grad):
    weighted = grad * gain
    d_value = factor * weighted - value * factor * factor * factor * jnp.mean(
        value * weighted, axis=-1, keepdims=True
    )
    return d_value, jnp.sum(grad * value * factor, axis=0)


def shards(
    tokens, cotangent, unit_order, block_seq, meta_tokens, input_gain, query_key_value_weight, w_xz,
    conv_kernel, state_proj, step_proj, step_bias, decay_log, skip_gain, attn_gain, ssm_gain,
    out_proj, ffn_gain, w_gate, w_up, w_down,
):
    devices = lax.axis_size("ctx")
    lanes = lax.axis_size("fsdp")
    place = lax.axis_index("ctx")
    own_rows = tokens.shape[1]
    model = tokens.shape[2]
    unit_rows = own_rows // 2
    slot_unit = unit_order[0]
    units = slot_unit.shape[0]
    rows = units * unit_rows
    width = conv_kernel.shape[1]
    hidden_width = w_gate.shape[1]
    heads = -(-QUERY_HEADS // devices)
    head_width = heads * HEAD_SIZE
    group = QUERY_HEADS // KEY_VALUE_HEADS
    query_width = QUERY_HEADS * HEAD_SIZE
    kv_width = KEY_VALUE_HEADS * HEAD_SIZE
    model_part = input_gain.shape[0]

    slot_ids = jnp.arange(units, dtype=jnp.int32)
    fixed = jnp.sum(
        jnp.where(slot_unit[None, :] == slot_ids[:, None], slot_ids[None, :], 0), axis=1
    ).astype(jnp.int32)
    slot = (2 * block_index(fixed // 2, place, devices) + fixed % 2).astype(jnp.int32)
    unit_seq = jnp.repeat(block_seq[0], 2)
    starts = jnp.concatenate([jnp.ones((1,), jnp.bool_), unit_seq[1:] != unit_seq[:-1]])
    starts_int = starts.astype(jnp.int32)
    low_block = (jnp.sum(unit_seq[None, :] < unit_seq[:, None], axis=1) // 2).astype(jnp.int32)
    my_units = lax.dynamic_slice_in_dim(slot_unit, 2 * place, 2)
    my_start = jnp.any((my_units[:, None] == slot_ids[None, :]) & starts[None, :], axis=1)

    x_part, z_part = split_pairs(w_xz, place, devices)

    small = after(
        jnp.concatenate([conv_kernel, state_proj, step_proj, decay_log], axis=0), x_part
    )
    small_all = lane_small_gather(small, lanes)
    marks = [conv_kernel.shape[0], state_proj.shape[0], step_proj.shape[0], decay_log.shape[0]]
    ends = [sum(marks[: i + 1]) for i in range(4)]
    conv_w = small_all[:, : ends[0]].reshape(-1, width).astype(F32)
    sel_w = small_all[:, ends[0] : ends[1]].reshape(-1, width)
    step_w = small_all[:, ends[1] : ends[2]].reshape(-1, width)
    decay = small_all[:, ends[2] :].reshape(-1, width).astype(F32)
    rate = -jnp.exp(decay)
    rate2 = rate * LOG2E
    meta_part = lane_small_gather(after(meta_tokens, x_part), lanes).reshape(-1, model_part)
    meta_rows = meta_part.shape[0]
    wide = jnp.concatenate(
        [meta_part, input_gain[None], ffn_gain[None], attn_gain[None]], axis=0
    )
    wide = place_gather(wide, place, devices)
    wide = jnp.transpose(wide, (1, 0, 2)).reshape(-1, model).astype(F32)
    meta = wide[:meta_rows]
    gain_in = wide[meta_rows]
    gain_ffn = wide[meta_rows + 1]
    gain_attn = lax.dynamic_slice_in_dim(
        pad_to(wide[meta_rows + 2], devices * head_width, 0), place * head_width, head_width
    )[None]
    bias = step_bias.astype(F32)[None]
    skip = skip_gain.astype(F32)[None]
    gain_ssm = ssm_gain.astype(F32)[None]

    first_kv = (place * heads) // group
    qkv_row = place_gather(after(query_key_value_weight, x_part), place, devices)
    qkv_row = jnp.transpose(qkv_row, (1, 0, 2)).reshape(qkv_row.shape[1], -1)
    q_part = lax.dynamic_slice_in_dim(
        pad_to(qkv_row[:, :query_width], devices * head_width, 1), place * head_width, head_width, 1
    )
    kv_room = (devices * heads // group + 3) * HEAD_SIZE
    k_part = lax.dynamic_slice_in_dim(
        pad_to(qkv_row[:, query_width : query_width + kv_width], kv_room, 1),
        first_kv * HEAD_SIZE, 2 * HEAD_SIZE, 1,
    )
    v_part = lax.dynamic_slice_in_dim(
        pad_to(qkv_row[:, query_width + kv_width :], kv_room, 1),
        first_kv * HEAD_SIZE, 2 * HEAD_SIZE, 1,
    )
    pair = jnp.clip(
        (place * heads + jnp.arange(heads, dtype=jnp.int32)) // group - first_kv, 0, 1
    ).astype(jnp.int32)
    qkv_width = head_width + 4 * HEAD_SIZE
    x_w = lane_gather(x_part)
    qkvz_w = lane_gather(jnp.concatenate([q_part, k_part, v_part, z_part], axis=1))
    qkv_w = qkvz_w[:, :qkv_width]
    z_w = qkvz_w[:, qkv_width:]
    out_cols = lane_gather(after(out_proj, x_w))
    gate_up_w = lane_gather(jnp.concatenate([after(w_gate, qkvz_w), w_up], axis=1))
    gate_w = gate_up_w[:, :hidden_width]
    up_w = gate_up_w[:, hidden_width:]
    down_cols = lane_gather(after(w_down, out_cols))
    blocks = jnp.concatenate(
        [
            pad_to(out_cols[:query_width], devices * head_width, 0).reshape(
                devices, head_width, model_part
            ),
            out_cols[query_width:].reshape(devices, width, model_part),
        ],
        axis=1,
    )
    out_w = columns_to_rows(blocks.reshape(-1, model_part), devices)
    down_w = columns_to_rows(down_cols, devices)

    own_tok = tokens[0]
    slot_start = jnp.sum(
        jnp.where(slot[None, :] == slot_ids[:, None], starts_int[None, :], 0), axis=1
    ).astype(jnp.int32)
    normed = norm_all(slot_start, meta, gain_in[None], gather_pieces(own_tok, devices))
    resid = jnp.where(
        my_start[:, None, None], meta[None], own_tok.reshape(2, unit_rows, model).astype(F32)
    ).reshape(own_rows, model)
    in_factor = rms_factor(resid)

    x_in = dot_nn(normed, x_w).astype(BF16)
    cot = offload_gather(after(cotangent[0], gate_up_w), place, devices)
    conv_out, ssm_in, select = conv_forward(
        slot, fixed, starts_int, x_in, conv_w, sel_w, unit_rows
    )
    select = all_sum(select, devices).astype(F32)
    qkv = dot_nn(normed, qkv_w).astype(BF16)
    queries = qkv[:, :head_width]
    keys = qkv[:, head_width : head_width + PAIR_WIDTH]
    values = qkv[:, head_width + PAIR_WIDTH :]
    attn, attn_comb, attn_stat = attn_forward(
        slot, low_block, pair, queries, keys, jnp.transpose(values), gain_attn, unit_rows
    )
    attn_out = rows_scatter(
        lambda a, b: dot_nn(attn_comb[a:b], out_w[:head_width]).astype(BF16), rows, devices
    )
    z_gate = dot_nn(normed, z_w).astype(BF16)
    step_low = select[:, :DT_RANK].astype(BF16)
    bc = jnp.transpose(select[:, DT_RANK:].reshape(units, unit_rows, 2 * STATE), (0, 2, 1))
    y_total, ssm_comb, ssm_square, wide_bc, states, last_states = scan_forward(
        slot, fixed, starts_int, ssm_in, z_gate, step_low, bc, step_w, bias, rate2, skip, gain_ssm,
        unit_rows,
    )
    ssm_out = rows_scatter(
        lambda a, b: dot_nn(ssm_comb[a:b], out_w[head_width:]).astype(BF16), rows, devices
    )
    squares = jnp.stack(
        [
            attn_stat[:, 1, :unit_rows].reshape(devices, own_rows),
            ssm_square[:, 0].reshape(devices, own_rows),
        ],
        axis=1,
    )
    squares = small_scatter(squares, place, devices)
    own_factors = lax.rsqrt(squares / jnp.array([[query_width], [devices * width]], F32) + EPS)
    mid = (
        resid
        + 0.5 * own_factors[0][:, None] * attn_out
        + 0.5 * own_factors[1][:, None] * ssm_out
    )
    mid_factor = rms_factor(mid)
    ffn_in = rows_gather((mid * mid_factor * gain_ffn).astype(BF16), devices)

    gate = dot_nn(ffn_in, gate_w)
    up = dot_nn(ffn_in, up_w)
    sig = jax.nn.sigmoid(gate)
    act = gate * sig
    hidden = (act * up).astype(BF16)
    d_hidden = dot_nt(cot, down_w)
    d_gate = (d_hidden * up * (sig * (1.0 + gate * (1.0 - sig)))).astype(BF16)
    d_up = (d_hidden * act).astype(BF16)
    d_ffn = rows_scatter(
        lambda a, b: (dot_nt(d_gate[a:b], gate_w) + dot_nt(d_up[a:b], up_w)).astype(BF16),
        rows, devices,
    )
    ffn_out = offload_scatter(dot_nn(hidden, down_w).astype(BF16), place, devices)
    layer_out = (mid + ffn_out).astype(BF16)[None]
    down_part = dot_tn(hidden, cot).astype(BF16)
    gate_up_part = jnp.concatenate(
        [dot_tn(ffn_in, d_gate).astype(BF16), dot_tn(ffn_in, d_up).astype(BF16)], axis=1
    )
    down_grad = lane_scatter(rows_to_columns(down_part, devices)).astype(F32)
    gate_up_grad = lane_scatter(gate_up_part).astype(F32)
    gate_grad, up_grad = gate_up_grad[:, :hidden_width], gate_up_grad[:, hidden_width:]
    d_ffn = after(d_ffn, gate_up_part, down_part)

    d_mid_norm, ffn_gain_part = norm_back(mid, mid_factor, gain_ffn, d_ffn)
    d_mid = cotangent[0].astype(F32) + d_mid_norm
    d_branch_own = d_mid.astype(BF16)
    d_branch = rows_gather(d_branch_own, devices)
    branch_f = d_branch_own.astype(F32)
    dots = jnp.stack(
        [
            jnp.sum(branch_f * attn_out, axis=1) * (0.5 / query_width),
            jnp.sum(branch_f * ssm_out, axis=1) * (0.5 / (devices * width)),
        ]
    )
    shifts = dots * own_factors * own_factors * own_factors
    spread_rows = small_gather(jnp.concatenate([own_factors, shifts], axis=0), place, devices)
    spread_rows = jnp.transpose(spread_rows, (1, 0, 2)).reshape(4, rows)
    factors, shifts = spread_rows[:2], spread_rows[2:]

    d_comb_attn = dot_nt(d_branch, out_w[:head_width])
    d_comb_ssm = dot_nt(d_branch, out_w[head_width:])
    attn_mixed = (attn * (0.5 * factors[0][:, None] * gain_attn)).astype(BF16)
    ssm_mixed = (ssm_comb.astype(F32) * (0.5 * factors[1][:, None])).astype(BF16)
    out_part = dot_tn(jnp.concatenate([attn_mixed, ssm_mixed], axis=1), d_branch).astype(BF16)
    out_back = rows_to_columns(out_part, devices).reshape(devices, -1, model_part)
    out_grad = lane_scatter(
        jnp.concatenate(
            [
                out_back[:, :head_width].reshape(-1, model_part)[:query_width],
                out_back[:, head_width:].reshape(-1, model_part),
            ],
            axis=0,
        )
    ).astype(F32)
    half = 0.5 * d_comb_attn
    d_attn = factors[0][:, None] * (half * gain_attn) - attn * shifts[0][:, None]
    attn_gain_part = jnp.sum(half * attn * factors[0][:, None], axis=0)
    stat = jnp.transpose(pad_to(jnp.stack([factors[1], shifts[1]]), 128, 0))
    d_z, x_part_grad, d_low, d_bc, step_grad, vec_grads, decay_sum = scan_backward(
        slot, fixed, starts_int, d_comb_ssm, stat, y_total, z_gate, ssm_in, step_low, wide_bc, states,
        last_states, step_w, bias, rate2, skip, gain_ssm, unit_rows,
    )
    d_bc = jnp.transpose(
        d_bc[:, :, 0].reshape(units, 2, unit_rows, STATE), (0, 2, 1, 3)
    ).reshape(rows, 2 * STATE)
    d_select = all_sum(jnp.concatenate([d_low, d_bc.astype(BF16)], axis=1), devices)
    z_part_grad = dot_tn(normed, d_z).astype(BF16)
    d_query, d_keys, d_values = attn_backward(
        slot, low_block, pair, queries, attn, d_attn.astype(BF16), attn_stat, keys,
        jnp.transpose(keys), values, unit_rows,
    )
    d_qkv = jnp.concatenate([d_query, d_keys.astype(BF16), d_values.astype(BF16)], axis=1)
    qkv_part_grad = dot_tn(normed, d_qkv).astype(BF16)
    d_select = after(d_select, z_part_grad, qkv_part_grad)
    d_x, conv_grads, select_grad = conv_backward(
        slot, fixed, starts_int, d_select, x_part_grad, conv_out, x_in, ssm_in, conv_w, sel_w,
        unit_rows,
    )
    d_normed = rows_scatter(
        lambda a, b: (
            dot_nt(d_qkv[a:b], qkv_w) + dot_nt(d_x[a:b], x_w) + dot_nt(d_z[a:b], z_w)
        ).astype(BF16),
        rows, devices,
    )
    z_grad = lane_scatter(z_part_grad)
    in_grad = lane_scatter(qkv_part_grad)
    x_grad = lane_scatter(dot_tn(normed, d_x).astype(BF16))
    xz_grad = join_pairs(x_grad, z_grad, place, devices).astype(F32)
    spread = jnp.zeros((in_grad.shape[0], devices * head_width), BF16)
    spread = lax.dynamic_update_slice_in_dim(spread, in_grad[:, :head_width], place * head_width, 1)
    kv_zero = jnp.zeros((in_grad.shape[0], kv_room), BF16)
    qkv_full = jnp.concatenate(
        [
            spread[:, :query_width],
            lax.dynamic_update_slice_in_dim(
                kv_zero, in_grad[:, head_width : head_width + 2 * HEAD_SIZE],
                first_kv * HEAD_SIZE, 1,
            )[:, :kv_width],
            lax.dynamic_update_slice_in_dim(
                kv_zero, in_grad[:, head_width + 2 * HEAD_SIZE : qkv_width],
                first_kv * HEAD_SIZE, 1,
            )[:, :kv_width],
        ],
        axis=1,
    )
    part = query_key_value_weight.shape[1]
    qkv_blocks = jnp.transpose(qkv_full.reshape(-1, devices, part), (1, 0, 2))
    qkv_grad = lax.psum_scatter(
        qkv_blocks, "ctx", scatter_dimension=0, tiled=False
    ).astype(F32)

    d_norm_in, in_gain_part = norm_back(resid, in_factor, gain_in, d_normed)
    d_resid = d_mid + d_norm_in
    halves = [
        (my_start[i], d_resid[i * unit_rows : (i + 1) * unit_rows]) for i in range(2)
    ]
    tokens_grad = jnp.concatenate(
        [jnp.where(flag, 0.0, half).astype(BF16) for flag, half in halves], axis=0
    )[None]
    meta_sum = sum(jnp.where(flag, half, 0.0) for flag, half in halves)

    gain_rows = jnp.stack(
        [
            in_gain_part,
            ffn_gain_part,
            lax.dynamic_update_slice_in_dim(
                jnp.zeros((devices * head_width,), F32), attn_gain_part, place * head_width, 0
            )[:query_width],
        ]
    )
    by_lane = jnp.concatenate(
        [
            meta_sum.reshape(lanes, -1, model),
            jnp.broadcast_to(gain_rows[None], (lanes, 3, model)),
        ],
        axis=1,
    )
    count = by_lane.shape[1]
    packed = jnp.transpose(
        by_lane.reshape(lanes, count, devices, model_part), (0, 2, 1, 3)
    ).reshape(lanes * devices, count, model_part)
    totals = jnp.sum(
        lax.all_to_all(
            packed.astype(BF16), ("fsdp", "ctx"), split_axis=0, concat_axis=0, tiled=True
        ).astype(F32),
        axis=0,
    )
    counts = [CONV, select_grad.shape[0], DT_RANK, STATE]
    local = jnp.concatenate(
        [
            part.reshape(lanes, -1, width)
            for part in (conv_grads[:CONV], select_grad, step_grad, rate * decay_sum)
        ]
        + [jnp.broadcast_to(vec_grads[None, :3], (lanes, 3, width))],
        axis=1,
    )
    local = lane_small_scatter(local, lanes)
    ends = [sum(counts[:i]) // lanes for i in range(5)]
    piece = lambda i: local[ends[i] : ends[i + 1]]
    vec = lambda i: local[ends[4] + i]
    return (
        layer_out,
        tokens_grad,
        totals[: count - 3],
        totals[count - 3],
        qkv_grad,
        xz_grad,
        piece(0),
        piece(1),
        piece(2),
        vec(2),
        piece(3),
        vec(1),
        totals[count - 1],
        vec(0),
        out_grad,
        totals[count - 2],
        gate_grad,
        up_grad,
        down_grad,
    )


def solution(mesh):
    rows = P("fsdp", "ctx", None)
    index = P("fsdp", None)
    mat = P("fsdp", "ctx")
    vec = P("ctx")
    return jax.shard_map(
        shards,
        mesh=mesh,
        in_specs=(
            rows, rows, index, index, mat, vec, mat, mat, mat, mat, mat, vec, mat, vec, vec, vec,
            mat, vec, mat, mat, mat,
        ),
        out_specs=(
            rows, rows, mat, vec, mat, mat, mat, mat, mat, vec, mat, vec, vec, vec, mat, vec, mat,
            mat, mat,
        ),
        check_vma=False,
    )
```

```python
import functools
import jax
import jax.numpy as jnp
from jax import lax
from jax.experimental import pallas as pl
from jax.experimental.layout import Layout, with_layout_constraint
from jax.experimental.pallas import tpu as pltpu
from jax.sharding import PartitionSpec as P

QUERY_HEADS = 25
KEY_VALUE_HEADS = 5
HEAD_SIZE = 64
INNER = 3200
STATE = 16
CONV = 4
DT_RANK = 100
EPS = 1e-06
LOG2E = 1.4426950408889634
LN2 = 0.6931471805599453
VMEM_LIMIT = 56 * 1024 * 1024
STEP_GROUP = 8
SMALL_COST = pl.CostEstimate(flops=1, bytes_accessed=1, transcendentals=0)
F32 = jnp.float32
BF16 = jnp.bfloat16


def sigmoid(value):
    return 0.5 * jnp.tanh(0.5 * value) + 0.5


def dot_nn(left, right):
    return lax.dot_general(left, right, (((1,), (0,)), ((), ())), preferred_element_type=F32)


def dot_nt(left, right):
    return lax.dot_general(left, right, (((1,), (1,)), ((), ())), preferred_element_type=F32)


def dot_tn(left, right):
    return lax.dot_general(left, right, (((0,), (0,)), ((), ())), preferred_element_type=F32)


def unit_spec(rows, width, reverse_units=None, which=0):
    if reverse_units is None:
        return pl.BlockSpec((rows, width), lambda u, *maps: (maps[which][u], 0))
    last = reverse_units - 1
    return pl.BlockSpec((rows, width), lambda i, *maps: (maps[which][last - i], 0))


def whole_spec(shape):
    zeros = (0,) * len(shape)
    return pl.BlockSpec(shape, lambda *_: zeros)


def later(kernel, before, deps):
    if not deps:
        return kernel
    count = len(deps)
    return lambda *refs: kernel(*refs[:before], *refs[before + count :])


def wait_specs(deps):
    return [pl.BlockSpec(memory_space=pl.ANY)] * len(deps)


def hold_kernel(in_ref, out_ref):
    out_ref[...] = in_ref[...]


def hold(value, *deps):
    return pl.pallas_call(
        later(hold_kernel, 1, deps),
        out_shape=jax.ShapeDtypeStruct(value.shape, value.dtype),
        in_specs=[pl.BlockSpec(memory_space=pltpu.VMEM)] + wait_specs(deps),
        out_specs=pl.BlockSpec(memory_space=pltpu.VMEM),
        compiler_params=pltpu.CompilerParams(vmem_limit_bytes=VMEM_LIMIT),
        cost_estimate=SMALL_COST,
    )(value, *deps)


def params():
    return pltpu.CompilerParams(
        dimension_semantics=("arbitrary",), vmem_limit_bytes=VMEM_LIMIT
    )


def norm_unit(value, meta, gain, begins):
    value = jnp.where(begins == 1, meta, value.astype(F32))
    factor = lax.rsqrt(jnp.mean(value * value, axis=-1, keepdims=True) + EPS)
    return (value * factor * gain).astype(BF16)


def norm_pieces_kernel(begins, meta_ref, gain_ref, *refs):
    pieces, out_ref = refs[:-1], refs[-1]
    unit_rows = meta_ref.shape[0]
    unit = 0
    for piece in pieces:
        for i in range(piece.shape[0] // unit_rows):
            out_ref[unit * unit_rows : (unit + 1) * unit_rows, :] = norm_unit(
                piece[i * unit_rows : (i + 1) * unit_rows, : meta_ref.shape[1]], meta_ref[...],
                gain_ref[...], begins[unit],
            )
            unit += 1


def norm_rows_kernel(begins, meta_ref, gain_ref, in_ref, out_ref):
    out_ref[...] = norm_unit(
        in_ref[:, : meta_ref.shape[1]], meta_ref[...], gain_ref[...], begins[pl.program_id(0)]
    )


def norm_all(begins, meta, gain, pieces):
    unit_rows, width = meta.shape
    rows = sum(piece.shape[0] for piece in pieces)
    shape = jax.ShapeDtypeStruct((rows, width), BF16)
    if len(pieces) > 1:
        return pl.pallas_call(
            norm_pieces_kernel,
            out_shape=shape,
            in_specs=[pl.BlockSpec(memory_space=pltpu.SMEM)]
            + [pl.BlockSpec(memory_space=pltpu.VMEM)] * (2 + len(pieces)),
            out_specs=pl.BlockSpec(memory_space=pltpu.VMEM),
            compiler_params=pltpu.CompilerParams(vmem_limit_bytes=VMEM_LIMIT),
        )(begins, meta, gain, *pieces)
    by_unit = lambda size: pl.BlockSpec((unit_rows, size), lambda u, *_: (u, 0))
    return pl.pallas_call(
        norm_rows_kernel,
        out_shape=shape,
        grid_spec=pltpu.PrefetchScalarGridSpec(
            num_scalar_prefetch=1,
            grid=(rows // unit_rows,),
            in_specs=[whole_spec((unit_rows, width)), whole_spec((1, width)), by_unit(pieces[0].shape[1])],
            out_specs=by_unit(width),
        ),
        compiler_params=params(),
    )(begins, meta, gain, pieces[0])


def conv_kernel_fwd(slot, fixed, start, xin_ref, w_ref, sel_ref, xc_ref, xs_ref, part_ref, ext):
    u = pl.program_id(0)
    rows = xin_ref.shape[0]
    keep = jnp.where(start[u] == 1, 0.0, 1.0)

    @pl.when(u == 0)
    def _():
        ext[...] = jnp.zeros_like(ext)

    ext[0:8, :] = ext[rows : rows + 8, :] * keep
    ext[8 : 8 + rows, :] = xin_ref[...].astype(F32)
    acc = w_ref[0:1, :] * ext[5 : 5 + rows, :]
    for k in range(1, CONV):
        acc = acc + w_ref[k : k + 1, :] * ext[5 + k : 5 + k + rows, :]
    xc_ref[...] = acc
    xs = (acc * sigmoid(acc)).astype(BF16)
    xs_ref[...] = xs
    part_ref[...] = dot_nt(xs, sel_ref[...]).astype(BF16)


def conv_forward(slot, fixed, start, xin, conv_w, sel_w, unit_rows):
    rows, width = xin.shape
    units = rows // unit_rows
    sel_rows = sel_w.shape[0]
    return pl.pallas_call(
        conv_kernel_fwd,
        out_shape=(
            jax.ShapeDtypeStruct((rows, width), F32),
            jax.ShapeDtypeStruct((rows, width), BF16),
            jax.ShapeDtypeStruct((rows, sel_rows), BF16),
        ),
        grid_spec=pltpu.PrefetchScalarGridSpec(
            num_scalar_prefetch=3,
            grid=(units,),
            in_specs=[
                unit_spec(unit_rows, width),
                whole_spec((CONV, width)),
                whole_spec((sel_rows, width)),
            ],
            out_specs=[
                unit_spec(unit_rows, width),
                unit_spec(unit_rows, width),
                unit_spec(unit_rows, sel_rows, None, 1),
            ],
            scratch_shapes=[pltpu.VMEM((unit_rows + 8, width), F32)],
        ),
        compiler_params=params(),
        cost_estimate=SMALL_COST,
    )(slot, fixed, start, xin, conv_w, sel_w)


def conv_kernel_bwd(
    slot, fixed, start, dsel_ref, part_ref, xc_ref, xin_ref, xs_ref, w_ref, sel_ref,
    dxin_ref, gw_ref, gsel_ref, dext,
):
    i = pl.program_id(0)
    units = pl.num_programs(0)
    u = units - 1 - i
    rows = xin_ref.shape[0]
    after = jnp.where(start[jnp.minimum(u + 1, units - 1)] == 1, 0.0, 1.0)

    @pl.when(i == 0)
    def _():
        dext[...] = jnp.zeros_like(dext)
        gw_ref[...] = jnp.zeros_like(gw_ref)
        gsel_ref[...] = jnp.zeros_like(gsel_ref)

    gsel_ref[...] += dot_tn(dsel_ref[...], xs_ref[...])
    dext[rows : rows + 8, :] = dext[0:8, :] * after
    xc = xc_ref[...]
    sig = sigmoid(xc)
    dxs = dot_nn(dsel_ref[...], sel_ref[...]) + part_ref[...]
    dxc = dxs * (sig * (1.0 + xc * (1.0 - sig)))
    dext[0:rows, :] = dxc
    acc = w_ref[CONV - 1 : CONV, :] * dxc
    for k in range(CONV - 1):
        off = CONV - 1 - k
        acc = acc + w_ref[k : k + 1, :] * dext[off : off + rows, :]
    dxin_ref[...] = acc.astype(BF16)
    xin = xin_ref[...].astype(F32)
    for k in range(CONV):
        off = CONV - 1 - k
        gw_ref[k : k + 1, :] += jnp.sum(dext[off : off + rows, :] * xin, axis=0, keepdims=True)


def conv_backward(slot, fixed, start, dsel, part, xc, xin, xs, conv_w, sel_w, unit_rows, deps=()):
    rows, width = xin.shape
    units = rows // unit_rows
    sel_rows = sel_w.shape[0]
    return pl.pallas_call(
later(        conv_kernel_bwd, 10, deps),
        out_shape=(
            jax.ShapeDtypeStruct((rows, width), BF16),
            jax.ShapeDtypeStruct((8, width), F32),
            jax.ShapeDtypeStruct((sel_rows, width), F32),
        ),
        grid_spec=pltpu.PrefetchScalarGridSpec(
            num_scalar_prefetch=3,
            grid=(units,),
            in_specs=[
                unit_spec(unit_rows, sel_rows, units, 1),
                unit_spec(unit_rows, width, units),
                unit_spec(unit_rows, width, units),
                unit_spec(unit_rows, width, units),
                unit_spec(unit_rows, width, units),
                whole_spec((CONV, width)),
                whole_spec((sel_rows, width)),
            ] + wait_specs(deps),
            out_specs=[
                unit_spec(unit_rows, width, units),
                whole_spec((8, width)),
                whole_spec((sel_rows, width)),
            ],
            scratch_shapes=[pltpu.VMEM((unit_rows + 8, width), F32)],
        ),
        compiler_params=params(),
        cost_estimate=SMALL_COST,
    )(slot, fixed, start, dsel, part, xc, xin, xs, conv_w, sel_w, *deps)


def step_sizes(low_ref, step_ref, bias_ref):
    pre = dot_nn(low_ref[...], step_ref[...]) + bias_ref[...]
    return jnp.maximum(pre, 0.0) + jnp.log(1.0 + jnp.exp(-jnp.abs(pre)))


def lane_tiles(width):
    return [(lo, min(width, lo + 128)) for lo in range(0, width, 128)]


def fold_into(total, value, k):
    line = lax.broadcasted_iota(jnp.int32, (STEP_GROUP, 128), 0)
    return jnp.where(
        line == k, jnp.sum(value[0:8] + value[8:STATE], axis=0, keepdims=True), total
    )


def store_tiles(ref, value):
    for i, (lo, hi) in enumerate(lane_tiles(value.shape[1])):
        ref[i] = widen(value[:, lo:hi])


def load_tiles(ref, width):
    tiles = lane_tiles(width)
    return jnp.concatenate([ref[i, :, : hi - lo] for i, (lo, hi) in enumerate(tiles)], axis=1)


def widen(value):
    size = value.shape[1]
    if size == 128:
        return value
    return jnp.concatenate([value, jnp.zeros((value.shape[0], 128 - size), value.dtype)], axis=1)


def row_over_states(ref, i, t):
    return jnp.broadcast_to(ref[i, pl.ds(t, 1), :], (STATE, 128))


def scan_kernel_fwd(
    slot, fixed, start, xs_ref, z_ref, low_ref, bc_ref, step_ref, bias_ref, rate_ref, skip_ref,
    gain_ref, y_ref, comb_ref, square_ref, wide_ref, before_ref, last_ref, dt_buf, dtx_buf, y_buf,
    state,
):
    u = pl.program_id(0)
    rows = xs_ref.shape[0]
    width = xs_ref.shape[1]
    tiles = lane_tiles(width)
    count = len(tiles)
    keep = jnp.where(start[u] == 1, 0.0, 1.0)

    @pl.when(u == 0)
    def _():
        state[...] = jnp.zeros_like(state)

    xs = xs_ref[...].astype(F32)
    dt = step_sizes(low_ref, step_ref, bias_ref)
    store_tiles(dt_buf, dt)
    store_tiles(dtx_buf, dt * xs)
    rates = [widen(rate_ref[:, lo:hi]) for lo, hi in tiles]
    bc = bc_ref[0]
    for t in range(rows):
        wide_ref[0, t] = jnp.broadcast_to(bc[:, t : t + 1], (2 * STATE, 128))

    def group(g, carry):
        base = pl.multiple_of(g * STEP_GROUP, STEP_GROUP)
        h = list(carry)
        y = [jnp.zeros((STEP_GROUP, 128), F32) for _ in tiles]
        for k in range(STEP_GROUP):
            b = wide_ref[0, base + k, 0:STATE]
            c = wide_ref[0, base + k, STATE : 2 * STATE]
            for i in range(count):
                before_ref[0, base + k, i] = h[i]
                decay = jnp.exp2(row_over_states(dt_buf, i, base + k) * rates[i])
                h[i] = decay * h[i] + row_over_states(dtx_buf, i, base + k) * b
                y[i] = fold_into(y[i], c * h[i], k)
        for i in range(count):
            y_buf[i, pl.ds(base, STEP_GROUP), :] = y[i]
        return tuple(h)

    last = lax.fori_loop(
        0, rows // STEP_GROUP, group, tuple(state[i] * keep for i in range(count)), unroll=2
    )
    for i in range(count):
        state[i] = last[i]
        last_ref[0, i] = last[i]
    y = load_tiles(y_buf, width) + skip_ref[...] * xs
    y_ref[...] = y
    z = z_ref[...].astype(F32)
    ys = y * (z * sigmoid(z))
    comb_ref[...] = (ys * gain_ref[...]).astype(BF16)
    square_ref[...] = jnp.broadcast_to(jnp.sum(ys * ys, axis=1, keepdims=True), square_ref.shape)


def scan_forward(slot, fixed, start, xs, z, low, bc, step_w, bias, rate2, skip, gain, unit_rows, deps=()):
    rows, width = xs.shape
    units = rows // unit_rows
    rank = low.shape[1]
    count = -(-width // 128)
    return pl.pallas_call(
later(        scan_kernel_fwd, 12, deps),
        out_shape=(
            jax.ShapeDtypeStruct((rows, width), F32),
            jax.ShapeDtypeStruct((rows, width), BF16),
            jax.ShapeDtypeStruct((rows, 128), F32),
            jax.ShapeDtypeStruct((units, unit_rows, 2 * STATE, 128), F32),
            jax.ShapeDtypeStruct((units, unit_rows, count, STATE, 128), F32),
            jax.ShapeDtypeStruct((units, count, STATE, 128), F32),
        ),
        grid_spec=pltpu.PrefetchScalarGridSpec(
            num_scalar_prefetch=3,
            grid=(units,),
            in_specs=[
                unit_spec(unit_rows, width),
                unit_spec(unit_rows, width),
                unit_spec(unit_rows, rank, None, 1),
                pl.BlockSpec(
                    (1, 2 * STATE, unit_rows), lambda u, slot, fixed, *_: (fixed[u], 0, 0)
                ),
                whole_spec((rank, width)),
                whole_spec((1, width)),
                whole_spec((STATE, width)),
                whole_spec((1, width)),
                whole_spec((1, width)),
            ] + wait_specs(deps),
            out_specs=[
                unit_spec(unit_rows, width),
                unit_spec(unit_rows, width),
                unit_spec(unit_rows, 128),
                pl.BlockSpec((1, unit_rows, 2 * STATE, 128), lambda u, *_: (u, 0, 0, 0)),
                pl.BlockSpec((1, unit_rows, count, STATE, 128), lambda u, *_: (u, 0, 0, 0, 0)),
                pl.BlockSpec((1, count, STATE, 128), lambda u, *_: (u, 0, 0, 0)),
            ],
            scratch_shapes=[
                pltpu.VMEM((count, unit_rows, 128), F32),
                pltpu.VMEM((count, unit_rows, 128), F32),
                pltpu.VMEM((count, unit_rows, 128), F32),
                pltpu.VMEM((count, STATE, 128), F32),
            ],
        ),
        compiler_params=params(),
        cost_estimate=SMALL_COST,
    )(slot, fixed, start, xs, z, low, bc, step_w, bias, rate2, skip, gain, *deps)


def scan_kernel_bwd(
    slot, fixed, start, dc_ref, stat_ref, y_ref, z_ref, xs_ref, low_ref, wide_ref, before_ref,
    last_ref, step_ref, bias_ref, rate_ref, skip_ref, gain_ref,
    dz_ref, part_ref, dlow_ref, dbc_ref, gstep_ref, gvec_ref, gdecay_ref,
    dt_buf, dtx_buf, dy_buf, gx_buf, ddt_buf, pb_buf, pc_buf, adj,
):
    i = pl.program_id(0)
    units = pl.num_programs(0)
    u = units - 1 - i
    rows = xs_ref.shape[0]
    width = xs_ref.shape[1]
    after = jnp.where(start[jnp.minimum(u + 1, units - 1)] == 1, 0.0, 1.0)

    @pl.when(i == 0)
    def _():
        adj[...] = jnp.zeros_like(adj)
        gstep_ref[...] = jnp.zeros_like(gstep_ref)
        gvec_ref[...] = jnp.zeros_like(gvec_ref)
        gdecay_ref[...] = jnp.zeros_like(gdecay_ref)

    xs = xs_ref[...].astype(F32)
    dt = step_sizes(low_ref, step_ref, bias_ref)
    store_tiles(dt_buf, dt)
    store_tiles(dtx_buf, dt * xs)
    tiles = lane_tiles(width)
    count = len(tiles)
    rates = [widen(rate_ref[:, lo:hi]) for lo, hi in tiles]

    factor = stat_ref[:, 0:1]
    shift = stat_ref[:, 1:2]
    z = z_ref[...].astype(F32)
    sig = sigmoid(z)
    gate = z * sig
    y = y_ref[...]
    ys = y * gate
    half = 0.5 * dc_ref[...]
    dys = factor * (half * gain_ref[...]) - ys * shift
    dy = dys * gate
    dz_ref[...] = (dys * y * (sig * (1.0 + z * (1.0 - sig)))).astype(BF16)
    store_tiles(dy_buf, dy)
    gvec_ref[0:1, :] += jnp.sum(half * ys * factor, axis=0, keepdims=True)
    gvec_ref[1:2, :] += jnp.sum(dy * xs, axis=0, keepdims=True)

    def group(index, carry):
        lams, accs, states = list(carry[0]), list(carry[1]), list(carry[2])
        g = rows // STEP_GROUP - 1 - index
        base = pl.multiple_of(g * STEP_GROUP, STEP_GROUP)
        gx = [jnp.zeros((STEP_GROUP, 128), F32) for _ in tiles]
        ddt = [jnp.zeros((STEP_GROUP, 128), F32) for _ in tiles]
        for k in range(STEP_GROUP - 1, -1, -1):
            t = base + k
            b = wide_ref[0, t, 0:STATE]
            c = wide_ref[0, t, STATE : 2 * STATE]
            pb = pc = None
            for i in range(count):
                dt_row = row_over_states(dt_buf, i, t)
                dy_row = row_over_states(dy_buf, i, t)
                lam = lams[i] + c * dy_row
                more_c = dy_row * states[i]
                more_b = row_over_states(dtx_buf, i, t) * lam
                pc = more_c if pc is None else pc + more_c
                pb = more_b if pb is None else pb + more_b
                gx[i] = fold_into(gx[i], b * lam, k)
                lams[i] = jnp.exp2(dt_row * rates[i]) * lam
                states[i] = before_ref[0, t, i]
                w = lams[i] * states[i]
                ddt[i] = fold_into(ddt[i], rates[i] * w, k)
                accs[i] = accs[i] + dt_row * w
            pb_buf[t] = pb
            pc_buf[t] = pc
        for i in range(count):
            gx_buf[i, pl.ds(base, STEP_GROUP), :] = gx[i]
            ddt_buf[i, pl.ds(base, STEP_GROUP), :] = ddt[i]
        return tuple(lams), tuple(accs), tuple(states)

    lams, accs, _ = lax.fori_loop(
        0,
        rows // STEP_GROUP,
        group,
        (
            tuple(adj[i] * after for i in range(count)),
            tuple(jnp.zeros((STATE, 128), F32) for _ in tiles),
            tuple(last_ref[0, i] for i in range(count)),
        ),
    )
    for i, (lo, hi) in enumerate(tiles):
        adj[i] = lams[i]
        gdecay_ref[:, lo:hi] += accs[i][:, : hi - lo]
    gx = load_tiles(gx_buf, width)
    part_ref[...] = gx * dt + skip_ref[...] * dy
    ddt = gx * xs + LN2 * load_tiles(ddt_buf, width)
    dpre = (ddt * (1.0 - jnp.exp(-dt))).astype(BF16)
    gstep_ref[...] += dot_tn(low_ref[...], dpre)
    gvec_ref[2:3, :] += jnp.sum(dpre.astype(F32), axis=0, keepdims=True)
    dlow_ref[...] = dot_nt(dpre, step_ref[...]).astype(BF16)
    ones = jnp.ones((8, 128), BF16)
    dbc_ref[0, 0] = dot_nt(ones, pb_buf[...].reshape(rows * STATE, 128).astype(BF16))
    dbc_ref[0, 1] = dot_nt(ones, pc_buf[...].reshape(rows * STATE, 128).astype(BF16))


def scan_backward(
    slot, fixed, start, dc, stat, y, z, xs, low, wide, before, final, step_w, bias, rate2, skip, gain, unit_rows, deps=()
):
    rows, width = xs.shape
    units = rows // unit_rows
    rank = low.shape[1]
    count = -(-width // 128)
    last = units - 1
    return pl.pallas_call(
        later(scan_kernel_bwd, 3 + 14, deps),
        out_shape=(
            jax.ShapeDtypeStruct((rows, width), BF16),
            jax.ShapeDtypeStruct((rows, width), F32),
            jax.ShapeDtypeStruct((rows, rank), BF16),
            jax.ShapeDtypeStruct((units, 2, 8, unit_rows * STATE), F32),
            jax.ShapeDtypeStruct((rank, width), F32),
            jax.ShapeDtypeStruct((8, width), F32),
            jax.ShapeDtypeStruct((STATE, width), F32),
        ),
        grid_spec=pltpu.PrefetchScalarGridSpec(
            num_scalar_prefetch=3,
            grid=(units,),
            in_specs=[
                unit_spec(unit_rows, width, units),
                unit_spec(unit_rows, 128, units),
                unit_spec(unit_rows, width, units),
                unit_spec(unit_rows, width, units),
                unit_spec(unit_rows, width, units),
                unit_spec(unit_rows, rank, units, 1),
                pl.BlockSpec((1, unit_rows, 2 * STATE, 128), lambda i, *_: (last - i, 0, 0, 0)),
                pl.BlockSpec(
                    (1, unit_rows, count, STATE, 128), lambda i, *_: (last - i, 0, 0, 0, 0)
                ),
                pl.BlockSpec((1, count, STATE, 128), lambda i, *_: (last - i, 0, 0, 0)),
                whole_spec((rank, width)),
                whole_spec((1, width)),
                whole_spec((STATE, width)),
                whole_spec((1, width)),
                whole_spec((1, width)),
            ] + wait_specs(deps),
            out_specs=[
                unit_spec(unit_rows, width, units),
                unit_spec(unit_rows, width, units),
                unit_spec(unit_rows, rank, units, 1),
                pl.BlockSpec(
                    (1, 2, 8, unit_rows * STATE),
                    lambda i, slot, fixed, *_: (fixed[last - i], 0, 0, 0),
                ),
                whole_spec((rank, width)),
                whole_spec((8, width)),
                whole_spec((STATE, width)),
            ],
            scratch_shapes=[
                pltpu.VMEM((count, unit_rows, 128), F32),
                pltpu.VMEM((count, unit_rows, 128), F32),
                pltpu.VMEM((count, unit_rows, 128), F32),
                pltpu.VMEM((count, unit_rows, 128), F32),
                pltpu.VMEM((count, unit_rows, 128), F32),
                pltpu.VMEM((unit_rows, STATE, 128), F32),
                pltpu.VMEM((unit_rows, STATE, 128), F32),
                pltpu.VMEM((count, STATE, 128), F32),
            ],
        ),
        compiler_params=params(),
        cost_estimate=SMALL_COST,
    )(slot, fixed, start, dc, stat, y, z, xs, low, wide, before, final, step_w, bias, rate2, skip, gain, *deps)


PAIR_WIDTH = 2 * HEAD_SIZE


def stack_heads(value, pair):
    parts = []
    for h in range(value.shape[1] // HEAD_SIZE):
        part = value[:, h * HEAD_SIZE : (h + 1) * HEAD_SIZE]
        none = jnp.zeros_like(part)
        left = jnp.where(pair[h] == 0, part, none)
        right = jnp.where(pair[h] == 0, none, part)
        parts.append(jnp.concatenate([left, right], axis=1))
    return parts[0] if len(parts) == 1 else jnp.concatenate(parts, axis=0)


def unstack_heads(value, pair, rows):
    parts = []
    for h in range(value.shape[1] // rows):
        part = value[:, h * rows : (h + 1) * rows]
        parts.append(jnp.where(pair[h] == 0, part[:HEAD_SIZE], part[HEAD_SIZE:]))
    return jnp.transpose(parts[0] if len(parts) == 1 else jnp.concatenate(parts, axis=0))


def attn_kernel_fwd(
    slot, low_block, pair, q_ref, k_ref, vt_ref, gain_ref, o_ref, comb_ref, stat_ref
):
    u = pl.program_id(0)
    rows = q_ref.shape[0]
    heads = q_ref.shape[1] // HEAD_SIZE
    stacked = stack_heads(q_ref[...] * BF16(HEAD_SIZE**-0.5), pair)
    ones = jnp.ones((16, 2 * rows), BF16)

    def body(j, carry):
        top, acc = carry
        first = pl.multiple_of(slot[2 * j] * rows, rows)
        second = pl.multiple_of(slot[2 * j + 1] * rows, rows)
        kb = jnp.concatenate([k_ref[pl.ds(first, rows), :], k_ref[pl.ds(second, rows), :]], axis=0)
        vt = jnp.concatenate(
            [vt_ref[:, pl.ds(first, rows)], vt_ref[:, pl.ds(second, rows)]], axis=1
        )
        s = dot_nt(kb, stacked)
        new_top = jnp.maximum(top, jnp.max(s, axis=0, keepdims=True))
        p = jnp.exp(s - new_top).astype(BF16)
        acc = acc * jnp.exp(top - new_top) + dot_nn(jnp.concatenate([vt, ones], axis=0), p)
        return new_top, acc

    start = (
        jnp.full((1, heads * rows), -1e30, F32),
        jnp.zeros((PAIR_WIDTH + 16, heads * rows), F32),
    )
    top, acc = lax.fori_loop(low_block[u], u // 2 + 1, body, start)
    total = acc[PAIR_WIDTH : PAIR_WIDTH + 1]
    o = unstack_heads(acc[:PAIR_WIDTH] / total, pair, rows)
    o_ref[...] = o
    comb_ref[...] = (o * gain_ref[...]).astype(BF16)
    stat_ref[0, 0:1, :] = top + jnp.log(total)
    ones_row = jnp.ones((8, heads * HEAD_SIZE), F32)
    stat_ref[0, 1:2, 0:rows] = lax.dot_general(
        ones_row, o * o, (((1,), (1,)), ((), ())), precision=lax.Precision.HIGHEST,
        preferred_element_type=F32,
    )[0:1]


def attn_forward(slot, low_block, pair, q, k, vt, gain, unit_rows, deps=()):
    rows, width = q.shape
    units = rows // unit_rows
    lanes = width // HEAD_SIZE * unit_rows
    return pl.pallas_call(
later(        attn_kernel_fwd, 7, deps),
        out_shape=(
            jax.ShapeDtypeStruct((rows, width), F32),
            jax.ShapeDtypeStruct((rows, width), BF16),
            jax.ShapeDtypeStruct((units, 8, lanes), F32),
        ),
        grid_spec=pltpu.PrefetchScalarGridSpec(
            num_scalar_prefetch=3,
            grid=(units,),
            in_specs=[
                unit_spec(unit_rows, width),
                whole_spec(k.shape),
                whole_spec(vt.shape),
                whole_spec((1, width)),
            ] + wait_specs(deps),
            out_specs=[
                unit_spec(unit_rows, width),
                unit_spec(unit_rows, width),
                pl.BlockSpec((1, 8, lanes), lambda u, slot, *_: (slot[u], 0, 0)),
            ],
        ),
        compiler_params=params(),
        cost_estimate=SMALL_COST,
    )(slot, low_block, pair, q, k, vt, gain, *deps)


def attn_kernel_bwd(
    slot, low_block, pair, q_ref, o_ref, do_ref, stat_ref, k_ref, kt_ref, v_ref,
    dq_ref, dk_ref, dv_ref,
):
    u = pl.program_id(0)
    rows = q_ref.shape[0]
    heads = q_ref.shape[1] // HEAD_SIZE

    @pl.when(u == 0)
    def _():
        dk_ref[...] = jnp.zeros_like(dk_ref)
        dv_ref[...] = jnp.zeros_like(dv_ref)

    queries = stack_heads(q_ref[...] * BF16(HEAD_SIZE**-0.5), pair)
    do = do_ref[...]
    grads = stack_heads(do, pair)
    prod = do.astype(F32) * o_ref[...]
    prod = [prod[:, h * HEAD_SIZE : (h + 1) * HEAD_SIZE] for h in range(heads)]
    prod = prod[0] if heads == 1 else jnp.concatenate(prod, axis=0)
    delta = lax.dot_general(
        jnp.ones((8, HEAD_SIZE), F32), prod, (((1,), (1,)), ((), ())),
        precision=lax.Precision.HIGHEST, preferred_element_type=F32,
    )[0:1]
    log_total = stat_ref[0, 0:1, :]

    def body(j, dq):
        first = pl.multiple_of(slot[2 * j] * rows, rows)
        second = pl.multiple_of(slot[2 * j + 1] * rows, rows)
        kb = jnp.concatenate([k_ref[pl.ds(first, rows), :], k_ref[pl.ds(second, rows), :]], axis=0)
        vb = jnp.concatenate([v_ref[pl.ds(first, rows), :], v_ref[pl.ds(second, rows), :]], axis=0)
        kt = jnp.concatenate(
            [kt_ref[:, pl.ds(first, rows)], kt_ref[:, pl.ds(second, rows)]], axis=1
        )
        p = jnp.exp(dot_nt(kb, queries) - log_total)
        ds = (p * (dot_nt(vb, grads) - delta)).astype(BF16)
        dv = dot_nn(p.astype(BF16), grads)
        dk = dot_nn(ds, queries)
        dv_ref[pl.ds(first, rows), :] += dv[0:rows]
        dv_ref[pl.ds(second, rows), :] += dv[rows : 2 * rows]
        dk_ref[pl.ds(first, rows), :] += dk[0:rows]
        dk_ref[pl.ds(second, rows), :] += dk[rows : 2 * rows]
        return dq + dot_nn(kt, ds)

    dq = lax.fori_loop(
        low_block[u], u // 2 + 1, body, jnp.zeros((PAIR_WIDTH, heads * rows), F32)
    )
    dq_ref[...] = (unstack_heads(dq, pair, rows) * HEAD_SIZE**-0.5).astype(BF16)


def attn_backward(slot, low_block, pair, q, o, do, stat, k, kt, v, unit_rows, deps=()):
    rows, width = q.shape
    units = rows // unit_rows
    lanes = width // HEAD_SIZE * unit_rows
    return pl.pallas_call(
later(        attn_kernel_bwd, 10, deps),
        out_shape=(
            jax.ShapeDtypeStruct((rows, width), BF16),
            jax.ShapeDtypeStruct(k.shape, F32),
            jax.ShapeDtypeStruct(v.shape, F32),
        ),
        grid_spec=pltpu.PrefetchScalarGridSpec(
            num_scalar_prefetch=3,
            grid=(units,),
            in_specs=[
                unit_spec(unit_rows, width),
                unit_spec(unit_rows, width),
                unit_spec(unit_rows, width),
                pl.BlockSpec((1, 8, lanes), lambda u, slot, *_: (slot[u], 0, 0)),
                whole_spec(k.shape),
                whole_spec(kt.shape),
                whole_spec(v.shape),
            ] + wait_specs(deps),
            out_specs=[unit_spec(unit_rows, width), whole_spec(k.shape), whole_spec(v.shape)],
        ),
        compiler_params=params(),
        cost_estimate=SMALL_COST,
    )(slot, low_block, pair, q, o, do, stat, k, kt, v, *deps)


def fill_width(width):
    return -(-width // 128) * 128


def piece_specs(pieces, block_rows):
    if len(pieces) == 1:
        return [pl.BlockSpec((block_rows, pieces[0].shape[1]), lambda i, *_: (i, 0))]
    return [whole_spec(piece.shape) for piece in pieces]


def take_piece(refs, buf):
    if len(refs) == 1:
        buf[...] = refs[0][...]
        return
    step = pl.program_id(0)
    for k, ref in enumerate(refs):

        @pl.when(step == k)
        def _(ref=ref):
            buf[...] = ref[...]


def store_filled(ref, value):
    width = value.shape[1]
    ref[:, :width] = value.astype(ref.dtype)
    if ref.shape[1] > width:
        ref[:, width:] = jnp.zeros((ref.shape[0], ref.shape[1] - width), ref.dtype)


def whole_call(kernel, out_shape, *values, deps=()):
    return pl.pallas_call(
        later(kernel, len(values), deps),
        out_shape=out_shape,
        in_specs=[pl.BlockSpec(memory_space=pltpu.VMEM)] * len(values) + wait_specs(deps),
        out_specs=[pl.BlockSpec(memory_space=pltpu.VMEM)] * len(out_shape),
        compiler_params=pltpu.CompilerParams(vmem_limit_bytes=VMEM_LIMIT),
        cost_estimate=SMALL_COST,
    )(*values, *deps)


def chip_sum_kernel(mine, mate, own, to_x, to_y, keep_x, keep_y):
    size = own.shape[0]
    half = size // 2
    block = lambda i, a, b: (
        mine[i * size + a : i * size + b, :].astype(F32)
        + mate[i * size + a : i * size + b, :].astype(F32)
    )
    own[...] = block(0, 0, size)
    to_x[:half, :] = block(1, 0, half).astype(BF16)
    to_x[half:, :] = block(3, 0, half).astype(BF16)
    to_y[:half, :] = block(2, half, size).astype(BF16)
    to_y[half:, :] = block(3, half, size).astype(BF16)
    keep_x[...] = block(1, half, size)
    keep_y[...] = block(2, 0, half)


def near_sum_kernel(own, keep_x, keep_y, by_x, by_y, part, to_x, to_y):
    half = keep_x.shape[0]
    part[:half, :] = own[:half, :] + by_x[:half, :].astype(F32)
    part[half:, :] = own[half:, :] + by_y[:half, :].astype(F32)
    to_x[...] = (keep_x[...] + by_y[half:, :].astype(F32)).astype(BF16)
    to_y[...] = (keep_y[...] + by_x[half:, :].astype(F32)).astype(BF16)


def far_sum_kernel(part, by_y, by_x, out):
    half = by_y.shape[0]
    out[:half, :] = part[:half, :] + by_y[...].astype(F32)
    out[half:, :] = part[half:, :] + by_x[...].astype(F32)


def join_qkv_kernel(queries, keys, values, out):
    at = 0
    for ref in (queries, keys, values):
        out[:, at : at + ref.shape[1]] = ref[...].astype(BF16)
        at += ref.shape[1]


def cross_kernel(by_x, by_y, to_y, to_x):
    half = to_x.shape[0]
    to_y[...] = by_x[:half, :]
    to_x[...] = by_y[half:, :]


def join_kernel(left, right, out):
    out[:, : left.shape[1]] = left[...]
    out[:, left.shape[1] :] = right[...]


def two_sums_kernel(top, by_x, end, by_y, out_top, out_end):
    out_top[...] = (top[...].astype(F32) + by_x[...].astype(F32)).astype(BF16)
    out_end[...] = (end[...].astype(F32) + by_y[...].astype(F32)).astype(BF16)


def move_kernel(moves, in_ref, out_ref):
    out_ref[...] = jnp.zeros_like(out_ref)
    for a, lo, b, to, size in moves:
        out_ref[b, :, to : to + size] = in_ref[a, :, lo : lo + size]


def move_columns(value, moves, blocks, width, deps=()):
    return pl.pallas_call(
later(        functools.partial(move_kernel, tuple(moves)), 1, deps),
        out_shape=jax.ShapeDtypeStruct((blocks, value.shape[1], width), value.dtype),
        in_specs=[pl.BlockSpec(memory_space=pltpu.VMEM)] + wait_specs(deps),
        out_specs=pl.BlockSpec(memory_space=pltpu.VMEM),
        compiler_params=pltpu.CompilerParams(vmem_limit_bytes=VMEM_LIMIT),
    )(value, *deps)


def pick_kernel(cases, place_ref, in_ref, out_ref):
    out_ref[...] = jnp.zeros_like(out_ref)
    for place, moves in enumerate(cases):

        @pl.when(place_ref[0] == place)
        def _(moves=moves):
            for a, lo, _, to, size in moves:
                out_ref[:, to : to + size] = in_ref[a, :, lo : lo + size]


def pick_columns(value, place, cases, width, deps=()):
    return pl.pallas_call(
later(        functools.partial(pick_kernel, tuple(tuple(moves) for moves in cases)), 2, deps),
        out_shape=jax.ShapeDtypeStruct((value.shape[1], width), value.dtype),
        in_specs=[
            pl.BlockSpec(memory_space=pltpu.SMEM), pl.BlockSpec(memory_space=pltpu.VMEM),
        ] + wait_specs(deps),
        out_specs=pl.BlockSpec(memory_space=pltpu.VMEM),
        compiler_params=pltpu.CompilerParams(vmem_limit_bytes=VMEM_LIMIT),
    )(place.astype(jnp.int32).reshape(1), value, *deps)


def runs(spans, each):
    out = []
    for column, block, to, size in spans:
        while size > 0:
            part, lo = divmod(column, each)
            some = min(size, each - lo)
            out.append((part, lo, block, to, some))
            column, to, size = column + some, to + some, size - some
    return out


def project_kernel(count, added, cuts, half, *refs):
    lefts, weights = refs[:count], refs[count : 2 * count]
    outs = refs[2 * count + added :]
    total = None
    for left, weight, (lo, hi) in zip(lefts, weights, cuts):
        part = dot_nt(left[...], weight[:, lo:hi])
        total = part if total is None else total + part
    if added:
        total = total + refs[2 * count][:, : total.shape[1]].astype(F32)
    if half == 0:
        store_filled(outs[0], total)
        return

    @pl.when(pl.program_id(0) < half)
    def _():
        store_filled(outs[0], total)

    @pl.when(pl.program_id(0) >= half)
    def _():
        store_filled(outs[1], total)


def project(lefts, weights, cuts, block_rows, split=False, addend=None, deps=()):
    size = weights[0].shape[0]
    rows = lefts[0].shape[0]
    blocks = rows // block_rows
    half = blocks // 2 if split else 0
    by_rows_spec = lambda width: pl.BlockSpec(
        (block_rows, width), lambda i: ((i + half) % blocks, 0)
    )
    extra = [] if addend is None else [addend]
    shape = jax.ShapeDtypeStruct((rows // 2 if split else rows, fill_width(size)), BF16)
    block = (block_rows, fill_width(size))
    if split:
        out_shape = (shape, shape)
        out_specs = (
            pl.BlockSpec(block, lambda i: (jnp.minimum(i, half - 1), 0)),
            pl.BlockSpec(block, lambda i: (jnp.maximum(i - half, 0), 0)),
        )
    else:
        out_shape, out_specs = (shape,), (pl.BlockSpec(block, lambda i: (i, 0)),)
    return pl.pallas_call(
        later(
            functools.partial(project_kernel, len(lefts), bool(extra), cuts, half),
            2 * len(lefts) + len(extra), deps,
        ),
        out_shape=out_shape,
        grid=(blocks,),
        in_specs=[by_rows_spec(left.shape[1]) for left in lefts]
        + [whole_spec(weight.shape) for weight in weights]
        + [by_rows_spec(part.shape[1]) for part in extra]
        + wait_specs(deps),
        out_specs=out_specs,
        compiler_params=params(),
        cost_estimate=SMALL_COST,
    )(*lefts, *weights, *extra, *deps)


def ffn_kernel(count, model, order, *refs):
    x_refs, c_ref = refs[:count], refs[count]
    gate_ref, up_ref, down_ref = refs[count + 1 : count + 4]
    x_out, c_out, hidden_ref, dgate_ref, dup_ref, back_ref, out_ref, x_buf = refs[-8:]
    take_piece(x_refs, x_buf)
    x = x_buf[:, :model]
    c = c_ref[...]
    x_out[...] = x
    c_out[...] = c
    gate = dot_nn(x, gate_ref[...])
    up = dot_nn(x, up_ref[...])
    sig = sigmoid(gate)
    act = gate * sig
    hidden = (act * up).astype(BF16)
    d_hidden = dot_nn(c, down_ref[...])
    d_gate = (d_hidden * up * (sig * (1.0 + gate * (1.0 - sig)))).astype(BF16)
    d_up = (d_hidden * act).astype(BF16)
    hidden_ref[...] = hidden
    dgate_ref[...] = d_gate
    dup_ref[...] = d_up
    store_filled(back_ref, dot_nt(d_gate, gate_ref[...]) + dot_nt(d_up, up_ref[...]))
    store_filled(out_ref, dot_nt(hidden, down_ref[...]))


def ffn(order, x_pieces, cot, gate_w, up_w, down_wt, first, rows, block_rows, earlier=None):
    model, hidden = gate_w.shape
    all_rows = cot.shape[0]
    filled = x_pieces[0].shape[1]
    count = len(x_pieces)
    begin = first // block_rows
    carried = [model, model, hidden, hidden, hidden]
    extra = [] if earlier is None else list(earlier)
    in_count = count + 5
    place_spec = lambda width: pl.BlockSpec((block_rows, width), lambda i, *_: (begin + i, 0))
    own_spec = pl.BlockSpec((block_rows, fill_width(model)), lambda i, *_: (i, 0))
    return pl.pallas_call(
        functools.partial(ffn_kernel, count, model),
        out_shape=[jax.ShapeDtypeStruct((all_rows, width), BF16) for width in carried]
        + [jax.ShapeDtypeStruct((rows, fill_width(model)), BF16)] * 2,
        grid_spec=pltpu.PrefetchScalarGridSpec(
            num_scalar_prefetch=1,
            grid=(rows // block_rows,),
            in_specs=piece_specs(x_pieces, block_rows)
            + [pl.BlockSpec((block_rows, model), lambda i, order: (order[begin + i], 0))]
            + [whole_spec(gate_w.shape)] * 3
            + [pl.BlockSpec(memory_space=pl.ANY)] * len(extra),
            out_specs=[place_spec(width) for width in carried] + [own_spec] * 2,
            scratch_shapes=[pltpu.VMEM((block_rows, filled), BF16)],
        ),
        input_output_aliases={in_count + i: i for i in range(len(extra))},
        compiler_params=params(),
        cost_estimate=SMALL_COST,
    )(order, *x_pieces, cot, gate_w, up_w, down_wt, *extra)


def branch_kernel(count, model, split, *refs):
    pieces, weight_ref = refs[:count], refs[count]
    d_out, attn_ref, ssm_ref, buf = refs[count + 1 :]
    take_piece(pieces, buf)
    d = buf[:, :model]
    d_out[...] = d
    ssm_ref[...] = dot_nn(d, weight_ref[:, split:])
    attn_ref[...] = dot_nn(d, weight_ref[:, :split])


def branch(pieces, weight, split, block_rows):
    model, depth = weight.shape
    rows = sum(piece.shape[0] for piece in pieces)
    spec = lambda width: pl.BlockSpec((block_rows, width), lambda i: (i, 0))
    return pl.pallas_call(
        functools.partial(branch_kernel, len(pieces), model, split),
        out_shape=(
            jax.ShapeDtypeStruct((rows, model), BF16),
            jax.ShapeDtypeStruct((rows, split), F32),
            jax.ShapeDtypeStruct((rows, depth - split), F32),
        ),
        grid=(rows // block_rows,),
        in_specs=piece_specs(pieces, block_rows) + [whole_spec(weight.shape)],
        out_specs=(spec(model), spec(split), spec(depth - split)),
        scratch_shapes=[pltpu.VMEM((block_rows, pieces[0].shape[1]), BF16)],
        compiler_params=params(),
        cost_estimate=SMALL_COST,
    )(*pieces, weight)


ORDER = (0, 2, 4, 6, 1, 3, 5, 7)
CUBE = len(ORDER)


def by_rows(value):
    return with_layout_constraint(value, Layout(major_to_minor=tuple(range(value.ndim))))


def swap(value, mask):
    return lax.ppermute(value, "ctx", [(d, d ^ mask) for d in range(CUBE)])


def fill_lanes(value):
    more = -value.shape[1] % 128
    return jnp.pad(value.astype(BF16), ((0, 0), (0, more)))


def block_order(place, devices):
    if devices == CUBE:
        return place ^ jnp.array(ORDER, jnp.int32)
    return jnp.arange(devices, dtype=jnp.int32)


def block_index(owner, place, devices):
    if devices == CUBE:
        k = owner ^ place
        return k // 2 + (k % 2) * (CUBE // 2)
    return owner


def gather_pieces(own, devices):
    if devices != CUBE:
        return [lax.all_gather(own, "ctx", axis=0, tiled=True)]
    by_x, by_y, mate = swap(own, 2), swap(own, 4), swap(own, 1)
    part = jax.ShapeDtypeStruct((own.shape[0] // 2, own.shape[1]), own.dtype)
    to_y, to_x = whole_call(cross_kernel, [part, part], by_x, by_y)
    far = jnp.concatenate([swap(to_y, 4), swap(to_x, 2)], axis=0)
    return [own, by_x, by_y, far, mate, swap(by_x, 1), swap(by_y, 1), swap(far, 1)]


def row_halves(rows, devices):
    return [(rows // 2, rows // 2), (0, rows // 2)] if devices == CUBE else [(0, rows)]


def scatter_begin(part, devices):
    return swap(part, 1) if devices == CUBE else part


def scatter_chip(mine, from_mate, devices, deps=()):
    if devices != CUBE:
        return (mine,)
    size, width = mine.shape[0] * 2 // CUBE, mine.shape[1]
    shape = lambda rows, kind: jax.ShapeDtypeStruct((rows, width), kind)
    whole, half = shape(size, F32), shape(size // 2, F32)
    send = shape(size, BF16)
    return whole_call(
        chip_sum_kernel, [whole, send, send, half, half], mine, from_mate, deps=deps
    )


def scatter_links(parts, devices, deps=()):
    if devices != CUBE:
        return parts
    own, to_x, to_y, keep_x, keep_y = parts
    low = jax.ShapeDtypeStruct(keep_x.shape, BF16)
    return whole_call(
        near_sum_kernel, [jax.ShapeDtypeStruct(own.shape, F32), low, low],
        own, keep_x, keep_y, swap(to_x, 2), swap(to_y, 4), deps=deps,
    )


def scatter_near(mine, from_mate, devices):
    return scatter_links(scatter_chip(mine, from_mate, devices), devices)


def scatter_far(parts, width, devices, deps=()):
    if devices != CUBE:
        total = lax.psum_scatter(parts[0], "ctx", scatter_dimension=0, tiled=True)
        return total[:, :width].astype(F32)
    part, to_x, to_y = parts
    shape = jax.ShapeDtypeStruct(part.shape, F32)
    total = whole_call(
        far_sum_kernel, [shape], part, swap(to_y, 4), swap(to_x, 2), deps=deps
    )[0]
    return total[:, :width]


def scatter_end(mine, from_mate, width, devices):
    return scatter_far(scatter_near(mine, from_mate, devices), width, devices)


def exchange(blocks):
    return lax.all_to_all(blocks, "ctx", split_axis=0, concat_axis=0, tiled=True)


def small_scatter(value, place, devices):
    if devices != CUBE:
        return lax.psum_scatter(value, "ctx", scatter_dimension=0, tiled=False)
    return sum(swap(value[i], k) if k else value[i] for i, k in enumerate(ORDER))


def small_gather(value, place, devices):
    if devices != CUBE:
        return lax.all_gather(value, "ctx", axis=0)
    return jnp.stack([swap(value, k) if k else value for k in ORDER])


def in_places(got, place, devices):
    if devices != CUBE:
        return got
    got = jnp.stack(got)
    return got[block_index(jnp.arange(CUBE, dtype=jnp.int32), place, devices)]


def place_gather(value, place, devices, ordered=True):
    if devices != CUBE:
        return lax.all_gather(value, "ctx", axis=0)
    got = [swap(value, k) if k else value for k in ORDER]
    return in_places(got, place, devices) if ordered else got


def add_low(a, b):
    return (a.astype(F32) + b.astype(F32)).astype(BF16)


def all_sum_core(value, devices):
    return add_low(value, swap(value, 1)) if devices == CUBE else value


def all_sum_near(value, devices, deps=()):
    if devices != CUBE:
        return (value,)
    half = value.shape[0] // 2
    top, end = value[:half], value[half:]
    shape = jax.ShapeDtypeStruct(top.shape, top.dtype)
    return whole_call(two_sums_kernel, [shape, shape], top, swap(top, 2), end, swap(end, 4), deps=deps)


def all_sum_far(parts, devices):
    if devices != CUBE:
        return lax.psum(parts[0], "ctx")
    top, end = parts
    return jnp.concatenate([add_low(top, swap(top, 4)), add_low(end, swap(end, 2))], axis=0)


def lane_gather(value):
    return lax.all_gather(value, "fsdp", axis=0, tiled=True)


def lane_scatter(value):
    return lax.psum_scatter(value, "fsdp", scatter_dimension=0, tiled=True)


def lane_shift(value, lanes, step):
    return lax.ppermute(value, "fsdp", [(z, (z + step) % lanes) for z in range(lanes)])


def lane_small_gather(value, lanes):
    lane = lax.axis_index("fsdp")
    got = jnp.stack([value] + [lane_shift(value, lanes, k) for k in range(1, lanes)])
    return got[(lane - jnp.arange(lanes, dtype=jnp.int32)) % lanes]


def lane_small_exchange(blocks, lanes):
    lane = lax.axis_index("fsdp")
    pick = lambda k: lax.dynamic_index_in_dim(blocks, (lane + k) % lanes, 0, False)
    return tuple(lane_shift(pick(k), lanes, k) if k else pick(0) for k in range(lanes))


def lane_small_scatter(blocks, lanes):
    return sum(part.astype(F32) for part in lane_small_exchange(blocks, lanes))


def after(value, *earlier):
    return lax.optimization_barrier((value,) + earlier)[0]


def back(moves):
    return [(b, to, a, lo, size) for a, lo, b, to, size in moves]


def pair_routes(devices):
    half = devices // 2
    first = [(d, 2 * d) for d in range(half)] + [(d, 2 * (d - half) + 1) for d in range(half, devices)]
    second = [(d, 2 * d + 1) for d in range(half)] + [(d, 2 * (d - half)) for d in range(half, devices)]
    return first, second


def split_pairs(value, place, devices):
    width = value.shape[1] // 2
    first, second = pair_routes(devices)
    low, high = value[:, :width], value[:, width:]
    early = place < devices // 2
    got_a = lax.ppermute(jnp.where(early, low, high), "ctx", first)
    got_b = lax.ppermute(jnp.where(early, high, low), "ctx", second)
    even = place % 2 == 0
    return jnp.where(even, got_a, got_b), jnp.where(even, got_b, got_a)


def join_pairs(left, right, place, devices):
    first, second = pair_routes(devices)
    even = place % 2 == 0
    got_a = lax.ppermute(jnp.where(even, left, right), "ctx", [(b, a) for a, b in first])
    got_b = lax.ppermute(jnp.where(even, right, left), "ctx", [(b, a) for a, b in second])
    early = place < devices // 2
    return jnp.concatenate([jnp.where(early, got_a, got_b), jnp.where(early, got_b, got_a)], axis=1)


def pad_to(value, size, axis):
    widths = [(0, 0)] * value.ndim
    widths[axis] = (0, size - value.shape[axis])
    return jnp.pad(value, widths)


def rms_factor(value):
    return lax.rsqrt(jnp.mean(value * value, axis=-1, keepdims=True) + EPS)


def norm_back(value, factor, gain, grad):
    weighted = grad * gain
    d_value = factor * weighted - value * factor * factor * factor * jnp.mean(
        value * weighted, axis=-1, keepdims=True
    )
    return d_value, jnp.sum(grad * value * factor, axis=0)


def shards(
    tokens, cotangent, unit_order, block_seq, meta_tokens, input_gain, query_key_value_weight, w_xz,
    conv_kernel, state_proj, step_proj, step_bias, decay_log, skip_gain, attn_gain, ssm_gain,
    out_proj, ffn_gain, w_gate, w_up, w_down,
):
    devices = lax.axis_size("ctx")
    lanes = lax.axis_size("fsdp")
    place = lax.axis_index("ctx")
    own_rows = tokens.shape[1]
    model = tokens.shape[2]
    unit_rows = own_rows // 2
    slot_unit = unit_order[0]
    units = slot_unit.shape[0]
    rows = units * unit_rows
    width = conv_kernel.shape[1]
    hidden_width = w_gate.shape[1]
    heads = -(-QUERY_HEADS // devices)
    head_width = heads * HEAD_SIZE
    group = QUERY_HEADS // KEY_VALUE_HEADS
    query_width = QUERY_HEADS * HEAD_SIZE
    kv_width = KEY_VALUE_HEADS * HEAD_SIZE
    model_part = input_gain.shape[0]

    slot_ids = jnp.arange(units, dtype=jnp.int32)
    fixed = jnp.sum(
        jnp.where(slot_unit[None, :] == slot_ids[:, None], slot_ids[None, :], 0), axis=1
    ).astype(jnp.int32)
    slot = (2 * block_index(fixed // 2, place, devices) + fixed % 2).astype(jnp.int32)
    unit_seq = jnp.repeat(block_seq[0], 2)
    starts = jnp.concatenate([jnp.ones((1,), jnp.bool_), unit_seq[1:] != unit_seq[:-1]])
    starts_int = starts.astype(jnp.int32)
    low_block = (jnp.sum(unit_seq[None, :] < unit_seq[:, None], axis=1) // 2).astype(jnp.int32)
    my_units = lax.dynamic_slice_in_dim(slot_unit, 2 * place, 2)
    my_start = jnp.any((my_units[:, None] == slot_ids[None, :]) & starts[None, :], axis=1)

    x_part, z_part = split_pairs(w_xz, place, devices)

    small = after(
        jnp.concatenate(
            [conv_kernel, state_proj, step_proj, decay_log, meta_tokens.reshape(-1, width)], axis=0
        ),
        x_part,
    )
    small_all = lane_small_gather(small, lanes)
    marks = [conv_kernel.shape[0], state_proj.shape[0], step_proj.shape[0], decay_log.shape[0]]
    ends = [sum(marks[: i + 1]) for i in range(4)]
    conv_w = small_all[:, : ends[0]].reshape(-1, width).astype(F32)
    sel_w = small_all[:, ends[0] : ends[1]].reshape(-1, width)
    step_w = small_all[:, ends[1] : ends[2]].reshape(-1, width)
    decay = small_all[:, ends[2] : ends[3]].reshape(-1, width).astype(F32)
    rate = -jnp.exp(decay)
    rate2 = rate * LOG2E
    meta_part = small_all[:, ends[3] :].reshape(-1, model_part)
    meta_rows = meta_part.shape[0]
    wide = jnp.concatenate(
        [meta_part, input_gain[None], ffn_gain[None], attn_gain[None]], axis=0
    )
    wide = place_gather(wide, place, devices)
    wide = jnp.transpose(wide, (1, 0, 2)).reshape(-1, model).astype(F32)
    meta = wide[:meta_rows]
    gain_in = wide[meta_rows]
    gain_ffn = wide[meta_rows + 1]
    gain_attn = lax.dynamic_slice_in_dim(
        pad_to(wide[meta_rows + 2], devices * head_width, 0), place * head_width, head_width
    )[None]
    bias = step_bias.astype(F32)[None]
    skip = skip_gain.astype(F32)[None]
    gain_ssm = ssm_gain.astype(F32)[None]

    xz_w = lane_gather(jnp.concatenate([x_part, z_part], axis=1))
    x_w, z_w = xz_w[:, :width], xz_w[:, width:]
    out_held = hold(jnp.transpose(out_proj), small_all)
    out_cols = lax.all_gather(out_held, "fsdp", axis=0)
    order = block_order(place, devices)
    piece_rows = min(256, own_rows)

    own_tok = tokens[0]
    pieces = gather_pieces(fill_lanes(after(own_tok, x_part)), devices)
    slot_start = jnp.sum(
        jnp.where(slot[None, :] == slot_ids[:, None], starts_int[None, :], 0), axis=1
    ).astype(jnp.int32)
    normed = norm_all(slot_start, meta, gain_in[None], pieces)
    qkv_all = lax.all_gather(hold(query_key_value_weight, normed, out_held), "ctx", axis=0)
    resid = jnp.where(
        my_start[:, None, None], meta[None], own_tok.reshape(2, unit_rows, model).astype(F32)
    ).reshape(own_rows, model)
    in_factor = rms_factor(resid)

    x_in = dot_nn(normed, x_w).astype(BF16)

    conv_out, ssm_in, select = conv_forward(
        slot, fixed, starts_int, x_in, conv_w, sel_w, unit_rows
    )
    select = all_sum_core(select, devices)
    z_gate = dot_nn(normed, z_w).astype(BF16)
    near = all_sum_near(select, devices, (z_gate,))
    select = all_sum_far(near, devices).astype(F32)
    first_kv = (place * heads) // group
    kv_room = (devices * heads // group + 3) * HEAD_SIZE
    cases = []
    for d in range(devices):
        some = max(0, min(head_width, query_width - d * head_width))
        spans = [(d * head_width, 0, 0, some)]
        low_kv = d * heads // group * HEAD_SIZE
        some = max(0, min(PAIR_WIDTH, kv_width - low_kv))
        for i in range(2):
            begin = query_width + i * kv_width + low_kv
            spans.append((begin, 0, head_width + i * PAIR_WIDTH, some))
        cases.append(runs(spans, query_key_value_weight.shape[1]))
    qkv_width = head_width + 2 * PAIR_WIDTH
    qkv_part = pick_columns(qkv_all, place, cases, qkv_width, (near[0],))
    qkv_w = lane_gather(qkv_part)
    pair = jnp.clip(
        (place * heads + jnp.arange(heads, dtype=jnp.int32)) // group - first_kv, 0, 1
    ).astype(jnp.int32)
    cot_own = hold(cotangent[0], qkv_part)
    cot = lax.all_gather(cot_own, "ctx", axis=0, tiled=True)
    down_held = hold(jnp.transpose(w_down), cot_own)
    down_cols = lax.all_gather(down_held, "fsdp", axis=0)
    gate_held = hold(w_gate, down_held)
    gate_w = lane_gather(gate_held)
    up_held = hold(w_up, gate_held)
    up_w = lane_gather(up_held)
    spans = []
    for d in range(devices):
        some = max(0, min(head_width, query_width - d * head_width))
        spans += [(d * head_width, d, 0, some), (query_width + d * width, d, head_width, width)]
    out_moves = runs(spans, out_proj.shape[0])
    out_blocks = move_columns(out_cols, out_moves, devices, head_width + width, (select,))
    out_wt = exchange(out_blocks).reshape(model, -1)
    down_moves = runs(
        [(d * hidden_width, d, 0, hidden_width) for d in range(devices)], w_down.shape[0]
    )
    step_low = select[:, :DT_RANK].astype(BF16)
    bc = jnp.transpose(select[:, DT_RANK:].reshape(units, unit_rows, 2 * STATE), (0, 2, 1))
    y_total, ssm_comb, ssm_square, wide_bc, states, last_states = scan_forward(
        slot, fixed, starts_int, ssm_in, z_gate, step_low, bc, step_w, bias, rate2, skip, gain_ssm,
        unit_rows, (out_blocks, up_held),
    )

    cube = devices == CUBE

    def out_term(comb, lo, hi, *deps):
        return project([comb], [out_wt], [(lo, hi)], piece_rows, cube, None, deps)

    ssm_terms = out_term(ssm_comb, head_width, head_width + width)
    ssm_mate = scatter_begin(ssm_terms[0], devices)
    qkv = dot_nn(normed, qkv_w).astype(BF16)
    ssm_chip = scatter_chip(ssm_terms[-1], ssm_mate, devices, (qkv,))
    down_blocks = move_columns(down_cols, down_moves, devices, hidden_width, (ssm_chip[0],))
    down_wt = exchange(down_blocks).reshape(model, -1)
    queries = qkv[:, :head_width]
    keys = qkv[:, head_width : head_width + PAIR_WIDTH]
    values = qkv[:, head_width + PAIR_WIDTH :]
    attn, attn_comb, attn_stat = attn_forward(
        slot, low_block, pair, queries, keys, jnp.transpose(values), gain_attn, unit_rows,
        (ssm_chip[0], down_blocks),
    )
    ssm_near = scatter_links(ssm_chip, devices, (attn_comb,))
    attn_terms = out_term(attn_comb, 0, head_width, down_wt, ssm_near[0])
    ssm_out = scatter_far(ssm_near, model, devices)
    attn_mate = scatter_begin(attn_terms[0], devices)
    attn_out = scatter_end(attn_terms[-1], attn_mate, model, devices)
    squares = jnp.stack(
        [
            attn_stat[:, 1, :unit_rows].reshape(devices, own_rows),
            ssm_square[:, 0].reshape(devices, own_rows),
        ],
        axis=1,
    )
    squares = small_scatter(squares, place, devices)
    own_factors = lax.rsqrt(squares / jnp.array([[query_width], [devices * width]], F32) + EPS)
    mid = (
        resid
        + 0.5 * own_factors[0][:, None] * attn_out
        + 0.5 * own_factors[1][:, None] * ssm_out
    )
    mid_factor = rms_factor(mid)
    x_pieces = gather_pieces(fill_lanes(mid * mid_factor * gain_ffn), devices)

    carried = None
    back_terms, ffn_terms = [], []
    for first, count in row_halves(rows, devices):
        some = slice(first // own_rows, (first + count) // own_rows)
        x_some = x_pieces[some] if devices == CUBE else x_pieces
        *carried, back_term, ffn_term = ffn(
            order, x_some, cot, gate_w, up_w, down_wt, first, count, piece_rows, carried
        )
        back_terms.append(back_term)
        ffn_terms.append(ffn_term)
    ffn_in, cot_rows, hidden, d_gate, d_up = carried
    back_mate = scatter_begin(back_terms[0], devices)
    ffn_in = after(ffn_in, back_mate)
    gate_part = dot_tn(ffn_in, d_gate).astype(BF16)
    gate_grad = lane_scatter(gate_part)
    d_ffn = after(scatter_end(back_terms[-1], back_mate, model, devices), gate_part)

    d_mid_norm, ffn_gain_part = norm_back(mid, mid_factor, gain_ffn, d_ffn)
    d_mid = cotangent[0].astype(F32) + d_mid_norm
    d_branch_own = d_mid.astype(BF16)
    d_pieces = gather_pieces(fill_lanes(d_branch_own), devices)
    up_part = dot_tn(ffn_in, after(d_up, d_branch_own)).astype(BF16)
    up_grad = lane_scatter(up_part)
    down_part = dot_tn(cot_rows, after(hidden, d_branch_own)).astype(BF16)
    d_pieces[-1] = after(d_pieces[-1], up_part, down_part)
    down_back = exchange(after(down_part, d_pieces[-1]).reshape(devices, model_part, -1))
    ffn_mate = scatter_begin(ffn_terms[0], devices)
    ffn_chip = scatter_chip(ffn_terms[-1], ffn_mate, devices)
    branch_f = d_branch_own.astype(F32)
    dots = jnp.stack(
        [
            jnp.sum(branch_f * attn_out, axis=1) * (0.5 / query_width),
            jnp.sum(branch_f * ssm_out, axis=1) * (0.5 / (devices * width)),
        ]
    )
    shifts = dots * own_factors * own_factors * own_factors
    spread_rows = small_gather(jnp.concatenate([own_factors, shifts], axis=0), place, devices)
    spread_rows = jnp.transpose(spread_rows, (1, 0, 2)).reshape(4, rows)
    factors, shifts = spread_rows[:2], spread_rows[2:]

    d_branch, d_comb_attn, d_comb_ssm = branch(d_pieces, out_wt, head_width, piece_rows)
    stat = jnp.transpose(pad_to(jnp.stack([factors[1], shifts[1]]), 128, 0))
    d_z, x_part_grad, d_low, d_bc, step_grad, vec_grads, decay_sum = scan_backward(
        slot, fixed, starts_int, d_comb_ssm, stat, y_total, z_gate, ssm_in, step_low, wide_bc,
        states, last_states, step_w, bias, rate2, skip, gain_ssm, unit_rows,
        (ffn_chip[0],),
    )
    d_bc = jnp.transpose(
        d_bc[:, :, 0].reshape(units, 2, unit_rows, STATE), (0, 2, 1, 3)
    ).reshape(rows, 2 * STATE)
    ffn_near = scatter_links(ffn_chip, devices, (d_low,))
    down_back = move_columns(
        down_back, back(down_moves), lanes, w_down.shape[0], (ffn_near[0],)
    )
    down_grad = lax.psum_scatter(down_back, "fsdp", scatter_dimension=0, tiled=False)
    d_select = whole_call(
        join_kernel, [jax.ShapeDtypeStruct((rows, DT_RANK + 2 * STATE), BF16)],
        d_low, d_bc.astype(BF16), deps=(down_back,),
    )[0]
    attn_mixed = (attn * (0.5 * factors[0][:, None] * gain_attn)).astype(BF16)
    ssm_mixed = (ssm_comb.astype(F32) * (0.5 * factors[1][:, None])).astype(BF16)
    d_select = all_sum_core(d_select, devices)
    mixed = after(jnp.concatenate([attn_mixed, ssm_mixed], axis=1), d_select)
    out_part = dot_tn(d_branch, mixed).astype(BF16)
    d_near = all_sum_near(d_select, devices)
    d_near = lax.optimization_barrier(tuple(d_near) + (out_part,))[:-1]
    d_far = all_sum_far(d_near, devices)
    z_part_grad = dot_tn(normed, after(d_z, *d_near)).astype(BF16)
    d_far = after(d_far, z_part_grad)
    out_back = exchange(hold(out_part, d_far).reshape(devices, model_part, -1))
    if devices == CUBE:
        ffn_near = (ffn_near[0], hold(ffn_near[1], d_far), hold(ffn_near[2], d_far))
    half = 0.5 * d_comb_attn
    d_attn = factors[0][:, None] * (half * gain_attn) - attn * shifts[0][:, None]
    attn_gain_part = jnp.sum(half * attn * factors[0][:, None], axis=0)
    d_query, d_keys, d_values = attn_backward(
        slot, low_block, pair, queries, attn, d_attn.astype(BF16), attn_stat,
        keys, jnp.transpose(keys), values, unit_rows, (d_far, out_part),
    )
    out_back = move_columns(
        out_back, back(out_moves), lanes, out_proj.shape[0], (d_query,)
    )
    layer_out = mid + scatter_far(ffn_near, model, devices, (out_back,))
    d_qkv = whole_call(
        join_qkv_kernel, [jax.ShapeDtypeStruct((rows, qkv_width), BF16)],
        d_query, d_keys, d_values, deps=(layer_out,),
    )[0]
    layer_out = layer_out.astype(BF16)[None]
    qkv_part_grad = dot_tn(normed, d_qkv).astype(BF16)
    early = project(
        [d_qkv, after(d_z, d_qkv)], [qkv_w, z_w], [(0, qkv_width), (0, width)], piece_rows,
        False, None, (qkv_part_grad, z_part_grad),
    )[0]
    out_grad = lax.psum_scatter(
        out_back, "fsdp", scatter_dimension=0, tiled=False
    )
    z_grad = lane_scatter(z_part_grad)
    in_grad = lane_scatter(qkv_part_grad)
    d_x, conv_grads, select_grad = conv_backward(
        slot, fixed, starts_int, d_far, x_part_grad, conv_out, x_in, ssm_in, conv_w, sel_w, unit_rows,
        (early, layer_out, out_back, down_back),
    )
    in_terms = project([d_x], [x_w], [(0, width)], piece_rows, cube, early)
    in_mate = scatter_begin(in_terms[0], devices)
    x_part_sum = dot_tn(after(normed, in_mate), d_x).astype(BF16)
    in_chip = scatter_chip(in_terms[-1], in_mate, devices)
    in_near = scatter_links(in_chip, devices)
    d_normed = scatter_far(in_near, model, devices)
    sums = (down_grad, out_grad, gate_grad, up_grad, z_grad, in_grad, conv_grads, select_grad)
    sums += (step_grad, vec_grads, decay_sum)
    sums = lax.optimization_barrier(sums + tuple(in_near))[: len(sums)]
    down_grad, out_grad, gate_grad, up_grad, z_grad, in_grad, conv_grads, select_grad = sums[:8]
    step_grad, vec_grads, decay_sum = sums[8:]
    gate_grad, up_grad = gate_grad.astype(F32), up_grad.astype(F32)
    x_grad = lane_scatter(x_part_sum)
    in_grad = hold(in_grad, d_normed)
    spread = jnp.zeros((in_grad.shape[0], devices * head_width), BF16)
    spread = lax.dynamic_update_slice_in_dim(spread, in_grad[:, :head_width], place * head_width, 1)
    kv_zero = jnp.zeros((in_grad.shape[0], kv_room), BF16)
    qkv_full = jnp.concatenate(
        [
            spread[:, :query_width],
            lax.dynamic_update_slice_in_dim(
                kv_zero, in_grad[:, head_width : head_width + 2 * HEAD_SIZE],
                first_kv * HEAD_SIZE, 1,
            )[:, :kv_width],
            lax.dynamic_update_slice_in_dim(
                kv_zero, in_grad[:, head_width + 2 * HEAD_SIZE : qkv_width],
                first_kv * HEAD_SIZE, 1,
            )[:, :kv_width],
        ],
        axis=1,
    )
    part = query_key_value_weight.shape[1]
    qkv_blocks = jnp.transpose(qkv_full.reshape(-1, devices, part), (1, 0, 2))
    qkv_grad = lax.psum_scatter(
        qkv_blocks, "ctx", scatter_dimension=0, tiled=False
    ).astype(F32)

    d_norm_in, in_gain_part = norm_back(resid, in_factor, gain_in, d_normed)
    d_resid = d_mid + d_norm_in
    halves = [
        (my_start[i], d_resid[i * unit_rows : (i + 1) * unit_rows]) for i in range(2)
    ]
    tokens_grad = jnp.concatenate(
        [jnp.where(flag, 0.0, half).astype(BF16) for flag, half in halves], axis=0
    )[None]
    meta_sum = sum(jnp.where(flag, half, 0.0) for flag, half in halves)

    gain_rows = jnp.stack(
        [
            in_gain_part,
            ffn_gain_part,
            lax.dynamic_update_slice_in_dim(
                jnp.zeros((devices * head_width,), F32), attn_gain_part, place * head_width, 0
            )[:query_width],
        ]
    )
    by_lane = jnp.concatenate(
        [
            meta_sum.reshape(lanes, -1, model),
            jnp.broadcast_to(gain_rows[None], (lanes, 3, model)),
        ],
        axis=1,
    )
    count = by_lane.shape[1]
    packed = jnp.transpose(
        by_lane.reshape(lanes, count, devices, model_part), (0, 2, 1, 3)
    ).reshape(lanes * devices, count, model_part)
    totals = jnp.sum(
        lax.all_to_all(
            packed.astype(BF16), ("fsdp", "ctx"), split_axis=0, concat_axis=0, tiled=True
        ).astype(F32),
        axis=0,
    )
    xz_grad = join_pairs(x_grad, z_grad, place, devices).astype(F32)
    packed_low = packed.astype(BF16)
    down_grad, out_grad = (
        jnp.transpose(hold(part, packed_low).astype(F32)) for part in (down_grad, out_grad)
    )
    select_grad = hold(select_grad, packed_low)
    counts = [CONV, select_grad.shape[0], DT_RANK, STATE]
    local = jnp.concatenate(
        [
            part.reshape(lanes, -1, width)
            for part in (conv_grads[:CONV], select_grad, step_grad, rate * decay_sum)
        ]
        + [jnp.broadcast_to(vec_grads[None, :3], (lanes, 3, width))],
        axis=1,
    )
    local = lane_small_scatter(local, lanes)
    ends = [sum(counts[:i]) // lanes for i in range(5)]
    piece = lambda i: local[ends[i] : ends[i + 1]]
    vec = lambda i: local[ends[4] + i]
    return (
        layer_out,
        tokens_grad,
        totals[: count - 3],
        totals[count - 3],
        qkv_grad,
        xz_grad,
        piece(0),
        piece(1),
        piece(2),
        vec(2),
        piece(3),
        vec(1),
        totals[count - 1],
        vec(0),
        out_grad,
        totals[count - 2],
        gate_grad,
        up_grad,
        down_grad,
    )


def solution(mesh):
    rows = P("fsdp", "ctx", None)
    index = P("fsdp", None)
    mat = P("fsdp", "ctx")
    vec = P("ctx")
    return jax.shard_map(
        shards,
        mesh=mesh,
        in_specs=(
            rows, rows, index, index, mat, vec, mat, mat, mat, mat, mat, vec, mat, vec, vec, vec,
            mat, vec, mat, mat, mat,
        ),
        out_specs=(
            rows, rows, mat, vec, mat, mat, mat, mat, mat, vec, mat, vec, vec, vec, mat, vec, mat,
            mat, mat,
        ),
        check_vma=False,
    )
```

```python
import functools
import jax
import jax.numpy as jnp
from jax import lax
from jax.experimental import pallas as pl
from jax.experimental.layout import Layout, with_layout_constraint
from jax.experimental.pallas import tpu as pltpu
from jax.sharding import PartitionSpec as P

QUERY_HEADS = 25
KEY_VALUE_HEADS = 5
HEAD_SIZE = 64
INNER = 3200
STATE = 16
CONV = 4
DT_RANK = 100
EPS = 1e-06
LOG2E = 1.4426950408889634
LN2 = 0.6931471805599453
VMEM_LIMIT = 56 * 1024 * 1024
STEP_GROUP = 8
SMALL_COST = pl.CostEstimate(flops=1, bytes_accessed=1, transcendentals=0)
F32 = jnp.float32
BF16 = jnp.bfloat16


def sigmoid(value):
    return 0.5 * jnp.tanh(0.5 * value) + 0.5


def dot_nn(left, right):
    return lax.dot_general(left, right, (((1,), (0,)), ((), ())), preferred_element_type=F32)


def dot_nt(left, right):
    return lax.dot_general(left, right, (((1,), (1,)), ((), ())), preferred_element_type=F32)


def dot_tn(left, right):
    return lax.dot_general(left, right, (((0,), (0,)), ((), ())), preferred_element_type=F32)


def unit_spec(rows, width, reverse_units=None, which=0):
    if reverse_units is None:
        return pl.BlockSpec((rows, width), lambda u, *maps: (maps[which][u], 0))
    last = reverse_units - 1
    return pl.BlockSpec((rows, width), lambda i, *maps: (maps[which][last - i], 0))


def whole_spec(shape):
    zeros = (0,) * len(shape)
    return pl.BlockSpec(shape, lambda *_: zeros)


def later(kernel, before, deps):
    if not deps:
        return kernel
    count = len(deps)
    return lambda *refs: kernel(*refs[:before], *refs[before + count :])


def wait_specs(deps):
    return [pl.BlockSpec(memory_space=pl.ANY)] * len(deps)


def hold_kernel(in_ref, out_ref):
    out_ref[...] = in_ref[...]


def hold(value, *deps):
    return pl.pallas_call(
        later(hold_kernel, 1, deps),
        out_shape=jax.ShapeDtypeStruct(value.shape, value.dtype),
        in_specs=[pl.BlockSpec(memory_space=pltpu.VMEM)] + wait_specs(deps),
        out_specs=pl.BlockSpec(memory_space=pltpu.VMEM),
        compiler_params=pltpu.CompilerParams(vmem_limit_bytes=VMEM_LIMIT),
        cost_estimate=SMALL_COST,
    )(value, *deps)


def params():
    return pltpu.CompilerParams(
        dimension_semantics=("arbitrary",), vmem_limit_bytes=VMEM_LIMIT
    )


def norm_unit(value, meta, gain, begins):
    value = jnp.where(begins == 1, meta, value.astype(F32))
    factor = lax.rsqrt(jnp.mean(value * value, axis=-1, keepdims=True) + EPS)
    return (value * factor * gain).astype(BF16)


def norm_pieces_kernel(begins, meta_ref, gain_ref, *refs):
    pieces, out_ref = refs[:-1], refs[-1]
    unit_rows = meta_ref.shape[0]
    unit = 0
    for piece in pieces:
        for i in range(piece.shape[0] // unit_rows):
            out_ref[unit * unit_rows : (unit + 1) * unit_rows, :] = norm_unit(
                piece[i * unit_rows : (i + 1) * unit_rows, : meta_ref.shape[1]], meta_ref[...],
                gain_ref[...], begins[unit],
            )
            unit += 1


def norm_rows_kernel(begins, meta_ref, gain_ref, in_ref, out_ref):
    out_ref[...] = norm_unit(
        in_ref[:, : meta_ref.shape[1]], meta_ref[...], gain_ref[...], begins[pl.program_id(0)]
    )


def norm_all(begins, meta, gain, pieces):
    unit_rows, width = meta.shape
    rows = sum(piece.shape[0] for piece in pieces)
    shape = jax.ShapeDtypeStruct((rows, width), BF16)
    if len(pieces) > 1:
        return pl.pallas_call(
            norm_pieces_kernel,
            out_shape=shape,
            in_specs=[pl.BlockSpec(memory_space=pltpu.SMEM)]
            + [pl.BlockSpec(memory_space=pltpu.VMEM)] * (2 + len(pieces)),
            out_specs=pl.BlockSpec(memory_space=pltpu.VMEM),
            compiler_params=pltpu.CompilerParams(vmem_limit_bytes=VMEM_LIMIT),
        )(begins, meta, gain, *pieces)
    by_unit = lambda size: pl.BlockSpec((unit_rows, size), lambda u, *_: (u, 0))
    return pl.pallas_call(
        norm_rows_kernel,
        out_shape=shape,
        grid_spec=pltpu.PrefetchScalarGridSpec(
            num_scalar_prefetch=1,
            grid=(rows // unit_rows,),
            in_specs=[whole_spec((unit_rows, width)), whole_spec((1, width)), by_unit(pieces[0].shape[1])],
            out_specs=by_unit(width),
        ),
        compiler_params=params(),
    )(begins, meta, gain, pieces[0])


def conv_kernel_fwd(slot, fixed, start, xin_ref, w_ref, sel_ref, xc_ref, xs_ref, part_ref, ext):
    u = pl.program_id(0)
    rows = xin_ref.shape[0]
    keep = jnp.where(start[u] == 1, 0.0, 1.0)

    @pl.when(u == 0)
    def _():
        ext[...] = jnp.zeros_like(ext)

    ext[0:8, :] = ext[rows : rows + 8, :] * keep
    ext[8 : 8 + rows, :] = xin_ref[...].astype(F32)
    acc = w_ref[0:1, :] * ext[5 : 5 + rows, :]
    for k in range(1, CONV):
        acc = acc + w_ref[k : k + 1, :] * ext[5 + k : 5 + k + rows, :]
    xc_ref[...] = acc
    xs = (acc * sigmoid(acc)).astype(BF16)
    xs_ref[...] = xs
    part_ref[...] = dot_nt(xs, sel_ref[...]).astype(BF16)


def conv_forward(slot, fixed, start, xin, conv_w, sel_w, unit_rows):
    rows, width = xin.shape
    units = rows // unit_rows
    sel_rows = sel_w.shape[0]
    return pl.pallas_call(
        conv_kernel_fwd,
        out_shape=(
            jax.ShapeDtypeStruct((rows, width), F32),
            jax.ShapeDtypeStruct((rows, width), BF16),
            jax.ShapeDtypeStruct((rows, sel_rows), BF16),
        ),
        grid_spec=pltpu.PrefetchScalarGridSpec(
            num_scalar_prefetch=3,
            grid=(units,),
            in_specs=[
                unit_spec(unit_rows, width),
                whole_spec((CONV, width)),
                whole_spec((sel_rows, width)),
            ],
            out_specs=[
                unit_spec(unit_rows, width),
                unit_spec(unit_rows, width),
                unit_spec(unit_rows, sel_rows, None, 1),
            ],
            scratch_shapes=[pltpu.VMEM((unit_rows + 8, width), F32)],
        ),
        compiler_params=params(),
        cost_estimate=SMALL_COST,
    )(slot, fixed, start, xin, conv_w, sel_w)


def conv_kernel_bwd(
    slot, fixed, start, dsel_ref, part_ref, xc_ref, xin_ref, xs_ref, w_ref, sel_ref,
    dxin_ref, gw_ref, gsel_ref, dext,
):
    i = pl.program_id(0)
    units = pl.num_programs(0)
    u = units - 1 - i
    rows = xin_ref.shape[0]
    after = jnp.where(start[jnp.minimum(u + 1, units - 1)] == 1, 0.0, 1.0)

    @pl.when(i == 0)
    def _():
        dext[...] = jnp.zeros_like(dext)
        gw_ref[...] = jnp.zeros_like(gw_ref)
        gsel_ref[...] = jnp.zeros_like(gsel_ref)

    gsel_ref[...] += dot_tn(dsel_ref[...], xs_ref[...])
    dext[rows : rows + 8, :] = dext[0:8, :] * after
    xc = xc_ref[...]
    sig = sigmoid(xc)
    dxs = dot_nn(dsel_ref[...], sel_ref[...]) + part_ref[...]
    dxc = dxs * (sig * (1.0 + xc * (1.0 - sig)))
    dext[0:rows, :] = dxc
    acc = w_ref[CONV - 1 : CONV, :] * dxc
    for k in range(CONV - 1):
        off = CONV - 1 - k
        acc = acc + w_ref[k : k + 1, :] * dext[off : off + rows, :]
    dxin_ref[...] = acc.astype(BF16)
    xin = xin_ref[...].astype(F32)
    for k in range(CONV):
        off = CONV - 1 - k
        gw_ref[k : k + 1, :] += jnp.sum(dext[off : off + rows, :] * xin, axis=0, keepdims=True)


def conv_backward(slot, fixed, start, dsel, part, xc, xin, xs, conv_w, sel_w, unit_rows, deps=()):
    rows, width = xin.shape
    units = rows // unit_rows
    sel_rows = sel_w.shape[0]
    return pl.pallas_call(
later(        conv_kernel_bwd, 10, deps),
        out_shape=(
            jax.ShapeDtypeStruct((rows, width), BF16),
            jax.ShapeDtypeStruct((8, width), F32),
            jax.ShapeDtypeStruct((sel_rows, width), F32),
        ),
        grid_spec=pltpu.PrefetchScalarGridSpec(
            num_scalar_prefetch=3,
            grid=(units,),
            in_specs=[
                unit_spec(unit_rows, sel_rows, units, 1),
                unit_spec(unit_rows, width, units),
                unit_spec(unit_rows, width, units),
                unit_spec(unit_rows, width, units),
                unit_spec(unit_rows, width, units),
                whole_spec((CONV, width)),
                whole_spec((sel_rows, width)),
            ] + wait_specs(deps),
            out_specs=[
                unit_spec(unit_rows, width, units),
                whole_spec((8, width)),
                whole_spec((sel_rows, width)),
            ],
            scratch_shapes=[pltpu.VMEM((unit_rows + 8, width), F32)],
        ),
        compiler_params=params(),
        cost_estimate=SMALL_COST,
    )(slot, fixed, start, dsel, part, xc, xin, xs, conv_w, sel_w, *deps)


def step_sizes(low_ref, step_ref, bias_ref):
    pre = dot_nn(low_ref[...], step_ref[...]) + bias_ref[...]
    return jnp.maximum(pre, 0.0) + jnp.log(1.0 + jnp.exp(-jnp.abs(pre)))


def lane_tiles(width):
    return [(lo, min(width, lo + 128)) for lo in range(0, width, 128)]


def fold_into(total, value, k):
    line = lax.broadcasted_iota(jnp.int32, (STEP_GROUP, 128), 0)
    return jnp.where(
        line == k, jnp.sum(value[0:8] + value[8:STATE], axis=0, keepdims=True), total
    )


def store_tiles(ref, value):
    for i, (lo, hi) in enumerate(lane_tiles(value.shape[1])):
        ref[i] = widen(value[:, lo:hi])


def load_tiles(ref, width):
    tiles = lane_tiles(width)
    return jnp.concatenate([ref[i, :, : hi - lo] for i, (lo, hi) in enumerate(tiles)], axis=1)


def widen(value):
    size = value.shape[1]
    if size == 128:
        return value
    return jnp.concatenate([value, jnp.zeros((value.shape[0], 128 - size), value.dtype)], axis=1)


def row_over_states(ref, i, t):
    return jnp.broadcast_to(ref[i, pl.ds(t, 1), :], (STATE, 128))


def scan_kernel_fwd(
    slot, fixed, start, xs_ref, z_ref, low_ref, bc_ref, step_ref, bias_ref, rate_ref, skip_ref,
    gain_ref, y_ref, comb_ref, square_ref, wide_ref, before_ref, last_ref, dt_buf, dtx_buf, y_buf,
    state,
):
    u = pl.program_id(0)
    rows = xs_ref.shape[0]
    width = xs_ref.shape[1]
    tiles = lane_tiles(width)
    count = len(tiles)
    keep = jnp.where(start[u] == 1, 0.0, 1.0)

    @pl.when(u == 0)
    def _():
        state[...] = jnp.zeros_like(state)

    xs = xs_ref[...].astype(F32)
    dt = step_sizes(low_ref, step_ref, bias_ref)
    store_tiles(dt_buf, dt)
    store_tiles(dtx_buf, dt * xs)
    rates = [widen(rate_ref[:, lo:hi]) for lo, hi in tiles]
    bc = bc_ref[0]
    for t in range(rows):
        wide_ref[0, t] = jnp.broadcast_to(bc[:, t : t + 1], (2 * STATE, 128))

    def group(g, carry):
        base = pl.multiple_of(g * STEP_GROUP, STEP_GROUP)
        h = list(carry)
        y = [jnp.zeros((STEP_GROUP, 128), F32) for _ in tiles]
        for k in range(STEP_GROUP):
            b = wide_ref[0, base + k, 0:STATE]
            c = wide_ref[0, base + k, STATE : 2 * STATE]
            for i in range(count):
                before_ref[0, base + k, i] = h[i]
                decay = jnp.exp2(row_over_states(dt_buf, i, base + k) * rates[i])
                h[i] = decay * h[i] + row_over_states(dtx_buf, i, base + k) * b
                y[i] = fold_into(y[i], c * h[i], k)
        for i in range(count):
            y_buf[i, pl.ds(base, STEP_GROUP), :] = y[i]
        return tuple(h)

    last = lax.fori_loop(
        0, rows // STEP_GROUP, group, tuple(state[i] * keep for i in range(count)), unroll=2
    )
    for i in range(count):
        state[i] = last[i]
        last_ref[0, i] = last[i]
    y = load_tiles(y_buf, width) + skip_ref[...] * xs
    y_ref[...] = y
    z = z_ref[...].astype(F32)
    ys = y * (z * sigmoid(z))
    comb_ref[...] = (ys * gain_ref[...]).astype(BF16)
    square_ref[...] = jnp.broadcast_to(jnp.sum(ys * ys, axis=1, keepdims=True), square_ref.shape)


def scan_forward(slot, fixed, start, xs, z, low, bc, step_w, bias, rate2, skip, gain, unit_rows, deps=()):
    rows, width = xs.shape
    units = rows // unit_rows
    rank = low.shape[1]
    count = -(-width // 128)
    return pl.pallas_call(
later(        scan_kernel_fwd, 12, deps),
        out_shape=(
            jax.ShapeDtypeStruct((rows, width), F32),
            jax.ShapeDtypeStruct((rows, width), BF16),
            jax.ShapeDtypeStruct((rows, 128), F32),
            jax.ShapeDtypeStruct((units, unit_rows, 2 * STATE, 128), F32),
            jax.ShapeDtypeStruct((units, unit_rows, count, STATE, 128), F32),
            jax.ShapeDtypeStruct((units, count, STATE, 128), F32),
        ),
        grid_spec=pltpu.PrefetchScalarGridSpec(
            num_scalar_prefetch=3,
            grid=(units,),
            in_specs=[
                unit_spec(unit_rows, width),
                unit_spec(unit_rows, width),
                unit_spec(unit_rows, rank, None, 1),
                pl.BlockSpec(
                    (1, 2 * STATE, unit_rows), lambda u, slot, fixed, *_: (fixed[u], 0, 0)
                ),
                whole_spec((rank, width)),
                whole_spec((1, width)),
                whole_spec((STATE, width)),
                whole_spec((1, width)),
                whole_spec((1, width)),
            ] + wait_specs(deps),
            out_specs=[
                unit_spec(unit_rows, width),
                unit_spec(unit_rows, width),
                unit_spec(unit_rows, 128),
                pl.BlockSpec((1, unit_rows, 2 * STATE, 128), lambda u, *_: (u, 0, 0, 0)),
                pl.BlockSpec((1, unit_rows, count, STATE, 128), lambda u, *_: (u, 0, 0, 0, 0)),
                pl.BlockSpec((1, count, STATE, 128), lambda u, *_: (u, 0, 0, 0)),
            ],
            scratch_shapes=[
                pltpu.VMEM((count, unit_rows, 128), F32),
                pltpu.VMEM((count, unit_rows, 128), F32),
                pltpu.VMEM((count, unit_rows, 128), F32),
                pltpu.VMEM((count, STATE, 128), F32),
            ],
        ),
        compiler_params=params(),
        cost_estimate=SMALL_COST,
    )(slot, fixed, start, xs, z, low, bc, step_w, bias, rate2, skip, gain, *deps)


def scan_kernel_bwd(
    slot, fixed, start, dc_ref, stat_ref, y_ref, z_ref, xs_ref, low_ref, wide_ref, before_ref,
    last_ref, step_ref, bias_ref, rate_ref, skip_ref, gain_ref,
    dz_ref, part_ref, dlow_ref, dbc_ref, gstep_ref, gvec_ref, gdecay_ref,
    dt_buf, dtx_buf, dy_buf, gx_buf, ddt_buf, pb_buf, pc_buf, adj,
):
    i = pl.program_id(0)
    units = pl.num_programs(0)
    u = units - 1 - i
    rows = xs_ref.shape[0]
    width = xs_ref.shape[1]
    after = jnp.where(start[jnp.minimum(u + 1, units - 1)] == 1, 0.0, 1.0)

    @pl.when(i == 0)
    def _():
        adj[...] = jnp.zeros_like(adj)
        gstep_ref[...] = jnp.zeros_like(gstep_ref)
        gvec_ref[...] = jnp.zeros_like(gvec_ref)
        gdecay_ref[...] = jnp.zeros_like(gdecay_ref)

    xs = xs_ref[...].astype(F32)
    dt = step_sizes(low_ref, step_ref, bias_ref)
    store_tiles(dt_buf, dt)
    store_tiles(dtx_buf, dt * xs)
    tiles = lane_tiles(width)
    count = len(tiles)
    rates = [widen(rate_ref[:, lo:hi]) for lo, hi in tiles]

    factor = stat_ref[:, 0:1]
    shift = stat_ref[:, 1:2]
    z = z_ref[...].astype(F32)
    sig = sigmoid(z)
    gate = z * sig
    y = y_ref[...]
    ys = y * gate
    half = 0.5 * dc_ref[...]
    dys = factor * (half * gain_ref[...]) - ys * shift
    dy = dys * gate
    dz_ref[...] = (dys * y * (sig * (1.0 + z * (1.0 - sig)))).astype(BF16)
    store_tiles(dy_buf, dy)
    gvec_ref[0:1, :] += jnp.sum(half * ys * factor, axis=0, keepdims=True)
    gvec_ref[1:2, :] += jnp.sum(dy * xs, axis=0, keepdims=True)

    def group(index, carry):
        lams, accs, states = list(carry[0]), list(carry[1]), list(carry[2])
        g = rows // STEP_GROUP - 1 - index
        base = pl.multiple_of(g * STEP_GROUP, STEP_GROUP)
        gx = [jnp.zeros((STEP_GROUP, 128), F32) for _ in tiles]
        ddt = [jnp.zeros((STEP_GROUP, 128), F32) for _ in tiles]
        for k in range(STEP_GROUP - 1, -1, -1):
            t = base + k
            b = wide_ref[0, t, 0:STATE]
            c = wide_ref[0, t, STATE : 2 * STATE]
            pb = pc = None
            for i in range(count):
                dt_row = row_over_states(dt_buf, i, t)
                dy_row = row_over_states(dy_buf, i, t)
                lam = lams[i] + c * dy_row
                more_c = dy_row * states[i]
                more_b = row_over_states(dtx_buf, i, t) * lam
                pc = more_c if pc is None else pc + more_c
                pb = more_b if pb is None else pb + more_b
                gx[i] = fold_into(gx[i], b * lam, k)
                lams[i] = jnp.exp2(dt_row * rates[i]) * lam
                states[i] = before_ref[0, t, i]
                w = lams[i] * states[i]
                ddt[i] = fold_into(ddt[i], rates[i] * w, k)
                accs[i] = accs[i] + dt_row * w
            pb_buf[t] = pb
            pc_buf[t] = pc
        for i in range(count):
            gx_buf[i, pl.ds(base, STEP_GROUP), :] = gx[i]
            ddt_buf[i, pl.ds(base, STEP_GROUP), :] = ddt[i]
        return tuple(lams), tuple(accs), tuple(states)

    lams, accs, _ = lax.fori_loop(
        0,
        rows // STEP_GROUP,
        group,
        (
            tuple(adj[i] * after for i in range(count)),
            tuple(jnp.zeros((STATE, 128), F32) for _ in tiles),
            tuple(last_ref[0, i] for i in range(count)),
        ),
    )
    for i, (lo, hi) in enumerate(tiles):
        adj[i] = lams[i]
        gdecay_ref[:, lo:hi] += accs[i][:, : hi - lo]
    gx = load_tiles(gx_buf, width)
    part_ref[...] = gx * dt + skip_ref[...] * dy
    ddt = gx * xs + LN2 * load_tiles(ddt_buf, width)
    dpre = (ddt * (1.0 - jnp.exp(-dt))).astype(BF16)
    gstep_ref[...] += dot_tn(low_ref[...], dpre)
    gvec_ref[2:3, :] += jnp.sum(dpre.astype(F32), axis=0, keepdims=True)
    dlow_ref[...] = dot_nt(dpre, step_ref[...]).astype(BF16)
    ones = jnp.ones((8, 128), BF16)
    dbc_ref[0, 0] = dot_nt(ones, pb_buf[...].reshape(rows * STATE, 128).astype(BF16))
    dbc_ref[0, 1] = dot_nt(ones, pc_buf[...].reshape(rows * STATE, 128).astype(BF16))


def scan_backward(
    slot, fixed, start, dc, stat, y, z, xs, low, wide, before, final, step_w, bias, rate2, skip, gain, unit_rows, deps=()
):
    rows, width = xs.shape
    units = rows // unit_rows
    rank = low.shape[1]
    count = -(-width // 128)
    last = units - 1
    return pl.pallas_call(
        later(scan_kernel_bwd, 3 + 14, deps),
        out_shape=(
            jax.ShapeDtypeStruct((rows, width), BF16),
            jax.ShapeDtypeStruct((rows, width), F32),
            jax.ShapeDtypeStruct((rows, rank), BF16),
            jax.ShapeDtypeStruct((units, 2, 8, unit_rows * STATE), F32),
            jax.ShapeDtypeStruct((rank, width), F32),
            jax.ShapeDtypeStruct((8, width), F32),
            jax.ShapeDtypeStruct((STATE, width), F32),
        ),
        grid_spec=pltpu.PrefetchScalarGridSpec(
            num_scalar_prefetch=3,
            grid=(units,),
            in_specs=[
                unit_spec(unit_rows, width, units),
                unit_spec(unit_rows, 128, units),
                unit_spec(unit_rows, width, units),
                unit_spec(unit_rows, width, units),
                unit_spec(unit_rows, width, units),
                unit_spec(unit_rows, rank, units, 1),
                pl.BlockSpec((1, unit_rows, 2 * STATE, 128), lambda i, *_: (last - i, 0, 0, 0)),
                pl.BlockSpec(
                    (1, unit_rows, count, STATE, 128), lambda i, *_: (last - i, 0, 0, 0, 0)
                ),
                pl.BlockSpec((1, count, STATE, 128), lambda i, *_: (last - i, 0, 0, 0)),
                whole_spec((rank, width)),
                whole_spec((1, width)),
                whole_spec((STATE, width)),
                whole_spec((1, width)),
                whole_spec((1, width)),
            ] + wait_specs(deps),
            out_specs=[
                unit_spec(unit_rows, width, units),
                unit_spec(unit_rows, width, units),
                unit_spec(unit_rows, rank, units, 1),
                pl.BlockSpec(
                    (1, 2, 8, unit_rows * STATE),
                    lambda i, slot, fixed, *_: (fixed[last - i], 0, 0, 0),
                ),
                whole_spec((rank, width)),
                whole_spec((8, width)),
                whole_spec((STATE, width)),
            ],
            scratch_shapes=[
                pltpu.VMEM((count, unit_rows, 128), F32),
                pltpu.VMEM((count, unit_rows, 128), F32),
                pltpu.VMEM((count, unit_rows, 128), F32),
                pltpu.VMEM((count, unit_rows, 128), F32),
                pltpu.VMEM((count, unit_rows, 128), F32),
                pltpu.VMEM((unit_rows, STATE, 128), F32),
                pltpu.VMEM((unit_rows, STATE, 128), F32),
                pltpu.VMEM((count, STATE, 128), F32),
            ],
        ),
        compiler_params=params(),
        cost_estimate=SMALL_COST,
    )(slot, fixed, start, dc, stat, y, z, xs, low, wide, before, final, step_w, bias, rate2, skip, gain, *deps)


PAIR_WIDTH = 2 * HEAD_SIZE


def stack_heads(value, pair):
    parts = []
    for h in range(value.shape[1] // HEAD_SIZE):
        part = value[:, h * HEAD_SIZE : (h + 1) * HEAD_SIZE]
        none = jnp.zeros_like(part)
        left = jnp.where(pair[h] == 0, part, none)
        right = jnp.where(pair[h] == 0, none, part)
        parts.append(jnp.concatenate([left, right], axis=1))
    return parts[0] if len(parts) == 1 else jnp.concatenate(parts, axis=0)


def unstack_heads(value, pair, rows):
    parts = []
    for h in range(value.shape[1] // rows):
        part = value[:, h * rows : (h + 1) * rows]
        parts.append(jnp.where(pair[h] == 0, part[:HEAD_SIZE], part[HEAD_SIZE:]))
    return jnp.transpose(parts[0] if len(parts) == 1 else jnp.concatenate(parts, axis=0))


def attn_kernel_fwd(
    slot, low_block, pair, q_ref, k_ref, vt_ref, gain_ref, o_ref, comb_ref, stat_ref
):
    u = pl.program_id(0)
    rows = q_ref.shape[0]
    heads = q_ref.shape[1] // HEAD_SIZE
    stacked = stack_heads(q_ref[...] * BF16(HEAD_SIZE**-0.5), pair)
    ones = jnp.ones((16, 2 * rows), BF16)

    def body(j, carry):
        top, acc = carry
        first = pl.multiple_of(slot[2 * j] * rows, rows)
        second = pl.multiple_of(slot[2 * j + 1] * rows, rows)
        kb = jnp.concatenate([k_ref[pl.ds(first, rows), :], k_ref[pl.ds(second, rows), :]], axis=0)
        vt = jnp.concatenate(
            [vt_ref[:, pl.ds(first, rows)], vt_ref[:, pl.ds(second, rows)]], axis=1
        )
        s = dot_nt(kb, stacked)
        new_top = jnp.maximum(top, jnp.max(s, axis=0, keepdims=True))
        p = jnp.exp(s - new_top).astype(BF16)
        acc = acc * jnp.exp(top - new_top) + dot_nn(jnp.concatenate([vt, ones], axis=0), p)
        return new_top, acc

    start = (
        jnp.full((1, heads * rows), -1e30, F32),
        jnp.zeros((PAIR_WIDTH + 16, heads * rows), F32),
    )
    top, acc = lax.fori_loop(low_block[u], u // 2 + 1, body, start)
    total = acc[PAIR_WIDTH : PAIR_WIDTH + 1]
    o = unstack_heads(acc[:PAIR_WIDTH] / total, pair, rows)
    o_ref[...] = o
    comb_ref[...] = (o * gain_ref[...]).astype(BF16)
    stat_ref[0, 0:1, :] = top + jnp.log(total)
    ones_row = jnp.ones((8, heads * HEAD_SIZE), F32)
    stat_ref[0, 1:2, 0:rows] = lax.dot_general(
        ones_row, o * o, (((1,), (1,)), ((), ())), precision=lax.Precision.HIGHEST,
        preferred_element_type=F32,
    )[0:1]


def attn_forward(slot, low_block, pair, q, k, vt, gain, unit_rows, deps=()):
    rows, width = q.shape
    units = rows // unit_rows
    lanes = width // HEAD_SIZE * unit_rows
    return pl.pallas_call(
later(        attn_kernel_fwd, 7, deps),
        out_shape=(
            jax.ShapeDtypeStruct((rows, width), F32),
            jax.ShapeDtypeStruct((rows, width), BF16),
            jax.ShapeDtypeStruct((units, 8, lanes), F32),
        ),
        grid_spec=pltpu.PrefetchScalarGridSpec(
            num_scalar_prefetch=3,
            grid=(units,),
            in_specs=[
                unit_spec(unit_rows, width),
                whole_spec(k.shape),
                whole_spec(vt.shape),
                whole_spec((1, width)),
            ] + wait_specs(deps),
            out_specs=[
                unit_spec(unit_rows, width),
                unit_spec(unit_rows, width),
                pl.BlockSpec((1, 8, lanes), lambda u, slot, *_: (slot[u], 0, 0)),
            ],
        ),
        compiler_params=params(),
        cost_estimate=SMALL_COST,
    )(slot, low_block, pair, q, k, vt, gain, *deps)


def attn_kernel_bwd(
    slot, low_block, pair, q_ref, o_ref, do_ref, stat_ref, k_ref, kt_ref, v_ref,
    dq_ref, dk_ref, dv_ref,
):
    u = pl.program_id(0)
    rows = q_ref.shape[0]
    heads = q_ref.shape[1] // HEAD_SIZE

    @pl.when(u == 0)
    def _():
        dk_ref[...] = jnp.zeros_like(dk_ref)
        dv_ref[...] = jnp.zeros_like(dv_ref)

    queries = stack_heads(q_ref[...] * BF16(HEAD_SIZE**-0.5), pair)
    do = do_ref[...]
    grads = stack_heads(do, pair)
    prod = do.astype(F32) * o_ref[...]
    prod = [prod[:, h * HEAD_SIZE : (h + 1) * HEAD_SIZE] for h in range(heads)]
    prod = prod[0] if heads == 1 else jnp.concatenate(prod, axis=0)
    delta = lax.dot_general(
        jnp.ones((8, HEAD_SIZE), F32), prod, (((1,), (1,)), ((), ())),
        precision=lax.Precision.HIGHEST, preferred_element_type=F32,
    )[0:1]
    log_total = stat_ref[0, 0:1, :]

    def body(j, dq):
        first = pl.multiple_of(slot[2 * j] * rows, rows)
        second = pl.multiple_of(slot[2 * j + 1] * rows, rows)
        kb = jnp.concatenate([k_ref[pl.ds(first, rows), :], k_ref[pl.ds(second, rows), :]], axis=0)
        vb = jnp.concatenate([v_ref[pl.ds(first, rows), :], v_ref[pl.ds(second, rows), :]], axis=0)
        kt = jnp.concatenate(
            [kt_ref[:, pl.ds(first, rows)], kt_ref[:, pl.ds(second, rows)]], axis=1
        )
        p = jnp.exp(dot_nt(kb, queries) - log_total)
        ds = (p * (dot_nt(vb, grads) - delta)).astype(BF16)
        dv = dot_nn(p.astype(BF16), grads)
        dk = dot_nn(ds, queries)
        dv_ref[pl.ds(first, rows), :] += dv[0:rows]
        dv_ref[pl.ds(second, rows), :] += dv[rows : 2 * rows]
        dk_ref[pl.ds(first, rows), :] += dk[0:rows]
        dk_ref[pl.ds(second, rows), :] += dk[rows : 2 * rows]
        return dq + dot_nn(kt, ds)

    dq = lax.fori_loop(
        low_block[u], u // 2 + 1, body, jnp.zeros((PAIR_WIDTH, heads * rows), F32)
    )
    dq_ref[...] = (unstack_heads(dq, pair, rows) * HEAD_SIZE**-0.5).astype(BF16)


def attn_backward(slot, low_block, pair, q, o, do, stat, k, kt, v, unit_rows, deps=()):
    rows, width = q.shape
    units = rows // unit_rows
    lanes = width // HEAD_SIZE * unit_rows
    return pl.pallas_call(
later(        attn_kernel_bwd, 10, deps),
        out_shape=(
            jax.ShapeDtypeStruct((rows, width), BF16),
            jax.ShapeDtypeStruct(k.shape, F32),
            jax.ShapeDtypeStruct(v.shape, F32),
        ),
        grid_spec=pltpu.PrefetchScalarGridSpec(
            num_scalar_prefetch=3,
            grid=(units,),
            in_specs=[
                unit_spec(unit_rows, width),
                unit_spec(unit_rows, width),
                unit_spec(unit_rows, width),
                pl.BlockSpec((1, 8, lanes), lambda u, slot, *_: (slot[u], 0, 0)),
                whole_spec(k.shape),
                whole_spec(kt.shape),
                whole_spec(v.shape),
            ] + wait_specs(deps),
            out_specs=[unit_spec(unit_rows, width), whole_spec(k.shape), whole_spec(v.shape)],
        ),
        compiler_params=params(),
        cost_estimate=SMALL_COST,
    )(slot, low_block, pair, q, o, do, stat, k, kt, v, *deps)


def fill_width(width):
    return -(-width // 128) * 128


def piece_specs(pieces, block_rows):
    if len(pieces) == 1:
        return [pl.BlockSpec((block_rows, pieces[0].shape[1]), lambda i, *_: (i, 0))]
    return [whole_spec(piece.shape) for piece in pieces]


def take_piece(refs, buf):
    if len(refs) == 1:
        buf[...] = refs[0][...]
        return
    step = pl.program_id(0)
    for k, ref in enumerate(refs):

        @pl.when(step == k)
        def _(ref=ref):
            buf[...] = ref[...]


def store_filled(ref, value):
    width = value.shape[1]
    ref[:, :width] = value.astype(ref.dtype)
    if ref.shape[1] > width:
        ref[:, width:] = jnp.zeros((ref.shape[0], ref.shape[1] - width), ref.dtype)


def whole_call(kernel, out_shape, *values, deps=()):
    return pl.pallas_call(
        later(kernel, len(values), deps),
        out_shape=out_shape,
        in_specs=[pl.BlockSpec(memory_space=pltpu.VMEM)] * len(values) + wait_specs(deps),
        out_specs=[pl.BlockSpec(memory_space=pltpu.VMEM)] * len(out_shape),
        compiler_params=pltpu.CompilerParams(vmem_limit_bytes=VMEM_LIMIT),
        cost_estimate=SMALL_COST,
    )(*values, *deps)


def chip_sum_kernel(mine, mate, own, to_x, to_y, keep_x, keep_y):
    size = own.shape[0]
    half = size // 2
    block = lambda i, a, b: (
        mine[i * size + a : i * size + b, :].astype(F32)
        + mate[i * size + a : i * size + b, :].astype(F32)
    )
    own[...] = block(0, 0, size)
    to_x[:half, :] = block(1, 0, half).astype(BF16)
    to_x[half:, :] = block(3, 0, half).astype(BF16)
    to_y[:half, :] = block(2, half, size).astype(BF16)
    to_y[half:, :] = block(3, half, size).astype(BF16)
    keep_x[...] = block(1, half, size)
    keep_y[...] = block(2, 0, half)


def near_sum_kernel(own, keep_x, keep_y, by_x, by_y, part, to_x, to_y):
    half = keep_x.shape[0]
    part[:half, :] = own[:half, :] + by_x[:half, :].astype(F32)
    part[half:, :] = own[half:, :] + by_y[:half, :].astype(F32)
    to_x[...] = (keep_x[...] + by_y[half:, :].astype(F32)).astype(BF16)
    to_y[...] = (keep_y[...] + by_x[half:, :].astype(F32)).astype(BF16)


def far_sum_kernel(part, by_y, by_x, out):
    half = by_y.shape[0]
    out[:half, :] = part[:half, :] + by_y[...].astype(F32)
    out[half:, :] = part[half:, :] + by_x[...].astype(F32)


def join_qkv_kernel(queries, keys, values, out):
    at = 0
    for ref in (queries, keys, values):
        out[:, at : at + ref.shape[1]] = ref[...].astype(BF16)
        at += ref.shape[1]


def cross_kernel(by_x, by_y, to_y, to_x):
    half = to_x.shape[0]
    to_y[...] = by_x[:half, :]
    to_x[...] = by_y[half:, :]


def join_kernel(left, right, out):
    out[:, : left.shape[1]] = left[...]
    out[:, left.shape[1] :] = right[...]


def two_sums_kernel(top, by_x, end, by_y, out_top, out_end):
    out_top[...] = (top[...].astype(F32) + by_x[...].astype(F32)).astype(BF16)
    out_end[...] = (end[...].astype(F32) + by_y[...].astype(F32)).astype(BF16)


def move_kernel(moves, in_ref, out_ref):
    out_ref[...] = jnp.zeros_like(out_ref)
    for a, lo, b, to, size in moves:
        out_ref[b, :, to : to + size] = in_ref[a, :, lo : lo + size]


def move_columns(value, moves, blocks, width, deps=()):
    return pl.pallas_call(
later(        functools.partial(move_kernel, tuple(moves)), 1, deps),
        out_shape=jax.ShapeDtypeStruct((blocks, value.shape[1], width), value.dtype),
        in_specs=[pl.BlockSpec(memory_space=pltpu.VMEM)] + wait_specs(deps),
        out_specs=pl.BlockSpec(memory_space=pltpu.VMEM),
        compiler_params=pltpu.CompilerParams(vmem_limit_bytes=VMEM_LIMIT),
    )(value, *deps)


def pick_kernel(cases, place_ref, in_ref, out_ref):
    out_ref[...] = jnp.zeros_like(out_ref)
    for place, moves in enumerate(cases):

        @pl.when(place_ref[0] == place)
        def _(moves=moves):
            for a, lo, _, to, size in moves:
                out_ref[:, to : to + size] = in_ref[a, :, lo : lo + size]


def pick_columns(value, place, cases, width, deps=()):
    return pl.pallas_call(
later(        functools.partial(pick_kernel, tuple(tuple(moves) for moves in cases)), 2, deps),
        out_shape=jax.ShapeDtypeStruct((value.shape[1], width), value.dtype),
        in_specs=[
            pl.BlockSpec(memory_space=pltpu.SMEM), pl.BlockSpec(memory_space=pltpu.VMEM),
        ] + wait_specs(deps),
        out_specs=pl.BlockSpec(memory_space=pltpu.VMEM),
        compiler_params=pltpu.CompilerParams(vmem_limit_bytes=VMEM_LIMIT),
    )(place.astype(jnp.int32).reshape(1), value, *deps)


def runs(spans, each):
    out = []
    for column, block, to, size in spans:
        while size > 0:
            part, lo = divmod(column, each)
            some = min(size, each - lo)
            out.append((part, lo, block, to, some))
            column, to, size = column + some, to + some, size - some
    return out


def project_kernel(count, added, cuts, half, *refs):
    lefts, weights = refs[:count], refs[count : 2 * count]
    outs = refs[2 * count + added :]
    total = None
    for left, weight, (lo, hi) in zip(lefts, weights, cuts):
        part = dot_nt(left[...], weight[:, lo:hi])
        total = part if total is None else total + part
    if added:
        total = total + refs[2 * count][:, : total.shape[1]].astype(F32)
    if half == 0:
        store_filled(outs[0], total)
        return

    @pl.when(pl.program_id(0) < half)
    def _():
        store_filled(outs[0], total)

    @pl.when(pl.program_id(0) >= half)
    def _():
        store_filled(outs[1], total)


def project(lefts, weights, cuts, block_rows, split=False, addend=None, deps=()):
    size = weights[0].shape[0]
    rows = lefts[0].shape[0]
    blocks = rows // block_rows
    half = blocks // 2 if split else 0
    by_rows_spec = lambda width: pl.BlockSpec(
        (block_rows, width), lambda i: ((i + half) % blocks, 0)
    )
    extra = [] if addend is None else [addend]
    shape = jax.ShapeDtypeStruct((rows // 2 if split else rows, fill_width(size)), BF16)
    block = (block_rows, fill_width(size))
    if split:
        out_shape = (shape, shape)
        out_specs = (
            pl.BlockSpec(block, lambda i: (jnp.minimum(i, half - 1), 0)),
            pl.BlockSpec(block, lambda i: (jnp.maximum(i - half, 0), 0)),
        )
    else:
        out_shape, out_specs = (shape,), (pl.BlockSpec(block, lambda i: (i, 0)),)
    return pl.pallas_call(
        later(
            functools.partial(project_kernel, len(lefts), bool(extra), cuts, half),
            2 * len(lefts) + len(extra), deps,
        ),
        out_shape=out_shape,
        grid=(blocks,),
        in_specs=[by_rows_spec(left.shape[1]) for left in lefts]
        + [whole_spec(weight.shape) for weight in weights]
        + [by_rows_spec(part.shape[1]) for part in extra]
        + wait_specs(deps),
        out_specs=out_specs,
        compiler_params=params(),
        cost_estimate=SMALL_COST,
    )(*lefts, *weights, *extra, *deps)


def ffn_kernel(count, model, order, *refs):
    x_refs, c_ref = refs[:count], refs[count]
    gate_ref, up_ref, down_ref = refs[count + 1 : count + 4]
    x_out, c_out, hidden_ref, dgate_ref, dup_ref, back_ref, out_ref, x_buf = refs[-8:]
    take_piece(x_refs, x_buf)
    x = x_buf[:, :model]
    c = c_ref[...]
    x_out[...] = x
    c_out[...] = c
    gate = dot_nn(x, gate_ref[...])
    up = dot_nn(x, up_ref[...])
    sig = sigmoid(gate)
    act = gate * sig
    hidden = (act * up).astype(BF16)
    d_hidden = dot_nn(c, down_ref[...])
    d_gate = (d_hidden * up * (sig * (1.0 + gate * (1.0 - sig)))).astype(BF16)
    d_up = (d_hidden * act).astype(BF16)
    hidden_ref[...] = hidden
    dgate_ref[...] = d_gate
    dup_ref[...] = d_up
    store_filled(back_ref, dot_nt(d_gate, gate_ref[...]) + dot_nt(d_up, up_ref[...]))
    store_filled(out_ref, dot_nt(hidden, down_ref[...]))


def ffn(order, x_pieces, cot, gate_w, up_w, down_wt, first, rows, block_rows, earlier=None):
    model, hidden = gate_w.shape
    all_rows = cot.shape[0]
    filled = x_pieces[0].shape[1]
    count = len(x_pieces)
    begin = first // block_rows
    carried = [model, model, hidden, hidden, hidden]
    extra = [] if earlier is None else list(earlier)
    in_count = count + 5
    place_spec = lambda width: pl.BlockSpec((block_rows, width), lambda i, *_: (begin + i, 0))
    own_spec = pl.BlockSpec((block_rows, fill_width(model)), lambda i, *_: (i, 0))
    return pl.pallas_call(
        functools.partial(ffn_kernel, count, model),
        out_shape=[jax.ShapeDtypeStruct((all_rows, width), BF16) for width in carried]
        + [jax.ShapeDtypeStruct((rows, fill_width(model)), BF16)] * 2,
        grid_spec=pltpu.PrefetchScalarGridSpec(
            num_scalar_prefetch=1,
            grid=(rows // block_rows,),
            in_specs=piece_specs(x_pieces, block_rows)
            + [pl.BlockSpec((block_rows, model), lambda i, order: (order[begin + i], 0))]
            + [whole_spec(gate_w.shape)] * 3
            + [pl.BlockSpec(memory_space=pl.ANY)] * len(extra),
            out_specs=[place_spec(width) for width in carried] + [own_spec] * 2,
            scratch_shapes=[pltpu.VMEM((block_rows, filled), BF16)],
        ),
        input_output_aliases={in_count + i: i for i in range(len(extra))},
        compiler_params=params(),
        cost_estimate=SMALL_COST,
    )(order, *x_pieces, cot, gate_w, up_w, down_wt, *extra)


def branch_kernel(count, model, split, *refs):
    pieces, weight_ref = refs[:count], refs[count]
    d_out, attn_ref, ssm_ref, buf = refs[count + 1 :]
    take_piece(pieces, buf)
    d = buf[:, :model]
    d_out[...] = d
    ssm_ref[...] = dot_nn(d, weight_ref[:, split:])
    attn_ref[...] = dot_nn(d, weight_ref[:, :split])


def branch(pieces, weight, split, block_rows):
    model, depth = weight.shape
    rows = sum(piece.shape[0] for piece in pieces)
    spec = lambda width: pl.BlockSpec((block_rows, width), lambda i: (i, 0))
    return pl.pallas_call(
        functools.partial(branch_kernel, len(pieces), model, split),
        out_shape=(
            jax.ShapeDtypeStruct((rows, model), BF16),
            jax.ShapeDtypeStruct((rows, split), F32),
            jax.ShapeDtypeStruct((rows, depth - split), F32),
        ),
        grid=(rows // block_rows,),
        in_specs=piece_specs(pieces, block_rows) + [whole_spec(weight.shape)],
        out_specs=(spec(model), spec(split), spec(depth - split)),
        scratch_shapes=[pltpu.VMEM((block_rows, pieces[0].shape[1]), BF16)],
        compiler_params=params(),
        cost_estimate=SMALL_COST,
    )(*pieces, weight)


ORDER = (0, 2, 4, 6, 1, 3, 5, 7)
CUBE = len(ORDER)


def by_rows(value):
    return with_layout_constraint(value, Layout(major_to_minor=tuple(range(value.ndim))))


def swap(value, mask):
    return lax.ppermute(value, "ctx", [(d, d ^ mask) for d in range(CUBE)])


def fill_lanes(value):
    more = -value.shape[1] % 128
    return jnp.pad(value.astype(BF16), ((0, 0), (0, more)))


def block_order(place, devices):
    if devices == CUBE:
        return place ^ jnp.array(ORDER, jnp.int32)
    return jnp.arange(devices, dtype=jnp.int32)


def block_index(owner, place, devices):
    if devices == CUBE:
        k = owner ^ place
        return k // 2 + (k % 2) * (CUBE // 2)
    return owner


def gather_pieces(own, devices):
    if devices != CUBE:
        return [lax.all_gather(own, "ctx", axis=0, tiled=True)]
    by_x, by_y, mate = swap(own, 2), swap(own, 4), swap(own, 1)
    part = jax.ShapeDtypeStruct((own.shape[0] // 2, own.shape[1]), own.dtype)
    to_y, to_x = whole_call(cross_kernel, [part, part], by_x, by_y)
    far = jnp.concatenate([swap(to_y, 4), swap(to_x, 2)], axis=0)
    return [own, by_x, by_y, far, mate, swap(by_x, 1), swap(by_y, 1), swap(far, 1)]


def row_halves(rows, devices):
    return [(rows // 2, rows // 2), (0, rows // 2)] if devices == CUBE else [(0, rows)]


def scatter_begin(part, devices):
    return swap(part, 1) if devices == CUBE else part


def scatter_chip(mine, from_mate, devices, deps=()):
    if devices != CUBE:
        return (mine,)
    size, width = mine.shape[0] * 2 // CUBE, mine.shape[1]
    shape = lambda rows, kind: jax.ShapeDtypeStruct((rows, width), kind)
    whole, half = shape(size, F32), shape(size // 2, F32)
    send = shape(size, BF16)
    return whole_call(
        chip_sum_kernel, [whole, send, send, half, half], mine, from_mate, deps=deps
    )


def scatter_links(parts, devices, deps=()):
    if devices != CUBE:
        return parts
    own, to_x, to_y, keep_x, keep_y = parts
    low = jax.ShapeDtypeStruct(keep_x.shape, BF16)
    return whole_call(
        near_sum_kernel, [jax.ShapeDtypeStruct(own.shape, F32), low, low],
        own, keep_x, keep_y, swap(to_x, 2), swap(to_y, 4), deps=deps,
    )


def scatter_near(mine, from_mate, devices):
    return scatter_links(scatter_chip(mine, from_mate, devices), devices)


def scatter_far(parts, width, devices, deps=()):
    if devices != CUBE:
        total = lax.psum_scatter(parts[0], "ctx", scatter_dimension=0, tiled=True)
        return total[:, :width].astype(F32)
    part, to_x, to_y = parts
    shape = jax.ShapeDtypeStruct(part.shape, F32)
    total = whole_call(
        far_sum_kernel, [shape], part, swap(to_y, 4), swap(to_x, 2), deps=deps
    )[0]
    return total[:, :width]


def scatter_end(mine, from_mate, width, devices):
    return scatter_far(scatter_near(mine, from_mate, devices), width, devices)


def exchange(blocks):
    return lax.all_to_all(blocks, "ctx", split_axis=0, concat_axis=0, tiled=True)


def small_scatter(value, place, devices):
    if devices != CUBE:
        return lax.psum_scatter(value, "ctx", scatter_dimension=0, tiled=False)
    return sum(swap(value[i], k) if k else value[i] for i, k in enumerate(ORDER))


def small_gather(value, place, devices):
    if devices != CUBE:
        return lax.all_gather(value, "ctx", axis=0)
    return jnp.stack([swap(value, k) if k else value for k in ORDER])


def in_places(got, place, devices):
    if devices != CUBE:
        return got
    got = jnp.stack(got)
    return got[block_index(jnp.arange(CUBE, dtype=jnp.int32), place, devices)]


def place_gather(value, place, devices, ordered=True):
    if devices != CUBE:
        return lax.all_gather(value, "ctx", axis=0)
    got = [swap(value, k) if k else value for k in ORDER]
    return in_places(got, place, devices) if ordered else got


def add_low(a, b):
    return (a.astype(F32) + b.astype(F32)).astype(BF16)


def all_sum_core(value, devices):
    return add_low(value, swap(value, 1)) if devices == CUBE else value


def all_sum_near(value, devices, deps=()):
    if devices != CUBE:
        return (value,)
    half = value.shape[0] // 2
    top, end = value[:half], value[half:]
    shape = jax.ShapeDtypeStruct(top.shape, top.dtype)
    return whole_call(two_sums_kernel, [shape, shape], top, swap(top, 2), end, swap(end, 4), deps=deps)


def all_sum_far(parts, devices):
    if devices != CUBE:
        return lax.psum(parts[0], "ctx")
    top, end = parts
    return jnp.concatenate([add_low(top, swap(top, 4)), add_low(end, swap(end, 2))], axis=0)


def lane_gather(value):
    return lax.all_gather(value, "fsdp", axis=0, tiled=True)


def lane_scatter(value):
    return lax.psum_scatter(value, "fsdp", scatter_dimension=0, tiled=True)


def lane_shift(value, lanes, step):
    return lax.ppermute(value, "fsdp", [(z, (z + step) % lanes) for z in range(lanes)])


def lane_small_gather(value, lanes):
    lane = lax.axis_index("fsdp")
    got = jnp.stack([value] + [lane_shift(value, lanes, k) for k in range(1, lanes)])
    return got[(lane - jnp.arange(lanes, dtype=jnp.int32)) % lanes]


def lane_small_exchange(blocks, lanes):
    lane = lax.axis_index("fsdp")
    pick = lambda k: lax.dynamic_index_in_dim(blocks, (lane + k) % lanes, 0, False)
    return tuple(lane_shift(pick(k), lanes, k) if k else pick(0) for k in range(lanes))


def lane_small_scatter(blocks, lanes):
    return sum(part.astype(F32) for part in lane_small_exchange(blocks, lanes))


def after(value, *earlier):
    return lax.optimization_barrier((value,) + earlier)[0]


def back(moves):
    return [(b, to, a, lo, size) for a, lo, b, to, size in moves]


def pair_routes(devices):
    half = devices // 2
    first = [(d, 2 * d) for d in range(half)] + [(d, 2 * (d - half) + 1) for d in range(half, devices)]
    second = [(d, 2 * d + 1) for d in range(half)] + [(d, 2 * (d - half)) for d in range(half, devices)]
    return first, second


def split_pairs(value, place, devices):
    width = value.shape[1] // 2
    first, second = pair_routes(devices)
    low, high = value[:, :width], value[:, width:]
    early = place < devices // 2
    got_a = lax.ppermute(jnp.where(early, low, high), "ctx", first)
    got_b = lax.ppermute(jnp.where(early, high, low), "ctx", second)
    even = place % 2 == 0
    return jnp.where(even, got_a, got_b), jnp.where(even, got_b, got_a)


def join_pairs(left, right, place, devices):
    first, second = pair_routes(devices)
    send = lambda value, routes, odd: lax.ppermute(
        value, "ctx", [(b, a) for a, b in routes if b % 2 == odd]
    )
    early = place < devices // 2
    low = jnp.where(early, send(left, first, 0), send(right, second, 0))
    high = jnp.where(early, send(left, second, 1), send(right, first, 1))
    return jnp.concatenate([low, high], axis=1)


def pad_to(value, size, axis):
    widths = [(0, 0)] * value.ndim
    widths[axis] = (0, size - value.shape[axis])
    return jnp.pad(value, widths)


def rms_factor(value):
    return lax.rsqrt(jnp.mean(value * value, axis=-1, keepdims=True) + EPS)


def norm_back(value, factor, gain, grad):
    weighted = grad * gain
    d_value = factor * weighted - value * factor * factor * factor * jnp.mean(
        value * weighted, axis=-1, keepdims=True
    )
    return d_value, jnp.sum(grad * value * factor, axis=0)


def shards(
    tokens, cotangent, unit_order, block_seq, meta_tokens, input_gain, query_key_value_weight, w_xz,
    conv_kernel, state_proj, step_proj, step_bias, decay_log, skip_gain, attn_gain, ssm_gain,
    out_proj, ffn_gain, w_gate, w_up, w_down,
):
    devices = lax.axis_size("ctx")
    lanes = lax.axis_size("fsdp")
    place = lax.axis_index("ctx")
    own_rows = tokens.shape[1]
    model = tokens.shape[2]
    unit_rows = own_rows // 2
    slot_unit = unit_order[0]
    units = slot_unit.shape[0]
    rows = units * unit_rows
    width = conv_kernel.shape[1]
    hidden_width = w_gate.shape[1]
    heads = -(-QUERY_HEADS // devices)
    head_width = heads * HEAD_SIZE
    group = QUERY_HEADS // KEY_VALUE_HEADS
    query_width = QUERY_HEADS * HEAD_SIZE
    kv_width = KEY_VALUE_HEADS * HEAD_SIZE
    model_part = input_gain.shape[0]

    slot_ids = jnp.arange(units, dtype=jnp.int32)
    fixed = jnp.sum(
        jnp.where(slot_unit[None, :] == slot_ids[:, None], slot_ids[None, :], 0), axis=1
    ).astype(jnp.int32)
    slot = (2 * block_index(fixed // 2, place, devices) + fixed % 2).astype(jnp.int32)
    unit_seq = jnp.repeat(block_seq[0], 2)
    starts = jnp.concatenate([jnp.ones((1,), jnp.bool_), unit_seq[1:] != unit_seq[:-1]])
    starts_int = starts.astype(jnp.int32)
    low_block = (jnp.sum(unit_seq[None, :] < unit_seq[:, None], axis=1) // 2).astype(jnp.int32)
    my_units = lax.dynamic_slice_in_dim(slot_unit, 2 * place, 2)
    my_start = jnp.any((my_units[:, None] == slot_ids[None, :]) & starts[None, :], axis=1)

    x_part, z_part = split_pairs(w_xz, place, devices)

    small = after(
        jnp.concatenate(
            [conv_kernel, state_proj, step_proj, decay_log, meta_tokens.reshape(-1, width)], axis=0
        ),
        x_part,
    )
    small_all = lane_small_gather(small, lanes)
    marks = [conv_kernel.shape[0], state_proj.shape[0], step_proj.shape[0], decay_log.shape[0]]
    ends = [sum(marks[: i + 1]) for i in range(4)]
    conv_w = small_all[:, : ends[0]].reshape(-1, width).astype(F32)
    sel_w = small_all[:, ends[0] : ends[1]].reshape(-1, width)
    step_w = small_all[:, ends[1] : ends[2]].reshape(-1, width)
    decay = small_all[:, ends[2] : ends[3]].reshape(-1, width).astype(F32)
    rate = -jnp.exp(decay)
    rate2 = rate * LOG2E
    meta_part = small_all[:, ends[3] :].reshape(-1, model_part)
    meta_rows = meta_part.shape[0]
    wide = jnp.concatenate(
        [meta_part, input_gain[None], ffn_gain[None], attn_gain[None]], axis=0
    )
    wide = place_gather(wide, place, devices)
    wide = jnp.transpose(wide, (1, 0, 2)).reshape(-1, model).astype(F32)
    meta = wide[:meta_rows]
    gain_in = wide[meta_rows]
    gain_ffn = wide[meta_rows + 1]
    gain_attn = lax.dynamic_slice_in_dim(
        pad_to(wide[meta_rows + 2], devices * head_width, 0), place * head_width, head_width
    )[None]
    bias = step_bias.astype(F32)[None]
    skip = skip_gain.astype(F32)[None]
    gain_ssm = ssm_gain.astype(F32)[None]

    xz_w = lane_gather(jnp.concatenate([x_part, z_part], axis=1))
    x_w, z_w = xz_w[:, :width], xz_w[:, width:]
    out_held = hold(jnp.transpose(out_proj), small_all)
    out_cols = lax.all_gather(out_held, "fsdp", axis=0)
    order = block_order(place, devices)
    piece_rows = min(256, own_rows)

    own_tok = tokens[0]
    pieces = gather_pieces(fill_lanes(after(own_tok, x_part)), devices)
    slot_start = jnp.sum(
        jnp.where(slot[None, :] == slot_ids[:, None], starts_int[None, :], 0), axis=1
    ).astype(jnp.int32)
    normed = norm_all(slot_start, meta, gain_in[None], pieces)
    qkv_all = lax.all_gather(hold(query_key_value_weight, normed, out_held), "ctx", axis=0)
    resid = jnp.where(
        my_start[:, None, None], meta[None], own_tok.reshape(2, unit_rows, model).astype(F32)
    ).reshape(own_rows, model)
    in_factor = rms_factor(resid)

    x_in = dot_nn(normed, x_w).astype(BF16)

    conv_out, ssm_in, select = conv_forward(
        slot, fixed, starts_int, x_in, conv_w, sel_w, unit_rows
    )
    select = all_sum_core(select, devices)
    z_gate = dot_nn(normed, z_w).astype(BF16)
    near = all_sum_near(select, devices, (z_gate,))
    select = all_sum_far(near, devices).astype(F32)
    first_kv = (place * heads) // group
    kv_room = (devices * heads // group + 3) * HEAD_SIZE
    cases = []
    for d in range(devices):
        some = max(0, min(head_width, query_width - d * head_width))
        spans = [(d * head_width, 0, 0, some)]
        low_kv = d * heads // group * HEAD_SIZE
        some = max(0, min(PAIR_WIDTH, kv_width - low_kv))
        for i in range(2):
            begin = query_width + i * kv_width + low_kv
            spans.append((begin, 0, head_width + i * PAIR_WIDTH, some))
        cases.append(runs(spans, query_key_value_weight.shape[1]))
    qkv_width = head_width + 2 * PAIR_WIDTH
    qkv_part = pick_columns(qkv_all, place, cases, qkv_width, (near[0],))
    qkv_w = lane_gather(qkv_part)
    pair = jnp.clip(
        (place * heads + jnp.arange(heads, dtype=jnp.int32)) // group - first_kv, 0, 1
    ).astype(jnp.int32)
    cot_own = hold(cotangent[0], qkv_part)
    cot = lax.all_gather(cot_own, "ctx", axis=0, tiled=True)
    down_held = hold(jnp.transpose(w_down), cot_own)
    down_cols = lax.all_gather(down_held, "fsdp", axis=0)
    gate_held = hold(w_gate, down_held)
    gate_w = lane_gather(gate_held)
    up_held = hold(w_up, gate_held)
    up_w = lane_gather(up_held)
    spans = []
    for d in range(devices):
        some = max(0, min(head_width, query_width - d * head_width))
        spans += [(d * head_width, d, 0, some), (query_width + d * width, d, head_width, width)]
    out_moves = runs(spans, out_proj.shape[0])
    out_blocks = move_columns(out_cols, out_moves, devices, head_width + width, (select,))
    out_wt = exchange(out_blocks).reshape(model, -1)
    down_moves = runs(
        [(d * hidden_width, d, 0, hidden_width) for d in range(devices)], w_down.shape[0]
    )
    step_low = select[:, :DT_RANK].astype(BF16)
    bc = jnp.transpose(select[:, DT_RANK:].reshape(units, unit_rows, 2 * STATE), (0, 2, 1))
    y_total, ssm_comb, ssm_square, wide_bc, states, last_states = scan_forward(
        slot, fixed, starts_int, ssm_in, z_gate, step_low, bc, step_w, bias, rate2, skip, gain_ssm,
        unit_rows, (out_blocks, up_held),
    )

    cube = devices == CUBE

    def out_term(comb, lo, hi, *deps):
        return project([comb], [out_wt], [(lo, hi)], piece_rows, cube, None, deps)

    ssm_terms = out_term(ssm_comb, head_width, head_width + width)
    ssm_mate = scatter_begin(ssm_terms[0], devices)
    qkv = dot_nn(normed, qkv_w).astype(BF16)
    ssm_chip = scatter_chip(ssm_terms[-1], ssm_mate, devices, (qkv,))
    down_blocks = move_columns(down_cols, down_moves, devices, hidden_width, (ssm_chip[0],))
    down_wt = exchange(down_blocks).reshape(model, -1)
    queries = qkv[:, :head_width]
    keys = qkv[:, head_width : head_width + PAIR_WIDTH]
    values = qkv[:, head_width + PAIR_WIDTH :]
    attn, attn_comb, attn_stat = attn_forward(
        slot, low_block, pair, queries, keys, jnp.transpose(values), gain_attn, unit_rows,
        (ssm_chip[0], down_blocks),
    )
    ssm_near = scatter_links(ssm_chip, devices, (attn_comb,))
    attn_terms = out_term(attn_comb, 0, head_width, down_wt, ssm_near[0])
    ssm_out = scatter_far(ssm_near, model, devices)
    attn_mate = scatter_begin(attn_terms[0], devices)
    attn_out = scatter_end(attn_terms[-1], attn_mate, model, devices)
    squares = jnp.stack(
        [
            attn_stat[:, 1, :unit_rows].reshape(devices, own_rows),
            ssm_square[:, 0].reshape(devices, own_rows),
        ],
        axis=1,
    )
    squares = small_scatter(squares, place, devices)
    own_factors = lax.rsqrt(squares / jnp.array([[query_width], [devices * width]], F32) + EPS)
    mid = (
        resid
        + 0.5 * own_factors[0][:, None] * attn_out
        + 0.5 * own_factors[1][:, None] * ssm_out
    )
    mid_factor = rms_factor(mid)
    x_pieces = gather_pieces(fill_lanes(mid * mid_factor * gain_ffn), devices)

    carried = None
    back_terms, ffn_terms = [], []
    for first, count in row_halves(rows, devices):
        some = slice(first // own_rows, (first + count) // own_rows)
        x_some = x_pieces[some] if devices == CUBE else x_pieces
        *carried, back_term, ffn_term = ffn(
            order, x_some, cot, gate_w, up_w, down_wt, first, count, piece_rows, carried
        )
        back_terms.append(back_term)
        ffn_terms.append(ffn_term)
    ffn_in, cot_rows, hidden, d_gate, d_up = carried
    back_mate = scatter_begin(back_terms[0], devices)
    ffn_in = after(ffn_in, back_mate)
    gate_part = dot_tn(ffn_in, d_gate).astype(BF16)
    gate_grad = lane_scatter(gate_part)
    d_ffn = after(scatter_end(back_terms[-1], back_mate, model, devices), gate_part)

    d_mid_norm, ffn_gain_part = norm_back(mid, mid_factor, gain_ffn, d_ffn)
    d_mid = cotangent[0].astype(F32) + d_mid_norm
    d_branch_own = d_mid.astype(BF16)
    d_pieces = gather_pieces(fill_lanes(d_branch_own), devices)
    up_part = dot_tn(ffn_in, after(d_up, d_branch_own)).astype(BF16)
    up_grad = lane_scatter(up_part)
    down_part = dot_tn(cot_rows, after(hidden, d_branch_own)).astype(BF16)
    d_pieces[-1] = after(d_pieces[-1], up_part, down_part)
    down_back = exchange(after(down_part, d_pieces[-1]).reshape(devices, model_part, -1))
    ffn_mate = scatter_begin(ffn_terms[0], devices)
    ffn_chip = scatter_chip(ffn_terms[-1], ffn_mate, devices)
    branch_f = d_branch_own.astype(F32)
    dots = jnp.stack(
        [
            jnp.sum(branch_f * attn_out, axis=1) * (0.5 / query_width),
            jnp.sum(branch_f * ssm_out, axis=1) * (0.5 / (devices * width)),
        ]
    )
    shifts = dots * own_factors * own_factors * own_factors
    spread_rows = small_gather(jnp.concatenate([own_factors, shifts], axis=0), place, devices)
    spread_rows = jnp.transpose(spread_rows, (1, 0, 2)).reshape(4, rows)
    factors, shifts = spread_rows[:2], spread_rows[2:]

    d_branch, d_comb_attn, d_comb_ssm = branch(d_pieces, out_wt, head_width, piece_rows)
    stat = jnp.transpose(pad_to(jnp.stack([factors[1], shifts[1]]), 128, 0))
    d_z, x_part_grad, d_low, d_bc, step_grad, vec_grads, decay_sum = scan_backward(
        slot, fixed, starts_int, d_comb_ssm, stat, y_total, z_gate, ssm_in, step_low, wide_bc,
        states, last_states, step_w, bias, rate2, skip, gain_ssm, unit_rows,
        (ffn_chip[0],),
    )
    d_bc = jnp.transpose(
        d_bc[:, :, 0].reshape(units, 2, unit_rows, STATE), (0, 2, 1, 3)
    ).reshape(rows, 2 * STATE)
    ffn_near = scatter_links(ffn_chip, devices, (d_low,))
    down_back = move_columns(
        down_back, back(down_moves), lanes, w_down.shape[0], (ffn_near[0],)
    )
    down_grad = lax.psum_scatter(down_back, "fsdp", scatter_dimension=0, tiled=False)
    d_select = whole_call(
        join_kernel, [jax.ShapeDtypeStruct((rows, DT_RANK + 2 * STATE), BF16)],
        d_low, d_bc.astype(BF16), deps=(down_back,),
    )[0]
    attn_mixed = (attn * (0.5 * factors[0][:, None] * gain_attn)).astype(BF16)
    ssm_mixed = (ssm_comb.astype(F32) * (0.5 * factors[1][:, None])).astype(BF16)
    d_select = all_sum_core(d_select, devices)
    mixed = after(jnp.concatenate([attn_mixed, ssm_mixed], axis=1), d_select)
    out_part = dot_tn(d_branch, mixed).astype(BF16)
    d_near = all_sum_near(d_select, devices)
    d_near = lax.optimization_barrier(tuple(d_near) + (out_part,))[:-1]
    d_far = all_sum_far(d_near, devices)
    z_part_grad = dot_tn(normed, after(d_z, *d_near)).astype(BF16)
    d_far = after(d_far, z_part_grad)
    out_back = exchange(hold(out_part, d_far).reshape(devices, model_part, -1))
    if devices == CUBE:
        ffn_near = (ffn_near[0], hold(ffn_near[1], d_far), hold(ffn_near[2], d_far))
    half = 0.5 * d_comb_attn
    d_attn = factors[0][:, None] * (half * gain_attn) - attn * shifts[0][:, None]
    attn_gain_part = jnp.sum(half * attn * factors[0][:, None], axis=0)
    d_query, d_keys, d_values = attn_backward(
        slot, low_block, pair, queries, attn, d_attn.astype(BF16), attn_stat,
        keys, jnp.transpose(keys), values, unit_rows, (d_far, out_part),
    )
    out_back = move_columns(
        out_back, back(out_moves), lanes, out_proj.shape[0], (d_query,)
    )
    layer_out = mid + scatter_far(ffn_near, model, devices, (out_back,))
    d_qkv = whole_call(
        join_qkv_kernel, [jax.ShapeDtypeStruct((rows, qkv_width), BF16)],
        d_query, d_keys, d_values, deps=(layer_out,),
    )[0]
    layer_out = layer_out.astype(BF16)[None]
    qkv_part_grad = dot_tn(normed, d_qkv).astype(BF16)
    early = project(
        [d_qkv, after(d_z, d_qkv)], [qkv_w, z_w], [(0, qkv_width), (0, width)], piece_rows,
        False, None, (qkv_part_grad, z_part_grad),
    )[0]
    out_grad = lax.psum_scatter(
        out_back, "fsdp", scatter_dimension=0, tiled=False
    )
    z_grad = lane_scatter(z_part_grad)
    in_grad = lane_scatter(qkv_part_grad)
    d_x, conv_grads, select_grad = conv_backward(
        slot, fixed, starts_int, d_far, x_part_grad, conv_out, x_in, ssm_in, conv_w, sel_w, unit_rows,
        (early, layer_out, out_back, down_back),
    )
    in_terms = project([d_x], [x_w], [(0, width)], piece_rows, cube, early)
    in_mate = scatter_begin(in_terms[0], devices)
    x_part_sum = dot_tn(after(normed, in_mate), d_x).astype(BF16)
    in_chip = scatter_chip(in_terms[-1], in_mate, devices)
    in_near = scatter_links(in_chip, devices)
    d_normed = scatter_far(in_near, model, devices)
    sums = (down_grad, out_grad, gate_grad, up_grad, z_grad, in_grad, conv_grads, select_grad)
    sums += (step_grad, vec_grads, decay_sum)
    sums = lax.optimization_barrier(sums + tuple(in_near))[: len(sums)]
    down_grad, out_grad, gate_grad, up_grad, z_grad, in_grad, conv_grads, select_grad = sums[:8]
    step_grad, vec_grads, decay_sum = sums[8:]
    gate_grad, up_grad = gate_grad.astype(F32), up_grad.astype(F32)
    x_grad = lane_scatter(x_part_sum)
    in_grad = hold(in_grad, d_normed)
    spread = jnp.zeros((in_grad.shape[0], devices * head_width), BF16)
    spread = lax.dynamic_update_slice_in_dim(spread, in_grad[:, :head_width], place * head_width, 1)
    kv_zero = jnp.zeros((in_grad.shape[0], kv_room), BF16)
    qkv_full = jnp.concatenate(
        [
            spread[:, :query_width],
            lax.dynamic_update_slice_in_dim(
                kv_zero, in_grad[:, head_width : head_width + 2 * HEAD_SIZE],
                first_kv * HEAD_SIZE, 1,
            )[:, :kv_width],
            lax.dynamic_update_slice_in_dim(
                kv_zero, in_grad[:, head_width + 2 * HEAD_SIZE : qkv_width],
                first_kv * HEAD_SIZE, 1,
            )[:, :kv_width],
        ],
        axis=1,
    )
    part = query_key_value_weight.shape[1]
    qkv_blocks = jnp.transpose(qkv_full.reshape(-1, devices, part), (1, 0, 2))
    qkv_grad = lax.psum_scatter(
        qkv_blocks, "ctx", scatter_dimension=0, tiled=False
    ).astype(F32)

    d_norm_in, in_gain_part = norm_back(resid, in_factor, gain_in, d_normed)
    d_resid = d_mid + d_norm_in
    halves = [
        (my_start[i], d_resid[i * unit_rows : (i + 1) * unit_rows]) for i in range(2)
    ]
    tokens_grad = jnp.concatenate(
        [jnp.where(flag, 0.0, half).astype(BF16) for flag, half in halves], axis=0
    )[None]
    meta_sum = sum(jnp.where(flag, half, 0.0) for flag, half in halves)

    gain_rows = jnp.stack(
        [
            in_gain_part,
            ffn_gain_part,
            lax.dynamic_update_slice_in_dim(
                jnp.zeros((devices * head_width,), F32), attn_gain_part, place * head_width, 0
            )[:query_width],
        ]
    )
    by_lane = jnp.concatenate(
        [
            meta_sum.reshape(lanes, -1, model),
            jnp.broadcast_to(gain_rows[None], (lanes, 3, model)),
        ],
        axis=1,
    )
    count = by_lane.shape[1]
    packed = jnp.transpose(
        by_lane.reshape(lanes, count, devices, model_part), (0, 2, 1, 3)
    ).reshape(lanes * devices, count, model_part)
    totals = jnp.sum(
        lax.all_to_all(
            packed.astype(BF16), ("fsdp", "ctx"), split_axis=0, concat_axis=0, tiled=True
        ).astype(F32),
        axis=0,
    )
    xz_grad = join_pairs(x_grad, z_grad, place, devices).astype(F32)
    packed_low = packed.astype(BF16)
    down_grad, out_grad = (
        jnp.transpose(hold(part, packed_low).astype(F32)) for part in (down_grad, out_grad)
    )
    select_grad = hold(select_grad, packed_low)
    counts = [CONV, select_grad.shape[0], DT_RANK, STATE]
    local = jnp.concatenate(
        [
            part.reshape(lanes, -1, width)
            for part in (conv_grads[:CONV], select_grad, step_grad, rate * decay_sum)
        ]
        + [jnp.broadcast_to(vec_grads[None, :3], (lanes, 3, width))],
        axis=1,
    )
    local = lane_small_scatter(local, lanes)
    ends = [sum(counts[:i]) // lanes for i in range(5)]
    piece = lambda i: local[ends[i] : ends[i + 1]]
    vec = lambda i: local[ends[4] + i]
    return (
        layer_out,
        tokens_grad,
        totals[: count - 3],
        totals[count - 3],
        qkv_grad,
        xz_grad,
        piece(0),
        piece(1),
        piece(2),
        vec(2),
        piece(3),
        vec(1),
        totals[count - 1],
        vec(0),
        out_grad,
        totals[count - 2],
        gate_grad,
        up_grad,
        down_grad,
    )


def solution(mesh):
    rows = P("fsdp", "ctx", None)
    index = P("fsdp", None)
    mat = P("fsdp", "ctx")
    vec = P("ctx")
    return jax.shard_map(
        shards,
        mesh=mesh,
        in_specs=(
            rows, rows, index, index, mat, vec, mat, mat, mat, mat, mat, vec, mat, vec, vec, vec,
            mat, vec, mat, mat, mat,
        ),
        out_specs=(
            rows, rows, mat, vec, mat, mat, mat, mat, mat, vec, mat, vec, vec, vec, mat, vec, mat,
            mat, mat,
        ),
        check_vma=False,
    )
```
